32 devices in a mesh: groups: 2 (over y), pool: 4 (over x, core), tensor: 4 (over z).
Axes of the slice: x: 2, y: 2, z: 4, core: 2. Of those that a mesh axis runs over, the one named last changes fastest.
Arguments:
- hidden: bfloat16 [1024, 28672], P(('groups', 'pool'), 'tensor'), parts along dimension 0, may hold values from -6 to 6
- down_weight: bfloat16 [28672, 8192], P('tensor', 'pool'), may hold values from -0.03125 to 0.03125
- adapter_input_maps: bfloat16 [64, 64, 28672], P('pool', None, 'tensor'), may hold values from -0.03125 to 0.03125
- adapter_output_maps: bfloat16 [4096, 8192], P(('pool', 'tensor')), may hold values from -0.75 to 0.75
- request_list_slot: int32 [1024], P('groups'), parts along dimension 0, may hold values from 0 to 15
- group_adapter_lists: int32 [8, 16], P('groups'), parts along dimension 0, may hold values from 0 to 63, as said below
Outputs:
- mixed: bfloat16 [1024, 8192], P(('groups', 'tensor'), 'pool'), parts along dimension 0
The draws below stay inside these ranges and needn't reach their ends.
There are 2 independent parts, one for each index of `groups`. The reference program is written for one: setup_inputs(seed, part) draws one part's arguments, and reference() takes and returns one part's arrays. A program takes and returns all parts, laid end to end along the dimension named above; an argument that names none is the same for every part. Nothing has to cross between parts.
Inputs may be any that keep to these rules, and one draw needn't show every extreme that they name: `group_adapter_lists`: row g lists 16 distinct adapters for request group g. The owner of adapter a is a // 16; each row's adapters belong to exactly 4 owners, exactly 4 from each of them.
All inputs are finite; a program needn't handle non-finite values.
Results may differ from the reference program's by a relative error of at most 0.0065.
Values may be sent and summed in bfloat16 or wider, within the bound.
No kernel may reach another device: no remote copies, remote signals or barrier semaphores. Data moves between devices by JAX's collectives and lax.ppermute only.
A program may use at most 192 MiB of HBM per device.

```python
import jax
import jax.numpy as jnp
from jax import lax

MODEL_WIDTH = 8192
HIDDEN_UNITS = 28672
ADAPTER_RANK = 64
ROWS = 128
ADP_DEV = 16
SLOTS = 16
CAP = 4
ADAPTER_TOTAL = 64
ROWS_ALL = 512
N_POOL = 4


def draw_group_adapter_lists(key, part):
    key = jax.random.fold_in(key, 7)
    key_hot, key_owner, key_place, key_shuffle = jax.random.split(key, 4)
    owner_count = SLOTS // CAP
    hot_owner = jax.random.randint(key_hot, (), 0, N_POOL)
    owner_ids = jnp.arange(N_POOL, dtype=jnp.int32)
    owner_scores = jax.random.randint(key_owner, (N_POOL, N_POOL), 0, 4096) * N_POOL + owner_ids[None, :]
    owner_scores = owner_scores + (owner_ids[None, :] == hot_owner).astype(jnp.int32) * (4096 * N_POOL)
    chosen_owners = lax.top_k(owner_scores, owner_count)[1].astype(jnp.int32)
    place_ids = jnp.arange(ADP_DEV, dtype=jnp.int32)
    place_scores = jax.random.randint(key_place, (N_POOL, owner_count, ADP_DEV), 0, 4096) * ADP_DEV + place_ids
    chosen_places = lax.top_k(place_scores, CAP)[1].astype(jnp.int32)
    listed_adapters = (chosen_owners[:, :, None] * ADP_DEV + chosen_places).reshape(N_POOL, SLOTS)
    shuffle_scores = jax.random.randint(key_shuffle, (N_POOL, SLOTS), 0, 4096) * SLOTS + jnp.arange(SLOTS, dtype=jnp.int32)[None, :]
    order = jnp.argsort(shuffle_scores, axis=1, stable=True).astype(jnp.int32)
    return jnp.take_along_axis(listed_adapters, order, axis=1).astype(jnp.int32)


def touch_ends(result, stream_key, least, high):
    longest = result.shape.index(max(result.shape))
    spots = []
    for shift in (0, 1):
        where = [jax.random.randint(jax.random.fold_in(stream_key, axis), (), 0, length) for axis, length in enumerate(result.shape)]
        where[longest] = (where[longest] + shift) % result.shape[longest]
        spots.append(tuple(where))
    return result.at[spots[0]].set(least).at[spots[1]].set(high)


def levels(own_key, dims, cuts, least, top_value):
    def one(position, parts):
        draws = jax.random.uniform(jax.random.fold_in(jax.random.fold_in(own_key, 6), position), (parts,), jnp.float32, least / len(cuts), top_value / len(cuts))
        return jnp.repeat(jnp.exp(draws), dims[position] // parts).reshape((-1,) + (1,) * (len(dims) - position - 1))

    gain = one(*cuts[0])
    for cut in cuts[1:]:
        gain = gain * one(*cut)
    return gain


def centred(rng, shape, scale, most, shards=(), kind=jnp.bfloat16):
    array = scale * jax.random.normal(rng, shape, jnp.float32)
    if shards:
        array = array * levels(rng, shape, shards, -0.22, 0.18)
    return jnp.clip(array, -most, most).astype(kind)


def setup_inputs(seed: int = 0, part: int = 0) -> dict:
    arg_keys = jax.random.split(jax.random.key(seed), 7)
    part_splits = jax.random.split(jax.random.fold_in(arg_keys[6], part), 7)
    return {
        "hidden": centred(part_splits[0], (ROWS_ALL, HIDDEN_UNITS), 1.0, 6.0, ((0, 4), (1, 4))),
        "down_weight": centred(arg_keys[1], (HIDDEN_UNITS, MODEL_WIDTH), HIDDEN_UNITS ** -0.5, 0.03125, ((0, 4), (1, 4))),
        "adapter_input_maps": centred(arg_keys[2], (ADAPTER_TOTAL, ADAPTER_RANK, HIDDEN_UNITS), HIDDEN_UNITS ** -0.5, 0.03125, ((0, 4), (2, 4))),
        "adapter_output_maps": centred(arg_keys[3], (ADAPTER_TOTAL * ADAPTER_RANK, MODEL_WIDTH), ADAPTER_RANK ** -0.5, 0.75, ((0, 16),)),
        "request_list_slot": touch_ends(jax.random.randint(part_splits[4], (ROWS_ALL,), 0, SLOTS), jax.random.fold_in(part_splits[4], 1), 0, SLOTS - 1).astype(jnp.int32),
        "group_adapter_lists": draw_group_adapter_lists(jax.random.fold_in(jax.random.fold_in(arg_keys[6], part), 71), part),
    }


def reference(hidden, down_weight, adapter_input_maps, adapter_output_maps, request_list_slot, group_adapter_lists):
    total_rows = hidden.shape[0]
    group_hidden = hidden.reshape(N_POOL, ROWS, HIDDEN_UNITS)
    group_slots = request_list_slot.reshape(N_POOL, ROWS)
    output_maps = adapter_output_maps.reshape(ADAPTER_TOTAL, ADAPTER_RANK, MODEL_WIDTH)

    def one_group(inputs):
        rows_hidden, slot_rows, listed_adapters = inputs
        slot_hot = (slot_rows[:, None] == jnp.arange(SLOTS, dtype=jnp.int32)[None, :]).astype(jnp.float32)
        picked_input_maps = jnp.take(adapter_input_maps, listed_adapters, axis=0).astype(jnp.float32)
        scores = jnp.einsum("rf,skf->rsk", rows_hidden.astype(jnp.float32), picked_input_maps)
        lowrank = jnp.sum(scores * slot_hot[:, :, None], axis=1).astype(jnp.bfloat16)
        picked_output_maps = jnp.take(output_maps, listed_adapters, axis=0).astype(jnp.float32)
        spread = (slot_hot[:, :, None] * lowrank.astype(jnp.float32)[:, None, :]).reshape(ROWS, SLOTS * ADAPTER_RANK)
        delta = jnp.dot(spread, picked_output_maps.reshape(SLOTS * ADAPTER_RANK, MODEL_WIDTH))
        base = jnp.dot(rows_hidden, down_weight, preferred_element_type=jnp.float32)
        return (base + delta).astype(jnp.bfloat16)

    mixed = lax.map(one_group, (group_hidden, group_slots, group_adapter_lists))
    return mixed.reshape(total_rows, MODEL_WIDTH)
```

```python
import jax
import jax.numpy as jnp
from jax import lax
from jax.experimental import pallas as pl
from jax.experimental.pallas import tpu as pltpu
from jax.sharding import PartitionSpec as P

F32 = jnp.float32
BF16 = jnp.bfloat16
VMEM_LIMIT = 56 * 1024 * 1024
CHUNKS = 2


def partners(count, step):
    return [(i, i ^ step) for i in range(count)]


def swap(values, axis, step):
    return lax.ppermute(values, axis, partners(lax.axis_size(axis), step))


def base_kernel(a_ref, b_ref, w_ref, out_ref):
    step = pl.program_id(0)
    rows = jnp.concatenate([a_ref[...], b_ref[...]], axis=0)
    width = out_ref.shape[1]
    tile = 512
    for start in range(0, width, tile):
        term = jnp.dot(rows, w_ref[:, start : start + tile], preferred_element_type=F32)

        @pl.when(step == 0)
        def _():
            out_ref[:, start : start + tile] = term

        @pl.when(step > 0)
        def _():
            out_ref[:, start : start + tile] += term


def base_product(a, b, weight):
    rows, depth = a.shape
    width = weight.shape[1]
    block = 1024
    return pl.pallas_call(
        base_kernel,
        grid=(depth // block,),
        in_specs=[
            pl.BlockSpec((rows, block), lambda k: (0, k)),
            pl.BlockSpec((rows, block), lambda k: (0, k)),
            pl.BlockSpec((block, width), lambda k: (k, 0)),
        ],
        out_specs=pl.BlockSpec((2 * rows, width), lambda k: (0, 0)),
        out_shape=jax.ShapeDtypeStruct((2 * rows, width), F32),
        compiler_params=pltpu.CompilerParams(vmem_limit_bytes=VMEM_LIMIT),
        cost_estimate=pl.CostEstimate(
            flops=4 * rows * depth * width,
            bytes_accessed=2 * depth * (width + 2 * rows) + 8 * rows * width,
            transcendentals=0,
        ),
        name="base",
    )(a, b, weight)


def add_scores(a_ref, b_ref, maps_ref, total):
    step = pl.program_id(0)
    rows = jnp.concatenate([a_ref[...], b_ref[...]], axis=0)
    columns = maps_ref.shape[0]
    tile = 256
    for start in range(0, columns, tile):
        term = lax.dot_general(
            rows,
            maps_ref[start : start + tile, :],
            (((1,), (1,)), ((), ())),
            preferred_element_type=F32,
        )

        @pl.when(step == 0)
        def _():
            total[:, start : start + tile] = term

        @pl.when(step > 0)
        def _():
            total[:, start : start + tile] += term


def picked(place_ref, ids_ref, total):
    pair, rows, lanes = ids_ref.shape
    ids = ids_ref[...].reshape(pair * rows, lanes)
    upper = (lax.broadcasted_iota(jnp.int32, ids.shape, 1) >= lanes // 2).astype(jnp.int32)
    wanted = ids - upper - 16 * place_ref[0]
    found = jnp.zeros(ids.shape, F32)
    for start in range(0, total.shape[1], lanes):
        found += jnp.where(wanted == 2 * (start // lanes), total[:, start : start + lanes], 0.0)
    return found + pltpu.roll(found, lanes // 2, 1)


def near_scores_kernel(place_ref, a_ref, b_ref, maps_ref, ids_ref, out_ref, total):
    add_scores(a_ref, b_ref, maps_ref, total)

    @pl.when(pl.program_id(0) == pl.num_programs(0) - 1)
    def _():
        out_ref[...] = picked(place_ref, ids_ref, total)


def far_scores_kernel(place_ref, a_ref, b_ref, maps_ref, ids_ref, near_ref, out_ref, total):
    add_scores(a_ref, b_ref, maps_ref, total)

    @pl.when(pl.program_id(0) == pl.num_programs(0) - 1)
    def _():
        total[:, : out_ref.shape[1]] = picked(place_ref, ids_ref, total)
        place = place_ref[0]
        chip, core = place // 2, place % 2
        rows, lanes = out_ref.shape[0] // 2, out_ref.shape[1]
        half = (lax.broadcasted_iota(jnp.int32, (rows, lanes), 1) >= lanes // 2).astype(jnp.int32)
        for group in range(2):
            source = pl.ds(pl.multiple_of((group ^ core) * rows, rows), rows)
            out_ref[group * rows : (group + 1) * rows, :] = jnp.where(
                half == chip, near_ref[source, :], total[source, :lanes]
            )


def scores(place, a, b, maps, ids, near=None):
    rows, depth = a.shape
    columns = maps.shape[0]
    block = 1024
    lanes = 128
    in_specs = [
        pl.BlockSpec((rows, block), lambda k, s: (0, k)),
        pl.BlockSpec((rows, block), lambda k, s: (0, k)),
        pl.BlockSpec((columns, block), lambda k, s: (0, k)),
        pl.BlockSpec((2, rows, lanes), lambda k, s: (0, 0, 0)),
    ]
    args = [place, a, b, maps, ids]
    if near is not None:
        in_specs.append(pl.BlockSpec((2 * rows, lanes), lambda k, s: (0, 0)))
        args.append(near)
    return pl.pallas_call(
        near_scores_kernel if near is None else far_scores_kernel,
        grid_spec=pltpu.PrefetchScalarGridSpec(
            num_scalar_prefetch=1,
            grid=(depth // block,),
            in_specs=in_specs,
            out_specs=pl.BlockSpec((2 * rows, lanes), lambda k, s: (0, 0)),
            scratch_shapes=[pltpu.VMEM((2 * rows, columns), F32)],
        ),
        out_shape=jax.ShapeDtypeStruct((2 * rows, lanes), F32),
        compiler_params=pltpu.CompilerParams(vmem_limit_bytes=VMEM_LIMIT),
        cost_estimate=pl.CostEstimate(
            flops=4 * rows * depth * columns,
            bytes_accessed=2 * depth * (columns + 2 * rows),
            transcendentals=0,
        ),
        name="near_scores" if near is None else "far_scores",
    )(*args)


def combine_kernel(
    info_ref,
    near_ref,
    far_ref,
    lowrank_ref,
    ids_ref,
    own_ref,
    core_ref,
    mine_ref,
    other_ref,
    keep_ref,
    send_ref,
    spread,
    maps,
):
    rows, lanes = ids_ref.shape[1], ids_ref.shape[2]
    parity, place = info_ref[0], info_ref[1]
    half = rows

    @pl.when(pl.program_id(0) == 0)
    def _():
        upper = (lax.broadcasted_iota(jnp.int32, (rows, lanes), 1) >= lanes // 2).astype(jnp.int32)
        for slot in range(4):
            local = ((slot // 2) ^ parity) + 2 * (slot % 2)
            group = place ^ local
            packed = lowrank_ref[group % 2]
            values = jnp.where(
                upper == group // 2, packed, pltpu.roll(packed, lanes // 2, 1)
            )
            wanted = ids_ref[local] - upper
            for piece in range(8):
                spread[slot * rows : (slot + 1) * rows, piece * lanes : (piece + 1) * lanes] = (
                    jnp.where(wanted == info_ref[2 + piece], values, 0.0).astype(BF16)
                )

    maps[0:256, :] = own_ref[...]
    maps[256:512, :] = core_ref[...]
    maps[512:640, :] = mine_ref[0]
    maps[640:768, :] = mine_ref[1]
    maps[768:896, :] = other_ref[0]
    maps[896:1024, :] = other_ref[1]
    for slot in range(4):
        delta = jnp.dot(
            spread[slot * rows : (slot + 1) * rows, :], maps[...], preferred_element_type=F32
        )
        source = near_ref if slot % 2 == 0 else far_ref
        value = source[(slot // 2) ^ parity] + delta
        start = (slot % 2) * half
        if slot < 2:
            keep_ref[start : start + half, :] = value
        else:
            send_ref[start : start + half, :] = value.astype(BF16)


def combine(info, near, far, lowrank, ids, own_maps, core_maps, mine, other, chunk):
    rows, lanes = ids.shape[1], ids.shape[2]
    width = mine.shape[2]
    tile = 512
    steps = width // tile
    first = chunk * steps
    per_place = core_maps.shape[1] // tile
    held = own_maps.shape[0]
    return pl.pallas_call(
        combine_kernel,
        grid_spec=pltpu.PrefetchScalarGridSpec(
            num_scalar_prefetch=1,
            grid=(steps,),
            in_specs=[
                pl.BlockSpec((2, rows, tile), lambda n, s: (0, 0, first + n)),
                pl.BlockSpec((2, rows, tile), lambda n, s: (0, 0, first + n)),
                pl.BlockSpec((2, rows, lanes), lambda n, s: (0, 0, 0)),
                pl.BlockSpec((4, rows, lanes), lambda n, s: (0, 0, 0)),
                pl.BlockSpec((held, tile), lambda n, s: (0, s[1] * per_place + first + n)),
                pl.BlockSpec((held, tile), lambda n, s: (0, first + n)),
                pl.BlockSpec((2, held // 2, tile), lambda n, s: (0, 0, n)),
                pl.BlockSpec((2, held // 2, tile), lambda n, s: (0, 0, n)),
            ],
            out_specs=[
                pl.BlockSpec((2 * rows, tile), lambda n, s: (0, n)),
                pl.BlockSpec((2 * rows, tile), lambda n, s: (0, n)),
            ],
            scratch_shapes=[
                pltpu.VMEM((4 * rows, 4 * held), BF16),
                pltpu.VMEM((4 * held, tile), BF16),
            ],
        ),
        out_shape=[
            jax.ShapeDtypeStruct((2 * rows, width), F32),
            jax.ShapeDtypeStruct((2 * rows, width), BF16),
        ],
        compiler_params=pltpu.CompilerParams(vmem_limit_bytes=VMEM_LIMIT),
        cost_estimate=pl.CostEstimate(
            flops=32 * rows * held * width,
            bytes_accessed=26 * rows * width + 8 * held * width,
            transcendentals=0,
        ),
        name="combine",
    )(info, near, far, lowrank, ids, own_maps, core_maps, mine, other)


def per_device_fast(hidden, weight, input_maps, output_maps, slots, lists):
    rows, depth = hidden.shape
    x_core = lax.axis_index("pool")
    t = lax.axis_index("tensor")
    y = lax.axis_index("groups")
    holding, rank = input_maps.shape[:2]
    held, features = output_maps.shape
    width = features // 4
    chip, core = x_core // 2, x_core % 2

    far_a = swap(hidden, "pool", 2)
    near_b = swap(hidden, "pool", 1)

    core_maps = swap(
        lax.dynamic_slice(output_maps, (0, (x_core ^ 1) * width), (held, width)), "pool", 1
    )
    chunk_width = width // CHUNKS
    crossing = []
    for chunk in range(CHUNKS):
        start = (1 - chip) * 2 * width + chunk * chunk_width
        block = jnp.stack(
            [
                lax.dynamic_slice(
                    output_maps, (y * (held // 2), start + c * width), (held // 2, chunk_width)
                )
                for c in range(2)
            ]
        )
        block, _ = lax.optimization_barrier((block, near_b))
        crossing.append(swap(block, "pool", 2))

    order = x_core ^ jnp.arange(4, dtype=jnp.int32)
    hot = order[:, None] == jnp.arange(4, dtype=jnp.int32)[None, :]
    slots_local = jnp.sum(jnp.where(hot[:, :, None], slots.reshape(1, 4, rows), 0), axis=1)
    lists_local = jnp.sum(jnp.where(hot[:, :, None], lists[None, :, :], 0), axis=1)
    slot_ids = jnp.arange(lists.shape[1], dtype=jnp.int32)
    ids = jnp.sum(
        jnp.where(slots_local[:, :, None] == slot_ids, lists_local[:, None, :], 0), axis=2
    )
    ids = jnp.broadcast_to(ids[:, :, None], (4, rows, 128))
    place = x_core.reshape(1).astype(jnp.int32)

    flat_maps = input_maps.reshape(holding * rank, depth)
    near_lowrank = scores(place, hidden, near_b, flat_maps, ids[:2])
    near_base = base_product(hidden, near_b, weight)

    far_b = swap(far_a, "pool", 1)
    total = scores(place, far_a, far_b, flat_maps, ids[2:], near_lowrank)
    for axis, step in (("tensor", 1), ("tensor", 2), ("pool", 1), ("pool", 2)):
        total = total + swap(total.astype(BF16), axis, step).astype(F32)
    far_base = base_product(far_a, far_b, weight)
    lowrank = total.astype(BF16).astype(F32).reshape(2, rows, 128)

    mine, other = [], []
    for block in crossing:
        kept = lax.dynamic_index_in_dim(block, core, 0, keepdims=False)
        passed = lax.dynamic_index_in_dim(block, 1 - core, 0, keepdims=False)
        mine.append(jnp.stack([kept, swap(passed, "pool", 1)]))
        other.append(swap(mine[-1], "groups", 1))

    parity = (x_core ^ t) % 2
    per_owner = held // rank
    first = holding * order + per_owner * t
    half_step = per_owner // 2
    info = jnp.stack(
        [
            parity,
            x_core,
            first[0],
            first[0] + half_step,
            first[1],
            first[1] + half_step,
            first[2] + half_step * y,
            first[3] + half_step * y,
            first[2] + half_step * (1 - y),
            first[3] + half_step * (1 - y),
        ]
    ).astype(jnp.int32)

    near_base = near_base.reshape(2, rows, width)
    far_base = far_base.reshape(2, rows, width)
    side = ((x_core ^ t) // 2) % 2
    parts = []
    for chunk in range(CHUNKS):
        keep, send = combine(
            info, near_base, far_base, lowrank, ids, output_maps, core_maps,
            mine[chunk], other[chunk], chunk,
        )
        pair = keep + swap(send, "tensor", 1).astype(F32)
        pair = pair.reshape(2, rows, chunk_width)
        sent = jnp.where(side == 0, pair[1], pair[0]).astype(BF16)
        kept = jnp.where(side == 0, pair[0], pair[1])
        parts.append(kept + swap(sent, "tensor", 2).astype(F32))
    return jnp.concatenate(parts, axis=1).astype(BF16)


def per_device_general(hidden, weight, input_maps, output_maps, slots, lists):
    rows, depth = hidden.shape
    pool_count = lax.axis_size("pool")
    tensor_count = lax.axis_size("tensor")
    place = lax.axis_index("pool")
    t = lax.axis_index("tensor")
    holding, rank = input_maps.shape[:2]
    held = output_maps.shape[0]
    total_rows = rows * pool_count
    slot_ids = jnp.arange(lists.shape[1], dtype=jnp.int32)
    slot_hot = slots.reshape(pool_count, rows)[:, :, None] == slot_ids
    ids = jnp.sum(jnp.where(slot_hot, lists[:, None, :], 0), axis=2).reshape(total_rows)
    gathered = lax.all_gather(hidden, "pool", axis=0, tiled=True)
    scored = lax.dot_general(
        gathered,
        input_maps.reshape(holding * rank, depth),
        (((1,), (1,)), ((), ())),
        preferred_element_type=F32,
    ).reshape(total_rows, holding, rank)
    owned = place * holding + jnp.arange(holding, dtype=jnp.int32)
    partial = jnp.sum(
        jnp.where((ids[:, None] == owned[None, :])[:, :, None], scored, 0.0), axis=1
    )
    lowrank = lax.psum(partial, ("tensor", "pool")).astype(BF16)
    maps = lax.all_to_all(output_maps, "pool", split_axis=1, concat_axis=0, tiled=True)
    columns = jnp.arange(pool_count * held, dtype=jnp.int32)
    source = (columns // held * tensor_count + t) * held + columns % held
    pick = (source[None, :] % rank == jnp.arange(rank, dtype=jnp.int32)[:, None]).astype(BF16)
    placed = jnp.dot(lowrank, pick, preferred_element_type=F32).astype(BF16)
    spread = jnp.where(ids[:, None] == source[None, :] // rank, placed, jnp.zeros_like(placed))
    value = jnp.dot(gathered, weight, preferred_element_type=F32)
    value = value + jnp.dot(spread, maps, preferred_element_type=F32)
    mixed = lax.psum_scatter(value, "tensor", scatter_dimension=0, tiled=True)
    return mixed.astype(BF16)


def solution(mesh):
    shape = dict(mesh.shape)
    fast = shape["groups"] == 2 and shape["pool"] == 4 and shape["tensor"] == 4
    placed = (
        P(("groups", "pool"), "tensor"),
        P("tensor", "pool"),
        P("pool", None, "tensor"),
        P(("pool", "tensor"), None),
        P("groups"),
        P("groups", None),
    )
    return jax.shard_map(
        per_device_fast if fast else per_device_general,
        mesh=mesh,
        in_specs=placed,
        out_specs=P(("groups", "tensor"), "pool"),
        check_vma=False,
    )
```

```python
import jax
import jax.numpy as jnp
from jax import lax
from jax.experimental import pallas as pl
from jax.experimental.pallas import tpu as pltpu
from jax.sharding import PartitionSpec as P

F32 = jnp.float32
BF16 = jnp.bfloat16
VMEM_LIMIT = 56 * 1024 * 1024
CHUNKS = 4
CAP = 4
HALVES = 2


def partners(count, step):
    return [(i, i ^ step) for i in range(count)]


def swap(values, axis, step):
    return lax.ppermute(values, axis, partners(lax.axis_size(axis), step))


def tie(values, *after):
    return lax.optimization_barrier((values, *after))[0]


def params():
    return pltpu.CompilerParams(vmem_limit_bytes=VMEM_LIMIT)


def base_kernel(has_prior, *refs):
    if has_prior:
        prior_ref, refs = refs[0], refs[1:]
    a_ref, b_ref, w_ref, out_ref, rows = refs

    @pl.when(pl.program_id(0) == 0)
    def _():
        half = a_ref.shape[0]
        rows[:half, :] = a_ref[...]
        rows[half:, :] = b_ref[...]

    value = jnp.dot(rows[...], w_ref[...], preferred_element_type=F32)
    if has_prior:
        value += prior_ref[...]
    out_ref[...] = value


def base_product(a, b, weight, depth_block=0, prior=None, first=0, width=None):
    rows, depth = a.shape
    width = weight.shape[1] if width is None else width
    tile = 512
    in_specs = [
        pl.BlockSpec((rows, depth), lambda n: (0, 0)),
        pl.BlockSpec((rows, depth), lambda n: (0, 0)),
        pl.BlockSpec((depth, tile), lambda n: (depth_block, first // tile + n)),
    ]
    args = [a, b, weight]
    if prior is not None:
        in_specs.insert(0, pl.BlockSpec((2 * rows, tile), lambda n: (0, first // tile + n)))
        args.insert(0, prior)
    return pl.pallas_call(
        lambda *refs: base_kernel(prior is not None, *refs),
        grid=(width // tile,),
        in_specs=in_specs,
        out_specs=pl.BlockSpec((2 * rows, tile), lambda n: (0, n)),
        out_shape=jax.ShapeDtypeStruct((2 * rows, width), F32),
        scratch_shapes=[pltpu.VMEM((2 * rows, depth), BF16)],
        compiler_params=params(),
        cost_estimate=pl.CostEstimate(
            flops=4 * rows * depth * width,
            bytes_accessed=2 * depth * (width + 2 * rows) + 8 * rows * width,
            transcendentals=0,
        ),
        name="base",
    )(*args)


def scores_kernel(first, has_prior, last, chosen_ref, *refs):
    a_ref, b_ref = refs[:2]
    maps = refs[2 : 2 + 2 * CAP]
    refs = refs[2 + 2 * CAP :]
    if has_prior:
        prior_ref, refs = refs[0], refs[1:]
    if last:
        ids_ref, out_ref, total = refs
    else:
        (total,) = refs
    for pair, rows_ref in enumerate((a_ref, b_ref)):
        picked = jnp.concatenate([m[0] for m in maps[pair * CAP : (pair + 1) * CAP]], axis=0)
        term = lax.dot_general(
            rows_ref[...], picked, (((1,), (1,)), ((), ())), preferred_element_type=F32
        )

        @pl.when(pl.program_id(0) == 0)
        def _():
            total[pair] = term + prior_ref[pair] if has_prior else term

        @pl.when(pl.program_id(0) > 0)
        def _():
            total[pair] += term

    if last:

        @pl.when(pl.program_id(0) == pl.num_programs(0) - 1)
        def _():
            for pair in range(2):
                wanted = ids_ref[pair]
                lanes = wanted.shape[1]
                upper = lax.broadcasted_iota(jnp.int32, wanted.shape, 1) >= lanes // 2
                found = jnp.zeros(wanted.shape, F32)
                for k in range(0, CAP, 2):
                    spot = (first + pair) * CAP + k
                    mine = jnp.where(upper, chosen_ref[spot + 1], chosen_ref[spot])
                    column = (k // 2) * lanes
                    found += jnp.where(
                        wanted == mine, total[pair, :, column : column + lanes], 0.0
                    )
                out_ref[pair] = found + pltpu.roll(found, lanes // 2, 1)


def scores(chosen, first, a, b, maps, depth_block, prior=None, ids=None):
    rows, depth = a.shape
    rank = maps.shape[1]
    block = 1792
    steps = depth // block
    lanes = 128

    def maps_spec(spot):
        return pl.BlockSpec(
            (1, rank, block), lambda k, s: (s[spot], 0, depth_block * steps + k)
        )

    in_specs = [pl.BlockSpec((rows, block), lambda k, s: (0, k))] * 2
    in_specs += [maps_spec(first * CAP + spot) for spot in range(2 * CAP)]
    args = [a, b] + [maps] * (2 * CAP)
    if prior is not None:
        in_specs.append(pl.BlockSpec((2, rows, CAP * rank), lambda k, s: (0, 0, 0)))
        args.append(prior)
    last = ids is not None
    scratch = []
    out_columns = CAP * rank
    if last:
        in_specs.append(pl.BlockSpec((2, rows, lanes), lambda k, s: (first // 2, 0, 0)))
        args.append(ids)
        scratch = [pltpu.VMEM((2, rows, CAP * rank), F32)]
        out_columns = lanes
    has_prior = prior is not None
    return pl.pallas_call(
        lambda *refs: scores_kernel(first, has_prior, last, *refs),
        grid_spec=pltpu.PrefetchScalarGridSpec(
            num_scalar_prefetch=1,
            grid=(steps,),
            in_specs=in_specs,
            out_specs=pl.BlockSpec((2, rows, out_columns), lambda k, s: (0, 0, 0)),
            scratch_shapes=scratch,
        ),
        out_shape=jax.ShapeDtypeStruct((2, rows, out_columns), F32),
        compiler_params=params(),
        cost_estimate=pl.CostEstimate(
            flops=4 * rows * depth * CAP * rank,
            bytes_accessed=4 * depth * (CAP * rank + rows),
            transcendentals=0,
        ),
        name="scores",
    )(chosen, *args)


def spread_kernel(info_ref, lowrank_ref, ids_ref, spread_ref):
    rows, lanes = ids_ref.shape[1], ids_ref.shape[2]
    parity, place = info_ref[0], info_ref[1]
    upper = (lax.broadcasted_iota(jnp.int32, (rows, lanes), 1) >= lanes // 2).astype(jnp.int32)
    for slot in range(4):
        local = ((slot // 2) ^ parity) + 2 * (slot % 2)
        group = place ^ local
        packed = lowrank_ref[group % 2]
        values = jnp.where(upper == group // 2, packed, pltpu.roll(packed, lanes // 2, 1))
        wanted = ids_ref[local] - upper
        for piece in range(8):
            spread_ref[slot * rows : (slot + 1) * rows, piece * lanes : (piece + 1) * lanes] = (
                jnp.where(wanted == info_ref[2 + piece], values, 0.0).astype(BF16)
            )


def spread_rows(info, lowrank, ids):
    rows, lanes = ids.shape[1], ids.shape[2]
    return pl.pallas_call(
        spread_kernel,
        grid_spec=pltpu.PrefetchScalarGridSpec(
            num_scalar_prefetch=1,
            grid=(1,),
            in_specs=[
                pl.BlockSpec((2, rows, lanes), lambda n, s: (0, 0, 0)),
                pl.BlockSpec((4, rows, lanes), lambda n, s: (0, 0, 0)),
            ],
            out_specs=pl.BlockSpec((4 * rows, 8 * lanes), lambda n, s: (0, 0)),
        ),
        out_shape=jax.ShapeDtypeStruct((4 * rows, 8 * lanes), BF16),
        compiler_params=params(),
        cost_estimate=pl.CostEstimate(
            flops=16 * rows * lanes * 8, bytes_accessed=96 * rows * lanes, transcendentals=0
        ),
        name="spread",
    )(info, lowrank, ids)


def combine_kernel(
    info_ref, near_ref, far_ref, spread_ref, own_ref, core_ref, mine_ref, other_ref,
    keep_ref, send_ref, maps,
):
    parity = info_ref[0]
    rows = near_ref.shape[1]
    held = own_ref.shape[0]
    maps[0:held, :] = own_ref[...]
    maps[held : 2 * held, :] = core_ref[...]
    start = 2 * held
    for ref in (mine_ref, other_ref):
        for index in range(2):
            maps[start : start + held // 2, :] = ref[index]
            start += held // 2
    delta = jnp.dot(spread_ref[...], maps[...], preferred_element_type=F32)
    for slot in range(4):
        source = near_ref if slot % 2 == 0 else far_ref
        value = source[(slot // 2) ^ parity] + delta[slot * rows : (slot + 1) * rows]
        if slot < 2:
            keep_ref[slot % 2] = value
        else:
            send_ref[slot % 2] = value.astype(BF16)


def combine(info, near, far, spread, own_maps, core_maps, mine, other, chunk):
    width = mine.shape[2]
    rows = near.shape[1]
    tile = 256
    steps = width // tile
    first = chunk * steps
    per_place = core_maps.shape[1] // tile
    held = own_maps.shape[0]
    return pl.pallas_call(
        combine_kernel,
        grid_spec=pltpu.PrefetchScalarGridSpec(
            num_scalar_prefetch=1,
            grid=(steps,),
            in_specs=[
                pl.BlockSpec((2, rows, tile), lambda n, s: (0, 0, first + n)),
                pl.BlockSpec((2, rows, tile), lambda n, s: (0, 0, n)),
                pl.BlockSpec((4 * rows, 4 * held), lambda n, s: (0, 0)),
                pl.BlockSpec((held, tile), lambda n, s: (0, s[1] * per_place + first + n)),
                pl.BlockSpec((held, tile), lambda n, s: (0, first + n)),
                pl.BlockSpec((2, held // 2, tile), lambda n, s: (0, 0, n)),
                pl.BlockSpec((2, held // 2, tile), lambda n, s: (0, 0, n)),
            ],
            out_specs=[
                pl.BlockSpec((2, rows, tile), lambda n, s: (0, 0, n)),
                pl.BlockSpec((2, rows, tile), lambda n, s: (0, 0, n)),
            ],
            scratch_shapes=[pltpu.VMEM((4 * held, tile), BF16)],
        ),
        out_shape=[
            jax.ShapeDtypeStruct((2, rows, width), F32),
            jax.ShapeDtypeStruct((2, rows, width), BF16),
        ],
        compiler_params=params(),
        cost_estimate=pl.CostEstimate(
            flops=32 * rows * held * width,
            bytes_accessed=26 * rows * width + 8 * held * width,
            transcendentals=0,
        ),
        name="combine",
    )(info, near, far, spread, own_maps, core_maps, mine, other)


def per_device_fast(hidden, weight, input_maps, output_maps, slots, lists):
    rows, depth = hidden.shape
    place = lax.axis_index("pool")
    t = lax.axis_index("tensor")
    y = lax.axis_index("groups")
    holding, rank = input_maps.shape[:2]
    held, features = output_maps.shape
    width = features // 4
    chip, core = place >> 1, place & 1

    part = depth // HALVES
    crossed = []
    for half in range(HALVES):
        block = hidden[:, half * part : (half + 1) * part]
        if crossed:
            block = tie(block, previous)
        previous = block
        crossed.append(swap(block, "pool", 2))
    near_b = swap(tie(hidden, previous), "pool", 1)

    core_maps = swap(
        lax.dynamic_slice(output_maps, (0, (place ^ 1) * width), (held, width)), "pool", 1
    )
    chunk_width = width // CHUNKS
    blocks = []
    for chunk in range(CHUNKS):
        start = (1 - chip) * 2 * width + chunk * chunk_width
        blocks.append(
            jnp.stack(
                [
                    lax.dynamic_slice(
                        output_maps,
                        (y * (held // 2), start + c * width),
                        (held // 2, chunk_width),
                    )
                    for c in range(2)
                ]
            )
        )

    order = place ^ jnp.arange(4, dtype=jnp.int32)
    hot = order[:, None] == jnp.arange(4, dtype=jnp.int32)[None, :]
    slots_local = jnp.sum(jnp.where(hot[:, :, None], slots.reshape(1, 4, rows), 0), axis=1)
    lists_local = jnp.sum(jnp.where(hot[:, :, None], lists[None, :, :], 0), axis=1)
    positions = jnp.arange(lists.shape[1], dtype=jnp.int32)
    ids = jnp.sum(
        jnp.where(slots_local[:, :, None] == positions, lists_local[:, None, :], 0), axis=2
    )
    wide_ids = jnp.broadcast_to(ids[:, :, None], (4, rows, 128))
    owned_ids = wide_ids - place * holding
    owned = lists_local // holding == place
    earlier = positions[None, :] < positions[:, None]
    rank_in_list = jnp.sum(owned[:, None, :] & earlier[None], axis=2)
    caps = jnp.arange(CAP, dtype=jnp.int32)
    chosen = jnp.sum(
        jnp.where(
            owned[:, None, :] & (rank_in_list[:, None, :] == caps[None, :, None]),
            (lists_local % holding)[:, None, :],
            0,
        ),
        axis=2,
    ).reshape(4 * CAP)

    near_lowrank = scores(chosen, 0, hidden, near_b, input_maps, 0, ids=owned_ids)
    near_base = base_product(tie(hidden, near_lowrank), near_b, weight)
    blocks[0] = tie(blocks[0], near_b)
    crossing = [swap(block, "pool", 2) for block in blocks[: CHUNKS - 1]]

    a0 = tie(crossed[0], near_base)
    b0 = swap(a0, "pool", 1)
    raw = scores(chosen, 2, a0, b0, input_maps, 0)
    far_base = base_product(tie(a0, raw), b0, weight, 0)
    a1 = tie(crossed[1], far_base)
    b1 = swap(a1, "pool", 1)
    far_lowrank = scores(chosen, 2, a1, b1, input_maps, 1, prior=raw, ids=owned_ids)

    def by_core(values):
        return jnp.where(core == 0, values, values[::-1])

    near_lanes = (jnp.arange(128) // rank)[None, None, :] == chip
    total = jnp.where(near_lanes, by_core(near_lowrank), by_core(far_lowrank))
    total = total.reshape(2 * rows, 128)
    pieces = []
    for index, (axis, step) in enumerate(
        (("tensor", 1), ("tensor", 2), ("pool", 1), ("pool", 2))
    ):
        sent = total.astype(BF16)
        got = swap(sent, axis, step)
        if index > 0:
            crossing[index - 1] = tie(crossing[index - 1], sent)
        pieces.append(
            base_product(
                tie(a1, sent), b1, weight, 1, far_base, index * chunk_width, chunk_width
            )
        )
        if index == 3:
            crossing.append(swap(tie(blocks[-1], sent), "pool", 2))
        got = tie(got, pieces[-1])
        total = total + got.astype(F32)
    lowrank = total.reshape(2, rows, 128)

    mine, other = [], []
    for block in crossing:
        kept = jnp.where(core == 0, block[0], block[1])
        passed = jnp.where(core == 0, block[1], block[0])
        mine.append(jnp.stack([kept, swap(passed, "pool", 1)]))
        other.append(swap(mine[-1], "groups", 1))

    parity = (place ^ t) & 1
    per_owner = held // rank
    first = holding * order + per_owner * t
    half_step = per_owner // 2
    info = jnp.stack(
        [
            parity,
            place,
            first[0],
            first[0] + half_step,
            first[1],
            first[1] + half_step,
            first[2] + half_step * y,
            first[3] + half_step * y,
            first[2] + half_step * (1 - y),
            first[3] + half_step * (1 - y),
        ]
    ).astype(jnp.int32)

    spread = spread_rows(info, lowrank, wide_ids)
    near_base = near_base.reshape(2, rows, width)
    side = ((place ^ t) >> 1) & 1
    parts = []
    for chunk in range(CHUNKS):
        keep, send = combine(
            info, near_base, pieces[chunk].reshape(2, rows, chunk_width), spread,
            output_maps, core_maps, mine[chunk], other[chunk], chunk,
        )
        pair = keep + swap(send, "tensor", 1).astype(F32)
        sent = jnp.where(side == 0, pair[1], pair[0]).astype(BF16)
        kept = jnp.where(side == 0, pair[0], pair[1])
        parts.append(kept + swap(sent, "tensor", 2).astype(F32))
    return jnp.concatenate(parts, axis=1).astype(BF16)


def per_device_general(hidden, weight, input_maps, output_maps, slots, lists):
    rows, depth = hidden.shape
    pool_count = lax.axis_size("pool")
    tensor_count = lax.axis_size("tensor")
    place = lax.axis_index("pool")
    t = lax.axis_index("tensor")
    holding, rank = input_maps.shape[:2]
    held = output_maps.shape[0]
    total_rows = rows * pool_count
    slot_ids = jnp.arange(lists.shape[1], dtype=jnp.int32)
    slot_hot = slots.reshape(pool_count, rows)[:, :, None] == slot_ids
    ids = jnp.sum(jnp.where(slot_hot, lists[:, None, :], 0), axis=2).reshape(total_rows)
    gathered = lax.all_gather(hidden, "pool", axis=0, tiled=True)
    scored = lax.dot_general(
        gathered,
        input_maps.reshape(holding * rank, depth),
        (((1,), (1,)), ((), ())),
        preferred_element_type=F32,
    ).reshape(total_rows, holding, rank)
    owned = place * holding + jnp.arange(holding, dtype=jnp.int32)
    partial = jnp.sum(
        jnp.where((ids[:, None] == owned[None, :])[:, :, None], scored, 0.0), axis=1
    )
    lowrank = lax.psum(partial, ("tensor", "pool")).astype(BF16)
    maps = lax.all_to_all(output_maps, "pool", split_axis=1, concat_axis=0, tiled=True)
    columns = jnp.arange(pool_count * held, dtype=jnp.int32)
    source = (columns // held * tensor_count + t) * held + columns % held
    pick = (source[None, :] % rank == jnp.arange(rank, dtype=jnp.int32)[:, None]).astype(BF16)
    placed = jnp.dot(lowrank, pick, preferred_element_type=F32).astype(BF16)
    spread = jnp.where(ids[:, None] == source[None, :] // rank, placed, jnp.zeros_like(placed))
    value = jnp.dot(gathered, weight, preferred_element_type=F32)
    value = value + jnp.dot(spread, maps, preferred_element_type=F32)
    mixed = lax.psum_scatter(value, "tensor", scatter_dimension=0, tiled=True)
    return mixed.astype(BF16)


def solution(mesh):
    shape = dict(mesh.shape)
    fast = shape["groups"] == 2 and shape["pool"] == 4 and shape["tensor"] == 4
    placed = (
        P(("groups", "pool"), "tensor"),
        P("tensor", "pool"),
        P("pool", None, "tensor"),
        P(("pool", "tensor"), None),
        P("groups"),
        P("groups", None),
    )
    return jax.shard_map(
        per_device_fast if fast else per_device_general,
        mesh=mesh,
        in_specs=placed,
        out_specs=P(("groups", "tensor"), "pool"),
        check_vma=False,
    )
```

```python
import jax
import jax.numpy as jnp
from jax import lax
from jax.experimental import pallas as pl
from jax.experimental.pallas import tpu as pltpu
from jax.sharding import PartitionSpec as P

F32 = jnp.float32
BF16 = jnp.bfloat16
VMEM_LIMIT = 40 * 1024 * 1024
WIDTHS = (512, 512, 512, 512)
CAP = 4
HALVES = 2
HINT = 1000


def partners(count, step):
    return [(i, i ^ step) for i in range(count)]


def swap(values, axis, step):
    return lax.ppermute(values, axis, partners(lax.axis_size(axis), step))


def tie(values, *after):
    return lax.optimization_barrier((values, *after))[0]


def cost(flops, moved):
    return pl.CostEstimate(flops=flops // HINT, bytes_accessed=moved // HINT, transcendentals=0)


def params():
    return pltpu.CompilerParams(vmem_limit_bytes=VMEM_LIMIT)


def base_kernel(count, has_prior, *refs):
    a_ref, pieces, refs = refs[0], refs[1 : 1 + count], refs[1 + count :]
    if has_prior:
        prior_ref, refs = refs[0], refs[1:]
    w_ref, out_ref, rows = refs

    @pl.when(pl.program_id(0) == 0)
    def _():
        half = a_ref.shape[0]
        rows[:half, :] = a_ref[...]
        start = 0
        for piece in pieces:
            rows[half:, start : start + piece.shape[1]] = piece[...]
            start += piece.shape[1]

    value = jnp.dot(rows[...], w_ref[...], preferred_element_type=F32)
    if has_prior:
        value += prior_ref[...]
    out_ref[...] = value


def base_product(a, pieces, weight, depth_block=0, prior=None, first=0, width=None, tile=512):
    rows, depth = a.shape
    width = weight.shape[1] if width is None else width
    in_specs = [pl.BlockSpec(x.shape, lambda n: (0, 0)) for x in (a, *pieces)]
    args = [a, *pieces]
    if prior is not None:
        in_specs.append(pl.BlockSpec((2 * rows, tile), lambda n: (0, first // tile + n)))
        args.append(prior)
    in_specs.append(pl.BlockSpec((depth, tile), lambda n: (depth_block, first // tile + n)))
    args.append(weight)
    return pl.pallas_call(
        lambda *refs: base_kernel(len(pieces), prior is not None, *refs),
        grid=(width // tile,),
        in_specs=in_specs,
        out_specs=pl.BlockSpec((2 * rows, tile), lambda n: (0, n)),
        out_shape=jax.ShapeDtypeStruct((2 * rows, width), F32),
        scratch_shapes=[pltpu.VMEM((2 * rows, depth), BF16)],
        compiler_params=params(),
        cost_estimate=cost(
            4 * rows * depth * width, 2 * depth * (width + 2 * rows) + 8 * rows * width
        ),
        name="base",
    )(*args)


def scores_kernel(first, offset, count, has_prior, last, info_ref, *refs):
    a_ref, pieces, maps_ref = refs[0], refs[1 : 1 + count], refs[1 + count]
    refs = refs[2 + count :]
    if has_prior:
        prior_ref, refs = refs[0], refs[1:]
    if first == 2 and last:
        near_ref, refs = refs[0], refs[1:]
    if last:
        ids_ref, refs = refs[0], refs[1:]
    outs, (rows, maps, row_sems, map_sems) = refs[:-4], refs[-4:]
    depth = rows.shape[2]
    cut = depth // 2

    def map_copy(pair, k, part):
        chosen = info_ref[1 + (first + pair) * CAP + k]
        return pltpu.make_async_copy(
            maps_ref.at[chosen, :, pl.ds(offset + part * cut, cut)],
            maps.at[pair * CAP + k, :, pl.ds(part * cut, cut)],
            map_sems.at[pair, k, part],
        )

    row_copies = [pltpu.make_async_copy(a_ref, rows.at[0], row_sems.at[0])]
    start = 0
    for index, piece in enumerate(pieces):
        row_copies.append(
            pltpu.make_async_copy(
                piece, rows.at[1, :, pl.ds(start, piece.shape[1])], row_sems.at[1 + index]
            )
        )
        start += piece.shape[1]
    for pair in range(2):
        for copy in row_copies[:1] if pair == 0 else row_copies[1:]:
            copy.start()
        for part in range(2):
            for k in range(CAP):
                map_copy(pair, k, part).start()
    for pair in range(2):
        for copy in row_copies[:1] if pair == 0 else row_copies[1:]:
            copy.wait()
        total = prior_ref[pair] if has_prior else None
        for part in range(2):
            for k in range(CAP):
                map_copy(pair, k, part).wait()
            columns = slice(part * cut, (part + 1) * cut)
            chosen = maps[pair * CAP : (pair + 1) * CAP, :, columns]
            term = lax.dot_general(
                chosen.reshape(-1, cut),
                rows[pair, :, columns],
                (((1,), (1,)), ((), ())),
                preferred_element_type=F32,
            )
            total = term if total is None else total + term
        if not last:
            outs[0][pair] = total
            continue
        wanted = ids_ref[pair]
        rank = total.shape[0] // CAP
        found = jnp.zeros((rank, total.shape[1]), F32)
        for k in range(CAP):
            mine = info_ref[1 + (first + pair) * CAP + k]
            found += jnp.where(wanted == mine, total[k * rank : (k + 1) * rank], 0.0)
        if first == 0:
            outs[0][pair] = found
        else:
            near_group = info_ref[0] ^ pair
            far_group = near_group ^ 2
            outs[0][far_group] = found
            outs[1][far_group] = found.astype(BF16)
            outs[0][near_group] = near_ref[pair]
            outs[1][near_group] = near_ref[pair].astype(BF16)


def scores(info, first, a, pieces, maps, half, prior=None, near=None, ids=None):
    rows, depth = a.shape
    rank = maps.shape[1]
    has_prior, last = prior is not None, ids is not None
    whole = lambda x: pl.BlockSpec(x.shape, lambda k, s: (0,) * x.ndim)
    args = [a, *pieces, maps]
    in_specs = [pl.BlockSpec(memory_space=pl.ANY)] * len(args)
    if has_prior:
        in_specs.append(whole(prior))
        args.append(prior)
    if near is not None:
        in_specs.append(whole(near))
        args.append(near)
    if last:
        in_specs.append(
            pl.BlockSpec((2,) + ids.shape[1:], lambda k, s: (first // 2, 0, 0))
        )
        args.append(ids)
    if not last:
        out_shape = [jax.ShapeDtypeStruct((2, CAP * rank, rows), F32)]
    elif first == 0:
        out_shape = [jax.ShapeDtypeStruct((2, rank, rows), F32)]
    else:
        out_shape = [jax.ShapeDtypeStruct((4, rank, rows), kind) for kind in (F32, BF16)]
    return pl.pallas_call(
        lambda *refs: scores_kernel(first, half * depth, len(pieces), has_prior, last, *refs),
        grid_spec=pltpu.PrefetchScalarGridSpec(
            num_scalar_prefetch=1,
            grid=(1,),
            in_specs=in_specs,
            out_specs=[whole(x) for x in out_shape],
            scratch_shapes=[
                pltpu.VMEM((2, rows, depth), BF16),
                pltpu.VMEM((2 * CAP, rank, depth), BF16),
                pltpu.SemaphoreType.DMA((1 + len(pieces),)),
                pltpu.SemaphoreType.DMA((2, CAP, 2)),
            ],
        ),
        out_shape=out_shape,
        compiler_params=params(),
        cost_estimate=cost(4 * rows * depth * CAP * rank, 4 * depth * (CAP * rank + rows)),
        name="scores",
    )(info, *args)


def build_spread(info_ref, lowrank_ref, got_ref, ids_ref, spread):
    rows, lanes = ids_ref.shape[1], ids_ref.shape[2]
    parity, place = info_ref[0], info_ref[1]
    upper = (lax.broadcasted_iota(jnp.int32, (rows, lanes), 1) >= lanes // 2).astype(jnp.int32)
    for slot in range(4):
        local = ((slot // 2) ^ parity) + 2 * (slot % 2)
        group = place ^ local
        values = lowrank_ref[group] + got_ref[group].astype(F32)
        values = jnp.concatenate([values, values], axis=0).T
        wanted = ids_ref[local] - upper
        for piece in range(8):
            spread[slot * rows : (slot + 1) * rows, piece * lanes : (piece + 1) * lanes] = (
                jnp.where(wanted == info_ref[2 + piece], values, 0.0).astype(BF16)
            )


def combine_kernel(build, info_ref, *refs):
    if build:
        lowrank_ref, got_ref, ids_ref, refs = refs[0], refs[1], refs[2], refs[3:]
        near_ref, far_ref, own_ref, core_ref, *blocks, keep_ref, send_ref, spread_ref, maps = refs

        @pl.when(pl.program_id(0) == 0)
        def _():
            build_spread(info_ref, lowrank_ref, got_ref, ids_ref, spread_ref)

    else:
        spread_ref, near_ref, far_ref, own_ref, core_ref, *blocks, keep_ref, send_ref, maps = refs
    parity = info_ref[0]
    rows = near_ref.shape[1]
    held = own_ref.shape[0]
    maps[0:held, :] = own_ref[...]
    maps[held : 2 * held, :] = core_ref[...]
    start = 2 * held
    for ref in blocks:
        maps[start : start + held // 2, :] = ref[0]
        start += held // 2
    delta = jnp.dot(spread_ref[...], maps[...], preferred_element_type=F32)
    for slot in range(4):
        source = near_ref if slot % 2 == 0 else far_ref
        value = source[(slot // 2) ^ parity] + delta[slot * rows : (slot + 1) * rows]
        if slot < 2:
            keep_ref[slot % 2] = value
        else:
            send_ref[slot % 2] = value.astype(BF16)


def combine(info, near, far, own_maps, core_maps, blocks, start, spread=None, build=()):
    rows = near.shape[1]
    width = far.shape[2]
    tile = 512
    first = start // tile
    per_place = core_maps.shape[1] // tile
    held = own_maps.shape[0]
    whole = lambda shape: pl.BlockSpec(shape, lambda n, s: (0,) * len(shape))
    ahead = list(build) if build else [spread]
    spread_shape = (4 * rows, 4 * held)
    in_specs = [whole(x.shape) for x in ahead]
    in_specs += [
        pl.BlockSpec((2, rows, tile), lambda n, s: (0, 0, first + n)),
        pl.BlockSpec((2, rows, tile), lambda n, s: (0, 0, n)),
        pl.BlockSpec((held, tile), lambda n, s: (0, s[1] * per_place + first + n)),
        pl.BlockSpec((held, tile), lambda n, s: (0, first + n)),
    ]
    in_specs += [
        pl.BlockSpec((1, held // 2, tile), lambda n, s, index=index: (index, 0, n))
        for _, index in blocks
    ]
    out_specs = [pl.BlockSpec((2, rows, tile), lambda n, s: (0, 0, n))] * 2
    out_shape = [jax.ShapeDtypeStruct((2, rows, width), kind) for kind in (F32, BF16)]
    if build:
        out_specs.append(whole(spread_shape))
        out_shape.append(jax.ShapeDtypeStruct(spread_shape, BF16))
    return pl.pallas_call(
        lambda *refs: combine_kernel(bool(build), *refs),
        grid_spec=pltpu.PrefetchScalarGridSpec(
            num_scalar_prefetch=1,
            grid=(width // tile,),
            in_specs=in_specs,
            out_specs=out_specs,
            scratch_shapes=[pltpu.VMEM((4 * held, tile), BF16)],
        ),
        out_shape=out_shape,
        compiler_params=params(),
        cost_estimate=cost(
            32 * rows * held * width, 26 * rows * width + 8 * held * width
        ),
        name="combine",
    )(info, *ahead, near, far, own_maps, core_maps, *[block for block, _ in blocks])


def per_device_fast(hidden, weight, input_maps, output_maps, slots, lists):
    rows, depth = hidden.shape
    place = lax.axis_index("pool")
    t = lax.axis_index("tensor")
    y = lax.axis_index("groups")
    holding, rank = input_maps.shape[:2]
    held, features = output_maps.shape
    width = features // 4
    chip, core = place >> 1, place & 1
    starts = [sum(WIDTHS[:i]) for i in range(len(WIDTHS))]
    count = len(WIDTHS)

    part = depth // HALVES
    crossed = [swap(hidden[:, h * part : (h + 1) * part], "pool", 2) for h in range(HALVES)]
    near_b = swap(hidden, "pool", 1)

    core_block = lax.dynamic_slice(output_maps, (0, (place ^ 1) * width), (held, width))
    blocks = [
        jnp.stack(
            [
                lax.dynamic_slice(
                    output_maps,
                    (y * (held // 2), (place ^ other) * width + start),
                    (held // 2, wide),
                )
                for other in (2, 3)
            ]
        )
        for start, wide in zip(starts, WIDTHS)
    ]

    order = place ^ jnp.arange(4, dtype=jnp.int32)
    hot = order[:, None] == jnp.arange(4, dtype=jnp.int32)[None, :]
    slots_local = jnp.sum(jnp.where(hot[:, :, None], slots.reshape(1, 4, rows), 0), axis=1)
    lists_local = jnp.sum(jnp.where(hot[:, :, None], lists[None, :, :], 0), axis=1)
    positions = jnp.arange(lists.shape[1], dtype=jnp.int32)
    ids = jnp.sum(
        jnp.where(slots_local[:, :, None] == positions, lists_local[:, None, :], 0), axis=2
    )
    wide_ids = jnp.broadcast_to(ids[:, :, None], (4, rows, 128))
    owned_ids = (ids - place * holding).reshape(4, 1, rows)
    owned = (lists_local >= place * holding) & (lists_local < (place + 1) * holding)
    earlier = positions[None, :] < positions[:, None]
    rank_in_list = jnp.sum(owned[:, None, :] & earlier[None], axis=2)
    caps = jnp.arange(CAP, dtype=jnp.int32)
    chosen = jnp.sum(
        jnp.where(
            owned[:, None, :] & (rank_in_list[:, None, :] == caps[None, :, None]),
            (lists_local - place * holding)[:, None, :],
            0,
        ),
        axis=2,
    ).reshape(4 * CAP)
    picks = jnp.concatenate([place.reshape(1), chosen]).astype(jnp.int32)

    parity = (place ^ t) & 1
    per_owner = held // rank
    half_step = per_owner // 2
    owner_first = [holding * (place ^ j) + per_owner * t for j in range(4)]
    info = jnp.stack(
        [parity, place]
        + [owner_first[j] + half_step * h for j in (0, 1) for h in (0, 1)]
        + [owner_first[2] + half_step * y, owner_first[3] + half_step * y]
        + [owner_first[2] + half_step * (1 - y), owner_first[3] + half_step * (1 - y)]
    ).astype(jnp.int32)

    ready = lax.optimization_barrier(
        (hidden, near_b, picks, info, wide_ids, owned_ids, core_block, *blocks)
    )
    own_rows, near_b, picks, info, wide_ids, owned_ids, core_block, *blocks = ready
    core_maps = swap(core_block, "pool", 1)

    (near_lowrank,) = scores(picks, 0, own_rows, [near_b], input_maps, 0, ids=owned_ids)
    near_base = base_product(tie(own_rows, near_lowrank), [near_b], weight)
    crossing = [swap(block, "pool", 2) for block in blocks[: count - 1]]

    a0 = tie(crossed[0], near_base)
    b0 = [swap(a0[:, k * (part // 2) : (k + 1) * (part // 2)], "pool", 1) for k in range(2)]
    (raw,) = scores(picks, 2, a0, b0, input_maps, 0)
    far_base = base_product(tie(a0, raw), b0, weight, 0)
    a1 = tie(crossed[1], far_base)
    b1 = [swap(a1, "pool", 1)]
    total, sent = scores(
        picks, 2, a1, b1, input_maps, 1, prior=raw, near=near_lowrank, ids=owned_ids
    )

    def far_piece(index, after):
        return base_product(
            tie(a1, after), b1, weight, 1, far_base, starts[index], WIDTHS[index], 256
        ).reshape(2, rows, WIDTHS[index])

    hops = (("tensor", 1), ("tensor", 2), ("pool", 1), ("pool", 2))
    pieces = []
    for index, (axis, step) in enumerate(hops):
        if index > 0:
            sent = total.astype(BF16)
        got = swap(sent, axis, step)
        if index < count - 1:
            crossing[index] = tie(crossing[index], sent)
            got = tie(got, crossing[index])
        if index == 1:
            pieces.append(far_piece(0, sent))
            got = tie(got, pieces[-1])
        if index == 3:
            crossing.append(swap(tie(blocks[-1], sent), "pool", 2))
            break
        total = total + got.astype(F32)

    def over_y(index, after):
        block = crossing[index] if after is None else tie(crossing[index], after)
        return block, swap(block, "pool", 1), swap(block, "groups", 1)

    def blocks_of(index, after):
        block, beside, across = moved[index]
        across = across if after is None else tie(across, after)
        return [(block, 0), (beside, 1), (across, 0), (swap(across, "pool", 1), 1)]

    moved = [over_y(index, None) for index in range(count - 1)]

    near_base = near_base.reshape(2, rows, width)
    side = ((place ^ t) >> 1) & 1
    parts = []
    spread = send = None
    for chunk in range(count):
        common = (
            info, near_base, pieces[chunk], output_maps, core_maps,
            blocks_of(chunk, send if chunk else None), starts[chunk],
        )
        if chunk == 0:
            keep, send, spread = combine(*common, build=(total, got, wide_ids))
            moved.append(over_y(count - 1, send))
        else:
            keep, send = combine(*common, spread=spread)
        if chunk + 1 < count:
            pieces.append(far_piece(chunk + 1, send))
        pair = keep + swap(send, "tensor", 1).astype(F32)
        sent = jnp.where(side == 0, pair[1], pair[0]).astype(BF16)
        kept = jnp.where(side == 0, pair[0], pair[1])
        parts.append(kept + swap(sent, "tensor", 2).astype(F32))
    return jnp.concatenate(parts, axis=1).astype(BF16)


def per_device_general(hidden, weight, input_maps, output_maps, slots, lists):
    rows, depth = hidden.shape
    pool_count = lax.axis_size("pool")
    tensor_count = lax.axis_size("tensor")
    place = lax.axis_index("pool")
    t = lax.axis_index("tensor")
    holding, rank = input_maps.shape[:2]
    held = output_maps.shape[0]
    total_rows = rows * pool_count
    slot_ids = jnp.arange(lists.shape[1], dtype=jnp.int32)
    slot_hot = slots.reshape(pool_count, rows)[:, :, None] == slot_ids
    ids = jnp.sum(jnp.where(slot_hot, lists[:, None, :], 0), axis=2).reshape(total_rows)
    gathered = lax.all_gather(hidden, "pool", axis=0, tiled=True)
    scored = lax.dot_general(
        gathered,
        input_maps.reshape(holding * rank, depth),
        (((1,), (1,)), ((), ())),
        preferred_element_type=F32,
    ).reshape(total_rows, holding, rank)
    owned = place * holding + jnp.arange(holding, dtype=jnp.int32)
    partial = jnp.sum(
        jnp.where((ids[:, None] == owned[None, :])[:, :, None], scored, 0.0), axis=1
    )
    lowrank = lax.psum(partial, ("tensor", "pool")).astype(BF16)
    maps = lax.all_to_all(output_maps, "pool", split_axis=1, concat_axis=0, tiled=True)
    columns = jnp.arange(pool_count * held, dtype=jnp.int32)
    source = (columns // held * tensor_count + t) * held + columns % held
    pick = (source[None, :] % rank == jnp.arange(rank, dtype=jnp.int32)[:, None]).astype(BF16)
    placed = jnp.dot(lowrank, pick, preferred_element_type=F32).astype(BF16)
    spread = jnp.where(ids[:, None] == source[None, :] // rank, placed, jnp.zeros_like(placed))
    value = jnp.dot(gathered, weight, preferred_element_type=F32)
    value = value + jnp.dot(spread, maps, preferred_element_type=F32)
    mixed = lax.psum_scatter(value, "tensor", scatter_dimension=0, tiled=True)
    return mixed.astype(BF16)


def solution(mesh):
    shape = dict(mesh.shape)
    fast = shape["groups"] == 2 and shape["pool"] == 4 and shape["tensor"] == 4
    placed = (
        P(("groups", "pool"), "tensor"),
        P("tensor", "pool"),
        P("pool", None, "tensor"),
        P(("pool", "tensor"), None),
        P("groups"),
        P("groups", None),
    )
    return jax.shard_map(
        per_device_fast if fast else per_device_general,
        mesh=mesh,
        in_specs=placed,
        out_specs=P(("groups", "tensor"), "pool"),
        check_vma=False,
    )
```

```python
import jax
import jax.numpy as jnp
from jax import lax
from jax.experimental import pallas as pl
from jax.experimental.pallas import tpu as pltpu
from jax.sharding import PartitionSpec as P

F32 = jnp.float32
BF16 = jnp.bfloat16
VMEM_LIMIT = 40 * 1024 * 1024
WIDTHS = (512, 1024, 512)
EARLY = 2
CAP = 4
HALVES = 2
HINT = 1000


def partners(count, step):
    return [(i, i ^ step) for i in range(count)]


def swap(values, axis, step):
    return lax.ppermute(values, axis, partners(lax.axis_size(axis), step))


def tie(values, *after):
    return lax.optimization_barrier((values, *after))[0]


def cost(flops, moved):
    return pl.CostEstimate(flops=flops // HINT, bytes_accessed=moved // HINT, transcendentals=0)


def params():
    return pltpu.CompilerParams(vmem_limit_bytes=VMEM_LIMIT)


def base_kernel(lower, upper, has_prior, *refs):
    pieces, refs = refs[: lower + upper], refs[lower + upper :]
    if has_prior:
        prior_ref, refs = refs[0], refs[1:]
    w_ref, out_ref, rows = refs

    @pl.when(pl.program_id(0) == 0)
    def _():
        half = rows.shape[0] // 2
        for top, group in ((0, pieces[:lower]), (half, pieces[lower:])):
            start = 0
            for piece in group:
                rows[top : top + half, start : start + piece.shape[1]] = piece[...]
                start += piece.shape[1]

    value = jnp.dot(rows[...], w_ref[...], preferred_element_type=F32)
    if has_prior:
        value += prior_ref[...]
    out_ref[...] = value


def product(lower, upper, weight, depth_block, prior, first, width, tile, prior_first=0):
    rows = lower[0].shape[0]
    depth = sum(x.shape[1] for x in lower)
    args = [*lower, *upper]
    in_specs = [pl.BlockSpec(x.shape, lambda n: (0, 0)) for x in args]
    if prior is not None:
        in_specs.append(pl.BlockSpec((2 * rows, tile), lambda n: (0, prior_first // tile + n)))
        args.append(prior)
    in_specs.append(pl.BlockSpec((depth, tile), lambda n: (depth_block, first // tile + n)))
    args.append(weight)
    return pl.pallas_call(
        lambda *refs: base_kernel(len(lower), len(upper), prior is not None, *refs),
        grid=(width // tile,),
        in_specs=in_specs,
        out_specs=pl.BlockSpec((2 * rows, tile), lambda n: (0, n)),
        out_shape=jax.ShapeDtypeStruct((2 * rows, width), F32),
        scratch_shapes=[pltpu.VMEM((2 * rows, depth), BF16)],
        compiler_params=params(),
        cost_estimate=cost(
            4 * rows * depth * width, 2 * depth * (width + 2 * rows) + 8 * rows * width
        ),
        name="base",
    )(*args)


def base_product(a, pieces, weight, depth_block=0, prior=None, first=0, width=None, tile=512):
    width = weight.shape[1] if width is None else width
    return product([a], pieces, weight, depth_block, prior, first, width, tile)


def whole_product(a_pieces, b_pieces, weight, first, width, tile):
    flat = [x for pieces in b_pieces for x in pieces]
    return product(a_pieces, flat, weight, 0, None, first, width, tile)


def scores_kernel(first, offset, count, has_prior, last, info_ref, *refs):
    a_ref, pieces, maps_ref = refs[0], refs[1 : 1 + count], refs[1 + count]
    refs = refs[2 + count :]
    if has_prior:
        prior_ref, refs = refs[0], refs[1:]
    if first == 2 and last:
        near_ref, refs = refs[0], refs[1:]
    if last:
        ids_ref, refs = refs[0], refs[1:]
    outs, (rows, maps, row_sems, map_sems) = refs[:-4], refs[-4:]
    depth = rows.shape[2]
    cut = depth // 2

    def map_copy(pair, k, part):
        chosen = info_ref[1 + (first + pair) * CAP + k]
        return pltpu.make_async_copy(
            maps_ref.at[chosen, :, pl.ds(offset + part * cut, cut)],
            maps.at[pair * CAP + k, :, pl.ds(part * cut, cut)],
            map_sems.at[pair, k, part],
        )

    row_copies = [pltpu.make_async_copy(a_ref, rows.at[0], row_sems.at[0])]
    start = 0
    for index, piece in enumerate(pieces):
        row_copies.append(
            pltpu.make_async_copy(
                piece, rows.at[1, :, pl.ds(start, piece.shape[1])], row_sems.at[1 + index]
            )
        )
        start += piece.shape[1]
    for pair in range(2):
        for copy in row_copies[:1] if pair == 0 else row_copies[1:]:
            copy.start()
        for part in range(2):
            for k in range(CAP):
                map_copy(pair, k, part).start()
    for pair in range(2):
        for copy in row_copies[:1] if pair == 0 else row_copies[1:]:
            copy.wait()
        total = prior_ref[pair] if has_prior else None
        for part in range(2):
            for k in range(CAP):
                map_copy(pair, k, part).wait()
            columns = slice(part * cut, (part + 1) * cut)
            chosen = maps[pair * CAP : (pair + 1) * CAP, :, columns]
            term = lax.dot_general(
                chosen.reshape(-1, cut),
                rows[pair, :, columns],
                (((1,), (1,)), ((), ())),
                preferred_element_type=F32,
            )
            total = term if total is None else total + term
        if not last:
            outs[0][pair] = total
            continue
        wanted = ids_ref[pair]
        rank = total.shape[0] // CAP
        found = jnp.zeros((rank, total.shape[1]), F32)
        for k in range(CAP):
            mine = info_ref[1 + (first + pair) * CAP + k]
            found += jnp.where(wanted == mine, total[k * rank : (k + 1) * rank], 0.0)
        if first == 0:
            outs[0][pair] = found
        else:
            near_group = info_ref[0] ^ pair
            far_group = near_group ^ 2
            outs[0][far_group] = found
            outs[1][far_group] = found.astype(BF16)
            outs[0][near_group] = near_ref[pair]
            outs[1][near_group] = near_ref[pair].astype(BF16)


def scores(info, first, a, pieces, maps, half, prior=None, near=None, ids=None):
    rows, depth = a.shape
    rank = maps.shape[1]
    has_prior, last = prior is not None, ids is not None
    whole = lambda x: pl.BlockSpec(x.shape, lambda k, s: (0,) * x.ndim)
    args = [a, *pieces, maps]
    in_specs = [pl.BlockSpec(memory_space=pl.ANY)] * len(args)
    if has_prior:
        in_specs.append(whole(prior))
        args.append(prior)
    if near is not None:
        in_specs.append(whole(near))
        args.append(near)
    if last:
        in_specs.append(
            pl.BlockSpec((2,) + ids.shape[1:], lambda k, s: (first // 2, 0, 0))
        )
        args.append(ids)
    if not last:
        out_shape = [jax.ShapeDtypeStruct((2, CAP * rank, rows), F32)]
    elif first == 0:
        out_shape = [jax.ShapeDtypeStruct((2, rank, rows), F32)]
    else:
        out_shape = [jax.ShapeDtypeStruct((4, rank, rows), kind) for kind in (F32, BF16)]
    return pl.pallas_call(
        lambda *refs: scores_kernel(first, half * depth, len(pieces), has_prior, last, *refs),
        grid_spec=pltpu.PrefetchScalarGridSpec(
            num_scalar_prefetch=1,
            grid=(1,),
            in_specs=in_specs,
            out_specs=[whole(x) for x in out_shape],
            scratch_shapes=[
                pltpu.VMEM((2, rows, depth), BF16),
                pltpu.VMEM((2 * CAP, rank, depth), BF16),
                pltpu.SemaphoreType.DMA((1 + len(pieces),)),
                pltpu.SemaphoreType.DMA((2, CAP, 2)),
            ],
        ),
        out_shape=out_shape,
        compiler_params=params(),
        cost_estimate=cost(4 * rows * depth * CAP * rank, 4 * depth * (CAP * rank + rows)),
        name="scores",
    )(info, *args)


def build_spread(info_ref, lowrank_ref, got_ref, ids_ref, spread):
    rows, lanes = ids_ref.shape[1], ids_ref.shape[2]
    parity, place = info_ref[0], info_ref[1]
    upper = (lax.broadcasted_iota(jnp.int32, (rows, lanes), 1) >= lanes // 2).astype(jnp.int32)
    for slot in range(4):
        local = ((slot // 2) ^ parity) + 2 * (slot % 2)
        group = place ^ local
        values = lowrank_ref[group] + got_ref[group].astype(F32)
        values = jnp.concatenate([values, values], axis=0).T
        wanted = ids_ref[local] - upper
        for piece in range(8):
            spread[slot * rows : (slot + 1) * rows, piece * lanes : (piece + 1) * lanes] = (
                jnp.where(wanted == info_ref[2 + piece], values, 0.0).astype(BF16)
            )


def combine_kernel(build, info_ref, *refs):
    if build:
        lowrank_ref, got_ref, ids_ref, refs = refs[0], refs[1], refs[2], refs[3:]
        near_ref, far_ref, own_ref, core_ref, *blocks, keep_ref, send_ref, spread_ref, maps = refs

        @pl.when(pl.program_id(0) == 0)
        def _():
            build_spread(info_ref, lowrank_ref, got_ref, ids_ref, spread_ref)

    else:
        spread_ref, near_ref, far_ref, own_ref, core_ref, *blocks, keep_ref, send_ref, maps = refs
    parity = info_ref[0]
    rows = near_ref.shape[1]
    held = own_ref.shape[0]
    maps[0:held, :] = own_ref[...]
    maps[held : 2 * held, :] = core_ref[...]
    start = 2 * held
    for ref in blocks:
        maps[start : start + held // 2, :] = ref[0]
        start += held // 2
    delta = jnp.dot(spread_ref[...], maps[...], preferred_element_type=F32)
    for slot in range(4):
        source = near_ref if slot % 2 == 0 else far_ref
        value = source[(slot // 2) ^ parity] + delta[slot * rows : (slot + 1) * rows]
        if slot < 2:
            keep_ref[slot % 2] = value
        else:
            send_ref[slot % 2] = value.astype(BF16)


def combine(info, near, far, own_maps, core_maps, blocks, start, spread=None, build=()):
    rows = near.shape[1]
    width = far.shape[2]
    tile = 512
    first = start // tile
    per_place = core_maps.shape[1] // tile
    held = own_maps.shape[0]
    whole = lambda shape: pl.BlockSpec(shape, lambda n, s: (0,) * len(shape))
    ahead = list(build) if build else [spread]
    spread_shape = (4 * rows, 4 * held)
    in_specs = [whole(x.shape) for x in ahead]
    in_specs += [
        pl.BlockSpec((2, rows, tile), lambda n, s: (0, 0, first + n)),
        pl.BlockSpec((2, rows, tile), lambda n, s: (0, 0, n)),
        pl.BlockSpec((held, tile), lambda n, s: (0, s[1] * per_place + first + n)),
        pl.BlockSpec((held, tile), lambda n, s: (0, first + n)),
    ]
    in_specs += [
        pl.BlockSpec((1, held // 2, tile), lambda n, s, index=index: (index, 0, n))
        for _, index in blocks
    ]
    out_specs = [pl.BlockSpec((2, rows, tile), lambda n, s: (0, 0, n))] * 2
    out_shape = [jax.ShapeDtypeStruct((2, rows, width), kind) for kind in (F32, BF16)]
    if build:
        out_specs.append(whole(spread_shape))
        out_shape.append(jax.ShapeDtypeStruct(spread_shape, BF16))
    return pl.pallas_call(
        lambda *refs: combine_kernel(bool(build), *refs),
        grid_spec=pltpu.PrefetchScalarGridSpec(
            num_scalar_prefetch=1,
            grid=(width // tile,),
            in_specs=in_specs,
            out_specs=out_specs,
            scratch_shapes=[pltpu.VMEM((4 * held, tile), BF16)],
        ),
        out_shape=out_shape,
        compiler_params=params(),
        cost_estimate=cost(
            32 * rows * held * width, 26 * rows * width + 8 * held * width
        ),
        name="combine",
    )(info, *ahead, near, far, own_maps, core_maps, *[block for block, _ in blocks])


def per_device_fast(hidden, weight, input_maps, output_maps, slots, lists):
    rows, depth = hidden.shape
    place = lax.axis_index("pool")
    t = lax.axis_index("tensor")
    y = lax.axis_index("groups")
    holding, rank = input_maps.shape[:2]
    held, features = output_maps.shape
    width = features // 4
    chip, core = place >> 1, place & 1
    starts = [sum(WIDTHS[:i]) for i in range(len(WIDTHS))]
    count = len(WIDTHS)

    part = depth // HALVES
    near_b = swap(hidden, "pool", 1)
    crossed, block = [], None
    for h in range(HALVES):
        source = hidden if block is None else tie(hidden, block)
        block = source[:, h * part : (h + 1) * part]
        crossed.append(swap(block, "pool", 2))

    core_block = lax.dynamic_slice(output_maps, (0, (place ^ 1) * width), (held, width))
    blocks = [
        jnp.stack(
            [
                lax.dynamic_slice(
                    output_maps,
                    (y * (held // 2), (place ^ other) * width + start),
                    (held // 2, wide),
                )
                for other in (2, 3)
            ]
        )
        for start, wide in zip(starts, WIDTHS)
    ]

    order = place ^ jnp.arange(4, dtype=jnp.int32)
    hot = order[:, None] == jnp.arange(4, dtype=jnp.int32)[None, :]
    slots_local = jnp.sum(jnp.where(hot[:, :, None], slots.reshape(1, 4, rows), 0), axis=1)
    lists_local = jnp.sum(jnp.where(hot[:, :, None], lists[None, :, :], 0), axis=1)
    positions = jnp.arange(lists.shape[1], dtype=jnp.int32)
    ids = jnp.sum(
        jnp.where(slots_local[:, :, None] == positions, lists_local[:, None, :], 0), axis=2
    )
    wide_ids = jnp.broadcast_to(ids[:, :, None], (4, rows, 128))
    owned_ids = (ids - place * holding).reshape(4, 1, rows)
    owned = (lists_local >= place * holding) & (lists_local < (place + 1) * holding)
    earlier = positions[None, :] < positions[:, None]
    rank_in_list = jnp.sum(owned[:, None, :] & earlier[None], axis=2)
    caps = jnp.arange(CAP, dtype=jnp.int32)
    chosen = jnp.sum(
        jnp.where(
            owned[:, None, :] & (rank_in_list[:, None, :] == caps[None, :, None]),
            (lists_local - place * holding)[:, None, :],
            0,
        ),
        axis=2,
    ).reshape(4 * CAP)
    picks = jnp.concatenate([place.reshape(1), chosen]).astype(jnp.int32)

    parity = (place ^ t) & 1
    per_owner = held // rank
    half_step = per_owner // 2
    owner_first = [holding * (place ^ j) + per_owner * t for j in range(4)]
    info = jnp.stack(
        [parity, place]
        + [owner_first[j] + half_step * h for j in (0, 1) for h in (0, 1)]
        + [owner_first[2] + half_step * y, owner_first[3] + half_step * y]
        + [owner_first[2] + half_step * (1 - y), owner_first[3] + half_step * (1 - y)]
    ).astype(jnp.int32)

    ready = lax.optimization_barrier(
        (hidden, near_b, picks, info, wide_ids, owned_ids, core_block, *blocks)
    )
    own_rows, near_b, picks, info, wide_ids, owned_ids, core_block, *blocks = ready
    core_maps = swap(core_block, "pool", 1)

    (near_lowrank,) = scores(picks, 0, own_rows, [near_b], input_maps, 0, ids=owned_ids)
    near_base = base_product(tie(own_rows, near_lowrank), [near_b], weight)
    crossing = [swap(block, "pool", 2) for block in blocks[: count - 1]]

    a0 = tie(crossed[0], near_base)
    b0 = [swap(a0[:, k * (part // 2) : (k + 1) * (part // 2)], "pool", 1) for k in range(2)]
    (raw,) = scores(picks, 2, a0, b0, input_maps, 0)
    begun = []
    a0 = tie(a0, raw)
    for index in range(EARLY):
        begun.append(
            base_product(a0, b0, weight, 0, None, starts[index], WIDTHS[index])
        )
        a0 = tie(a0, begun[-1])
    a1 = tie(crossed[1], begun[-1])
    b1 = [swap(a1, "pool", 1)]
    total, sent = scores(
        picks, 2, a1, b1, input_maps, 1, prior=raw, near=near_lowrank, ids=owned_ids
    )

    def far_piece(index, after):
        shape = (2, rows, WIDTHS[index])
        left = tie(a1, after)
        if index < EARLY:
            piece = base_product(
                left, b1, weight, 1, begun[index], starts[index], WIDTHS[index], 256
            )
        else:
            piece = whole_product(
                [crossed[0], left], [b0, b1], weight, starts[index], WIDTHS[index], 256
            )
        return piece.reshape(shape)

    hops = (("tensor", 1), ("tensor", 2), ("pool", 1), ("pool", 2))
    arrivals = {0: 0, 2: 1}
    pieces = []
    for index, (axis, step) in enumerate(hops):
        if index > 0:
            sent = total.astype(BF16)
        got = swap(sent, axis, step)
        if index in arrivals:
            chunk = arrivals[index]
            crossing[chunk] = tie(crossing[chunk], sent)
            got = tie(got, crossing[chunk])
        if index == 3:
            crossing.append(swap(tie(blocks[-1], sent), "pool", 2))
            pieces.append(far_piece(0, sent))
            got = tie(got, pieces[-1])
            break
        total = total + got.astype(F32)

    def over_y(index, after):
        block = crossing[index] if after is None else tie(crossing[index], after)
        return block, swap(block, "pool", 1), swap(block, "groups", 1)

    def blocks_of(index, after):
        block, beside, across = moved[index]
        across = across if after is None else tie(across, after)
        return [(block, 0), (beside, 1), (across, 0), (swap(across, "pool", 1), 1)]

    moved = [over_y(index, None) for index in range(count - 1)]

    near_base = near_base.reshape(2, rows, width)
    side = ((place ^ t) >> 1) & 1
    parts = []
    spread = send = None
    halves = []

    def finish(index, after):
        keep, got = halves[index]
        got = got if after is None else tie(got, after)
        pair = keep + got.astype(F32)
        sent = jnp.where(side == 0, pair[1], pair[0]).astype(BF16)
        kept = jnp.where(side == 0, pair[0], pair[1])
        return kept + swap(sent, "tensor", 2).astype(F32)

    for chunk in range(count):
        common = (
            info, near_base, pieces[chunk], output_maps, core_maps,
            blocks_of(chunk, send if chunk else None), starts[chunk],
        )
        if chunk == 0:
            keep, send, spread = combine(*common, build=(total, got, wide_ids))
            moved.append(over_y(count - 1, send))
        else:
            keep, send = combine(*common, spread=spread)
        if chunk + 1 < count:
            pieces.append(far_piece(chunk + 1, send))
        halves.append((keep, swap(send, "tensor", 1)))
        if chunk > 0:
            parts.append(finish(chunk - 1, send))
    parts.append(finish(count - 1, None))
    return jnp.concatenate(parts, axis=1).astype(BF16)


def per_device_general(hidden, weight, input_maps, output_maps, slots, lists):
    rows, depth = hidden.shape
    pool_count = lax.axis_size("pool")
    tensor_count = lax.axis_size("tensor")
    place = lax.axis_index("pool")
    t = lax.axis_index("tensor")
    holding, rank = input_maps.shape[:2]
    held = output_maps.shape[0]
    total_rows = rows * pool_count
    slot_ids = jnp.arange(lists.shape[1], dtype=jnp.int32)
    slot_hot = slots.reshape(pool_count, rows)[:, :, None] == slot_ids
    ids = jnp.sum(jnp.where(slot_hot, lists[:, None, :], 0), axis=2).reshape(total_rows)
    gathered = lax.all_gather(hidden, "pool", axis=0, tiled=True)
    scored = lax.dot_general(
        gathered,
        input_maps.reshape(holding * rank, depth),
        (((1,), (1,)), ((), ())),
        preferred_element_type=F32,
    ).reshape(total_rows, holding, rank)
    owned = place * holding + jnp.arange(holding, dtype=jnp.int32)
    partial = jnp.sum(
        jnp.where((ids[:, None] == owned[None, :])[:, :, None], scored, 0.0), axis=1
    )
    lowrank = lax.psum(partial, ("tensor", "pool")).astype(BF16)
    maps = lax.all_to_all(output_maps, "pool", split_axis=1, concat_axis=0, tiled=True)
    columns = jnp.arange(pool_count * held, dtype=jnp.int32)
    source = (columns // held * tensor_count + t) * held + columns % held
    pick = (source[None, :] % rank == jnp.arange(rank, dtype=jnp.int32)[:, None]).astype(BF16)
    placed = jnp.dot(lowrank, pick, preferred_element_type=F32).astype(BF16)
    spread = jnp.where(ids[:, None] == source[None, :] // rank, placed, jnp.zeros_like(placed))
    value = jnp.dot(gathered, weight, preferred_element_type=F32)
    value = value + jnp.dot(spread, maps, preferred_element_type=F32)
    mixed = lax.psum_scatter(value, "tensor", scatter_dimension=0, tiled=True)
    return mixed.astype(BF16)


def solution(mesh):
    shape = dict(mesh.shape)
    fast = shape["groups"] == 2 and shape["pool"] == 4 and shape["tensor"] == 4
    placed = (
        P(("groups", "pool"), "tensor"),
        P("tensor", "pool"),
        P("pool", None, "tensor"),
        P(("pool", "tensor"), None),
        P("groups"),
        P("groups", None),
    )
    return jax.shard_map(
        per_device_fast if fast else per_device_general,
        mesh=mesh,
        in_specs=placed,
        out_specs=P(("groups", "tensor"), "pool"),
        check_vma=False,
    )
```

```python
import jax
import jax.numpy as jnp
from jax import lax
from jax.experimental import pallas as pl
from jax.experimental.pallas import tpu as pltpu
from jax.sharding import PartitionSpec as P

F32 = jnp.float32
BF16 = jnp.bfloat16
VMEM_LIMIT = 40 * 1024 * 1024
WIDTHS = (512, 512, 512, 512)
EARLY = 3
CAP = 4
HALVES = 2
HINT = 1000


def partners(count, step):
    return [(i, i ^ step) for i in range(count)]


def swap(values, axis, step):
    return lax.ppermute(values, axis, partners(lax.axis_size(axis), step))


def tie(values, *after):
    return lax.optimization_barrier((values, *after))[0]


def cost(flops, moved):
    return pl.CostEstimate(flops=flops // HINT, bytes_accessed=moved // HINT, transcendentals=0)


def params():
    return pltpu.CompilerParams(vmem_limit_bytes=VMEM_LIMIT)


def cut_kernel(ref, *refs):
    outs, sems = refs[:-1], refs[-1]
    copies, start = [], 0
    for index, out in enumerate(outs):
        wide = out.shape[1]
        copies.append(
            pltpu.make_async_copy(ref.at[:, pl.ds(start, wide)], out, sems.at[index])
        )
        start += wide
    for copy in copies:
        copy.start()
    for copy in copies:
        copy.wait()


def cut_columns(array, widths):
    return pl.pallas_call(
        cut_kernel,
        in_specs=[pl.BlockSpec(memory_space=pl.ANY)],
        out_specs=[pl.BlockSpec(memory_space=pl.ANY)] * len(widths),
        out_shape=[jax.ShapeDtypeStruct((array.shape[0], w), array.dtype) for w in widths],
        scratch_shapes=[pltpu.SemaphoreType.DMA((len(widths),))],
        compiler_params=params(),
        cost_estimate=cost(0, 4 * array.size),
        name="cut",
    )(array)


def product_kernel(lower, upper, has_prior, *refs):
    pieces, refs = refs[: lower + upper], refs[lower + upper :]
    if has_prior:
        prior_ref, refs = refs[0], refs[1:]
    w_ref, out_ref, rows = refs

    @pl.when(pl.program_id(0) == 0)
    def _():
        half = rows.shape[0] // 2
        for top, group in ((0, pieces[:lower]), (half, pieces[lower:])):
            start = 0
            for piece in group:
                rows[top : top + half, start : start + piece.shape[1]] = piece[...]
                start += piece.shape[1]

    value = jnp.dot(rows[...], w_ref[...], preferred_element_type=F32)
    if has_prior:
        value += prior_ref[...]
    out_ref[...] = value


def product(lower, upper, weight, depth_block, prior, first, width, tile):
    rows = lower[0].shape[0]
    depth = sum(x.shape[1] for x in lower)
    args = [*lower, *upper]
    in_specs = [pl.BlockSpec(x.shape, lambda n: (0, 0)) for x in args]
    if prior is not None:
        in_specs.append(pl.BlockSpec((2 * rows, tile), lambda n: (0, n)))
        args.append(prior)
    in_specs.append(pl.BlockSpec((depth, tile), lambda n: (depth_block, first // tile + n)))
    args.append(weight)
    return pl.pallas_call(
        lambda *refs: product_kernel(len(lower), len(upper), prior is not None, *refs),
        grid=(width // tile,),
        in_specs=in_specs,
        out_specs=pl.BlockSpec((2 * rows, tile), lambda n: (0, n)),
        out_shape=jax.ShapeDtypeStruct((2 * rows, width), F32),
        scratch_shapes=[pltpu.VMEM((2 * rows, depth), BF16)],
        compiler_params=params(),
        cost_estimate=cost(
            4 * rows * depth * width, 2 * depth * (width + 2 * rows) + 8 * rows * width
        ),
        name="base",
    )(*args)


def scores_kernel(first, offset, count, has_prior, last, info_ref, *refs):
    groups, maps_ref, refs = (refs[:count], refs[count : 2 * count]), refs[2 * count], refs[2 * count + 1 :]
    if has_prior:
        prior_ref, refs = refs[0], refs[1:]
    if first == 2 and last:
        near_ref, refs = refs[0], refs[1:]
    if last:
        ids_ref, refs = refs[0], refs[1:]
    outs, (rows, maps, row_sems, map_sems) = refs[:-4], refs[-4:]
    depth = rows.shape[2]
    cut = depth // 2

    def map_copy(pair, k, part):
        chosen = info_ref[1 + (first + pair) * CAP + k]
        return pltpu.make_async_copy(
            maps_ref.at[chosen, :, pl.ds(offset + part * cut, cut)],
            maps.at[pair * CAP + k, :, pl.ds(part * cut, cut)],
            map_sems.at[pair, k, part],
        )

    row_copies = []
    for pair, pieces in enumerate(groups):
        start = 0
        for index, piece in enumerate(pieces):
            row_copies.append(
                pltpu.make_async_copy(
                    piece,
                    rows.at[pair, :, pl.ds(start, piece.shape[1])],
                    row_sems.at[pair * count + index],
                )
            )
            start += piece.shape[1]
    for pair in range(2):
        for copy in row_copies[pair * count : (pair + 1) * count]:
            copy.start()
        for part in range(2):
            for k in range(CAP):
                map_copy(pair, k, part).start()
    for pair in range(2):
        for copy in row_copies[pair * count : (pair + 1) * count]:
            copy.wait()
        total = prior_ref[pair] if has_prior else None
        for part in range(2):
            for k in range(CAP):
                map_copy(pair, k, part).wait()
            columns = slice(part * cut, (part + 1) * cut)
            chosen = maps[pair * CAP : (pair + 1) * CAP, :, columns]
            term = lax.dot_general(
                chosen.reshape(-1, cut),
                rows[pair, :, columns],
                (((1,), (1,)), ((), ())),
                preferred_element_type=F32,
            )
            total = term if total is None else total + term
        if not last:
            outs[0][pair] = total
            continue
        wanted = ids_ref[pair]
        rank = total.shape[0] // CAP
        found = jnp.zeros((rank, total.shape[1]), F32)
        for k in range(CAP):
            mine = info_ref[1 + (first + pair) * CAP + k]
            found += jnp.where(wanted == mine, total[k * rank : (k + 1) * rank], 0.0)
        if first == 0:
            outs[0][pair] = found
        else:
            near_group = info_ref[0] ^ pair
            far_group = near_group ^ 2
            outs[0][far_group] = found
            outs[1][far_group] = found.astype(BF16)
            outs[0][near_group] = near_ref[pair]
            outs[1][near_group] = near_ref[pair].astype(BF16)


def scores(info, first, lower, upper, maps, half, prior=None, near=None, ids=None):
    rows, depth = lower[0].shape[0], sum(x.shape[1] for x in lower)
    rank = maps.shape[1]
    has_prior, last = prior is not None, ids is not None
    args_rows = [*lower, *upper]
    whole = lambda x: pl.BlockSpec(x.shape, lambda k, s: (0,) * x.ndim)
    args = [*lower, *upper, maps]
    in_specs = [pl.BlockSpec(memory_space=pl.ANY)] * len(args)
    if has_prior:
        in_specs.append(whole(prior))
        args.append(prior)
    if near is not None:
        in_specs.append(whole(near))
        args.append(near)
    if last:
        in_specs.append(
            pl.BlockSpec((2,) + ids.shape[1:], lambda k, s: (first // 2, 0, 0))
        )
        args.append(ids)
    if not last:
        out_shape = [jax.ShapeDtypeStruct((2, CAP * rank, rows), F32)]
    elif first == 0:
        out_shape = [jax.ShapeDtypeStruct((2, rank, rows), F32)]
    else:
        out_shape = [jax.ShapeDtypeStruct((4, rank, rows), kind) for kind in (F32, BF16)]
    return pl.pallas_call(
        lambda *refs: scores_kernel(first, half * depth, len(lower), has_prior, last, *refs),
        grid_spec=pltpu.PrefetchScalarGridSpec(
            num_scalar_prefetch=1,
            grid=(1,),
            in_specs=in_specs,
            out_specs=[whole(x) for x in out_shape],
            scratch_shapes=[
                pltpu.VMEM((2, rows, depth), BF16),
                pltpu.VMEM((2 * CAP, rank, depth), BF16),
                pltpu.SemaphoreType.DMA((len(args_rows),)),
                pltpu.SemaphoreType.DMA((2, CAP, 2)),
            ],
        ),
        out_shape=out_shape,
        compiler_params=params(),
        cost_estimate=cost(4 * rows * depth * CAP * rank, 4 * depth * (CAP * rank + rows)),
        name="scores",
    )(info, *args)


def build_spread(info_ref, lowrank_ref, got_ref, ids_ref, spread):
    rows, lanes = ids_ref.shape[1], ids_ref.shape[2]
    parity, place = info_ref[0], info_ref[1]
    upper = (lax.broadcasted_iota(jnp.int32, (rows, lanes), 1) >= lanes // 2).astype(jnp.int32)
    for slot in range(4):
        local = ((slot // 2) ^ parity) + 2 * (slot % 2)
        group = place ^ local
        values = lowrank_ref[group] + got_ref[group].astype(F32)
        values = jnp.concatenate([values, values], axis=0).T
        wanted = ids_ref[local] - upper
        for piece in range(8):
            spread[slot * rows : (slot + 1) * rows, piece * lanes : (piece + 1) * lanes] = (
                jnp.where(wanted == info_ref[2 + piece], values, 0.0).astype(BF16)
            )


def combine_kernel(build, info_ref, *refs):
    if build:
        lowrank_ref, got_ref, ids_ref, refs = refs[0], refs[1], refs[2], refs[3:]
        near_ref, far_ref, own_ref, core_ref, *blocks, keep_ref, send_ref, spread_ref, maps = refs

        @pl.when(pl.program_id(0) == 0)
        def _():
            build_spread(info_ref, lowrank_ref, got_ref, ids_ref, spread_ref)

    else:
        spread_ref, near_ref, far_ref, own_ref, core_ref, *blocks, keep_ref, send_ref, maps = refs
    parity = info_ref[0]
    rows = near_ref.shape[1]
    held = own_ref.shape[0]
    maps[0:held, :] = own_ref[...]
    maps[held : 2 * held, :] = core_ref[...]
    start = 2 * held
    for ref in blocks:
        maps[start : start + held // 2, :] = ref[0]
        start += held // 2
    delta = jnp.dot(spread_ref[...], maps[...], preferred_element_type=F32)
    for slot in range(4):
        source = near_ref if slot % 2 == 0 else far_ref
        value = source[(slot // 2) ^ parity] + delta[slot * rows : (slot + 1) * rows]
        if slot < 2:
            keep_ref[slot % 2] = value
        else:
            send_ref[slot % 2] = value.astype(BF16)


def combine(info, near, far, own_maps, core_maps, blocks, start, spread=None, build=()):
    rows = near.shape[1]
    width = far.shape[2]
    tile = 512
    first = start // tile
    per_place = core_maps.shape[1] // tile
    held = own_maps.shape[0]
    whole = lambda shape: pl.BlockSpec(shape, lambda n, s: (0,) * len(shape))
    ahead = list(build) if build else [spread]
    spread_shape = (4 * rows, 4 * held)
    in_specs = [whole(x.shape) for x in ahead]
    in_specs += [
        pl.BlockSpec((2, rows, tile), lambda n, s: (0, 0, first + n)),
        pl.BlockSpec((2, rows, tile), lambda n, s: (0, 0, n)),
        pl.BlockSpec((held, tile), lambda n, s: (0, s[1] * per_place + first + n)),
        pl.BlockSpec((held, tile), lambda n, s: (0, first + n)),
    ]
    in_specs += [
        pl.BlockSpec((1, held // 2, tile), lambda n, s, index=index: (index, 0, n))
        for _, index in blocks
    ]
    out_specs = [pl.BlockSpec((2, rows, tile), lambda n, s: (0, 0, n))] * 2
    out_shape = [jax.ShapeDtypeStruct((2, rows, width), kind) for kind in (F32, BF16)]
    if build:
        out_specs.append(whole(spread_shape))
        out_shape.append(jax.ShapeDtypeStruct(spread_shape, BF16))
    return pl.pallas_call(
        lambda *refs: combine_kernel(bool(build), *refs),
        grid_spec=pltpu.PrefetchScalarGridSpec(
            num_scalar_prefetch=1,
            grid=(width // tile,),
            in_specs=in_specs,
            out_specs=out_specs,
            scratch_shapes=[pltpu.VMEM((4 * held, tile), BF16)],
        ),
        out_shape=out_shape,
        compiler_params=params(),
        cost_estimate=cost(
            32 * rows * held * width, 26 * rows * width + 8 * held * width
        ),
        name="combine",
    )(info, *ahead, near, far, own_maps, core_maps, *[block for block, _ in blocks])


def per_device_fast(hidden, weight, input_maps, output_maps, slots, lists):
    rows, depth = hidden.shape
    place = lax.axis_index("pool")
    t = lax.axis_index("tensor")
    y = lax.axis_index("groups")
    holding, rank = input_maps.shape[:2]
    held, features = output_maps.shape
    width = features // 4
    chip, core = place >> 1, place & 1
    starts = [sum(WIDTHS[:i]) for i in range(len(WIDTHS))]
    count = len(WIDTHS)

    part = depth // HALVES
    near_b = swap(hidden, "pool", 1)
    first_a, first_b, second = (
        swap(block, "pool", 2) for block in cut_columns(hidden, (part // 2, part // 2, part))
    )

    core_block = lax.dynamic_slice(output_maps, (0, (place ^ 1) * width), (held, width))
    blocks = [
        jnp.stack(
            [
                lax.dynamic_slice(
                    output_maps,
                    (y * (held // 2), (place ^ other) * width + start),
                    (held // 2, wide),
                )
                for other in (2, 3)
            ]
        )
        for start, wide in zip(starts, WIDTHS)
    ]

    order = place ^ jnp.arange(4, dtype=jnp.int32)
    hot = order[:, None] == jnp.arange(4, dtype=jnp.int32)[None, :]
    slots_local = jnp.sum(jnp.where(hot[:, :, None], slots.reshape(1, 4, rows), 0), axis=1)
    lists_local = jnp.sum(jnp.where(hot[:, :, None], lists[None, :, :], 0), axis=1)
    positions = jnp.arange(lists.shape[1], dtype=jnp.int32)
    ids = jnp.sum(
        jnp.where(slots_local[:, :, None] == positions, lists_local[:, None, :], 0), axis=2
    )
    wide_ids = jnp.broadcast_to(ids[:, :, None], (4, rows, 128))
    owned_ids = (ids - place * holding).reshape(4, 1, rows)
    owned = (lists_local >= place * holding) & (lists_local < (place + 1) * holding)
    earlier = positions[None, :] < positions[:, None]
    rank_in_list = jnp.sum(owned[:, None, :] & earlier[None], axis=2)
    caps = jnp.arange(CAP, dtype=jnp.int32)
    chosen = jnp.sum(
        jnp.where(
            owned[:, None, :] & (rank_in_list[:, None, :] == caps[None, :, None]),
            (lists_local - place * holding)[:, None, :],
            0,
        ),
        axis=2,
    ).reshape(4 * CAP)
    picks = jnp.concatenate([place.reshape(1), chosen]).astype(jnp.int32)

    parity = (place ^ t) & 1
    per_owner = held // rank
    half_step = per_owner // 2
    owner_first = [holding * (place ^ j) + per_owner * t for j in range(4)]
    info = jnp.stack(
        [parity, place]
        + [owner_first[j] + half_step * h for j in (0, 1) for h in (0, 1)]
        + [owner_first[2] + half_step * y, owner_first[3] + half_step * y]
        + [owner_first[2] + half_step * (1 - y), owner_first[3] + half_step * (1 - y)]
    ).astype(jnp.int32)

    ready = lax.optimization_barrier(
        (hidden, near_b, picks, info, wide_ids, owned_ids, core_block, *blocks)
    )
    own_rows, near_b, picks, info, wide_ids, owned_ids, core_block, *blocks = ready
    core_maps = swap(core_block, "pool", 1)

    (near_lowrank,) = scores(picks, 0, [own_rows], [near_b], input_maps, 0, ids=owned_ids)
    near_base = product(
        [tie(own_rows, near_lowrank)], [near_b], weight, 0, None, 0, width, 512
    )
    crossing = [swap(blocks[0], "pool", 2)]

    first_a, first_b = lax.optimization_barrier((first_a, first_b, near_base))[:2]
    a0 = [first_a, first_b]
    b0 = [swap(x, "pool", 1) for x in a0]
    (raw,) = scores(picks, 2, a0, b0, input_maps, 0)
    begun = []
    after = raw
    for index in range(EARLY):
        begun.append(
            product(
                [tie(first_a, after), first_b], b0, weight, 0, None, starts[index], WIDTHS[index], 512
            )
        )
        after = begun[-1]
    a1 = [tie(second, after)]
    b1 = [swap(a1[0], "pool", 1)]
    total, sent = scores(
        picks, 2, a1, b1, input_maps, 1, prior=raw, near=near_lowrank, ids=owned_ids
    )

    def far_piece(index, after):
        left = [tie(a1[0], after)]
        if index < EARLY:
            piece = product(
                left, b1, weight, 1, begun[index], starts[index], WIDTHS[index], 256
            )
        else:
            piece = product(
                a0 + left, b0 + b1, weight, 0, None, starts[index], WIDTHS[index], 256
            )
        return piece.reshape(2, rows, WIDTHS[index])

    got = [swap(sent, "pool", step) for step in (2, 3, 1)]
    crossing.append(swap(tie(blocks[1], sent), "pool", 2))
    crossing[0] = tie(crossing[0], sent)
    got[0] = tie(got[0], crossing[0])
    total = total + sum(x.astype(F32) for x in got)
    sent = total.astype(BF16)
    got = swap(sent, "tensor", 1)
    crossing.append(swap(tie(blocks[2], sent), "pool", 2))
    crossing[1] = tie(crossing[1], sent)
    got = tie(got, crossing[1])
    total = total + got.astype(F32)
    sent = total.astype(BF16)
    got = swap(sent, "tensor", 2)
    crossing.append(swap(tie(blocks[3], sent), "pool", 2))
    crossing[2] = tie(crossing[2], sent)
    pieces = [far_piece(0, sent)]
    got = lax.optimization_barrier((got, crossing[2], pieces[0]))[0]

    def over_y(index, after):
        block = crossing[index] if after is None else tie(crossing[index], after)
        return block, swap(block, "pool", 1), swap(block, "groups", 1)

    def blocks_of(index, after):
        block, beside, across = moved[index]
        across = across if after is None else tie(across, after)
        return [(block, 0), (beside, 1), (across, 0), (swap(across, "pool", 1), 1)]

    moved = [over_y(index, None) for index in range(count - 1)]

    near_base = near_base.reshape(2, rows, width)
    side = ((place ^ t) >> 1) & 1
    parts = []
    spread = send = None
    halves = []

    def finish(index, after):
        keep, got = halves[index]
        got = got if after is None else tie(got, after)
        pair = keep + got.astype(F32)
        sent = jnp.where(side == 0, pair[1], pair[0]).astype(BF16)
        kept = jnp.where(side == 0, pair[0], pair[1])
        return kept + swap(sent, "tensor", 2).astype(F32)

    for chunk in range(count):
        common = (
            info, near_base, pieces[chunk], output_maps, core_maps,
            blocks_of(chunk, send if chunk else None), starts[chunk],
        )
        if chunk == 0:
            keep, send, spread = combine(*common, build=(total, got, wide_ids))
            moved.append(over_y(count - 1, send))
        else:
            keep, send = combine(*common, spread=spread)
        if chunk + 1 < count:
            pieces.append(far_piece(chunk + 1, send))
        halves.append((keep, swap(send, "tensor", 1)))
        if chunk > 0:
            parts.append(finish(chunk - 1, send))
    parts.append(finish(count - 1, None))
    return jnp.concatenate(parts, axis=1).astype(BF16)


def per_device_general(hidden, weight, input_maps, output_maps, slots, lists):
    rows, depth = hidden.shape
    pool_count = lax.axis_size("pool")
    tensor_count = lax.axis_size("tensor")
    place = lax.axis_index("pool")
    t = lax.axis_index("tensor")
    holding, rank = input_maps.shape[:2]
    held = output_maps.shape[0]
    total_rows = rows * pool_count
    slot_ids = jnp.arange(lists.shape[1], dtype=jnp.int32)
    slot_hot = slots.reshape(pool_count, rows)[:, :, None] == slot_ids
    ids = jnp.sum(jnp.where(slot_hot, lists[:, None, :], 0), axis=2).reshape(total_rows)
    gathered = lax.all_gather(hidden, "pool", axis=0, tiled=True)
    scored = lax.dot_general(
        gathered,
        input_maps.reshape(holding * rank, depth),
        (((1,), (1,)), ((), ())),
        preferred_element_type=F32,
    ).reshape(total_rows, holding, rank)
    owned = place * holding + jnp.arange(holding, dtype=jnp.int32)
    partial = jnp.sum(
        jnp.where((ids[:, None] == owned[None, :])[:, :, None], scored, 0.0), axis=1
    )
    lowrank = lax.psum(partial, ("tensor", "pool")).astype(BF16)
    maps = lax.all_to_all(output_maps, "pool", split_axis=1, concat_axis=0, tiled=True)
    columns = jnp.arange(pool_count * held, dtype=jnp.int32)
    source = (columns // held * tensor_count + t) * held + columns % held
    pick = (source[None, :] % rank == jnp.arange(rank, dtype=jnp.int32)[:, None]).astype(BF16)
    placed = jnp.dot(lowrank, pick, preferred_element_type=F32).astype(BF16)
    spread = jnp.where(ids[:, None] == source[None, :] // rank, placed, jnp.zeros_like(placed))
    value = jnp.dot(gathered, weight, preferred_element_type=F32)
    value = value + jnp.dot(spread, maps, preferred_element_type=F32)
    mixed = lax.psum_scatter(value, "tensor", scatter_dimension=0, tiled=True)
    return mixed.astype(BF16)


def solution(mesh):
    shape = dict(mesh.shape)
    fast = shape["groups"] == 2 and shape["pool"] == 4 and shape["tensor"] == 4
    placed = (
        P(("groups", "pool"), "tensor"),
        P("tensor", "pool"),
        P("pool", None, "tensor"),
        P(("pool", "tensor"), None),
        P("groups"),
        P("groups", None),
    )
    return jax.shard_map(
        per_device_fast if fast else per_device_general,
        mesh=mesh,
        in_specs=placed,
        out_specs=P(("groups", "tensor"), "pool"),
        check_vma=False,
    )
```

```python
import jax
import jax.numpy as jnp
from jax import lax
from jax.experimental import pallas as pl
from jax.experimental.pallas import tpu as pltpu
from jax.sharding import PartitionSpec as P

F32 = jnp.float32
BF16 = jnp.bfloat16
VMEM_LIMIT = 40 * 1024 * 1024
WIDTHS = (512, 512, 512, 512)
EARLY = 2
CAP = 4
HALVES = 2
HINT = 1000


def partners(count, step):
    return [(i, i ^ step) for i in range(count)]


def swap(values, axis, step):
    return lax.ppermute(values, axis, partners(lax.axis_size(axis), step))


def tie(values, *after):
    return lax.optimization_barrier((values, *after))[0]


def cost(flops, moved, hint=HINT):
    return pl.CostEstimate(flops=flops // hint, bytes_accessed=moved // hint, transcendentals=0)


def params():
    return pltpu.CompilerParams(vmem_limit_bytes=VMEM_LIMIT)


def cut_kernel(ref, *refs):
    outs, sems = refs[:-1], refs[-1]
    copies, start = [], 0
    for index, out in enumerate(outs):
        wide = out.shape[1]
        copies.append(
            pltpu.make_async_copy(ref.at[:, pl.ds(start, wide)], out, sems.at[index])
        )
        start += wide
    for copy in copies:
        copy.start()
    for copy in copies:
        copy.wait()


def cut_columns(array, widths):
    return pl.pallas_call(
        cut_kernel,
        in_specs=[pl.BlockSpec(memory_space=pl.ANY)],
        out_specs=[pl.BlockSpec(memory_space=pl.ANY)] * len(widths),
        out_shape=[jax.ShapeDtypeStruct((array.shape[0], w), array.dtype) for w in widths],
        scratch_shapes=[pltpu.SemaphoreType.DMA((len(widths),))],
        compiler_params=params(),
        cost_estimate=cost(0, 4 * array.size),
        name="cut",
    )(array)


def product_kernel(lower, upper, has_prior, *refs):
    pieces, refs = refs[: lower + upper], refs[lower + upper :]
    if has_prior:
        prior_ref, refs = refs[0], refs[1:]
    w_ref, out_ref, rows = refs

    @pl.when(pl.program_id(0) == 0)
    def _():
        half = rows.shape[0] // 2
        for top, group in ((0, pieces[:lower]), (half, pieces[lower:])):
            start = 0
            for piece in group:
                rows[top : top + half, start : start + piece.shape[1]] = piece[...]
                start += piece.shape[1]

    value = jnp.dot(rows[...], w_ref[...], preferred_element_type=F32)
    if has_prior:
        value += prior_ref[...]
    out_ref[...] = value


def product(lower, upper, weight, depth_block, prior, first, width, tile, hint=HINT):
    rows = lower[0].shape[0]
    depth = sum(x.shape[1] for x in lower)
    args = [*lower, *upper]
    in_specs = [pl.BlockSpec(x.shape, lambda n: (0, 0)) for x in args]
    if prior is not None:
        in_specs.append(pl.BlockSpec((2 * rows, tile), lambda n: (0, n)))
        args.append(prior)
    in_specs.append(pl.BlockSpec((depth, tile), lambda n: (depth_block, first // tile + n)))
    args.append(weight)
    return pl.pallas_call(
        lambda *refs: product_kernel(len(lower), len(upper), prior is not None, *refs),
        grid=(width // tile,),
        in_specs=in_specs,
        out_specs=pl.BlockSpec((2 * rows, tile), lambda n: (0, n)),
        out_shape=jax.ShapeDtypeStruct((2 * rows, width), F32),
        scratch_shapes=[pltpu.VMEM((2 * rows, depth), BF16)],
        compiler_params=params(),
        cost_estimate=cost(
            4 * rows * depth * width, 2 * depth * (width + 2 * rows) + 8 * rows * width, hint
        ),
        name="base",
    )(*args)


def scores_kernel(first, offset, count, has_prior, last, info_ref, *refs):
    groups, maps_ref, refs = (refs[:count], refs[count : 2 * count]), refs[2 * count], refs[2 * count + 1 :]
    if has_prior:
        prior_ref, refs = refs[0], refs[1:]
    if first == 2 and last:
        near_ref, refs = refs[0], refs[1:]
    if last:
        ids_ref, refs = refs[0], refs[1:]
    outs, (rows, maps, row_sems, map_sems) = refs[:-4], refs[-4:]
    depth = rows.shape[2]
    cut = depth // 2

    def map_copy(pair, k, part):
        chosen = info_ref[1 + (first + pair) * CAP + k]
        return pltpu.make_async_copy(
            maps_ref.at[chosen, :, pl.ds(offset + part * cut, cut)],
            maps.at[pair * CAP + k, :, pl.ds(part * cut, cut)],
            map_sems.at[pair, k, part],
        )

    row_copies = []
    for pair, pieces in enumerate(groups):
        start = 0
        for index, piece in enumerate(pieces):
            row_copies.append(
                pltpu.make_async_copy(
                    piece,
                    rows.at[pair, :, pl.ds(start, piece.shape[1])],
                    row_sems.at[pair * count + index],
                )
            )
            start += piece.shape[1]
    for pair in range(2):
        for copy in row_copies[pair * count : (pair + 1) * count]:
            copy.start()
        for part in range(2):
            for k in range(CAP):
                map_copy(pair, k, part).start()
    for pair in range(2):
        for copy in row_copies[pair * count : (pair + 1) * count]:
            copy.wait()
        total = prior_ref[pair] if has_prior else None
        for part in range(2):
            for k in range(CAP):
                map_copy(pair, k, part).wait()
            columns = slice(part * cut, (part + 1) * cut)
            chosen = maps[pair * CAP : (pair + 1) * CAP, :, columns]
            term = lax.dot_general(
                chosen.reshape(-1, cut),
                rows[pair, :, columns],
                (((1,), (1,)), ((), ())),
                preferred_element_type=F32,
            )
            total = term if total is None else total + term
        if not last:
            outs[0][pair] = total
            continue
        wanted = ids_ref[pair]
        rank = total.shape[0] // CAP
        found = jnp.zeros((rank, total.shape[1]), F32)
        for k in range(CAP):
            mine = info_ref[1 + (first + pair) * CAP + k]
            found += jnp.where(wanted == mine, total[k * rank : (k + 1) * rank], 0.0)
        if first == 0:
            outs[0][pair] = found
        else:
            near_group = info_ref[0] ^ pair
            far_group = near_group ^ 2
            outs[0][far_group] = found
            outs[1][far_group] = found.astype(BF16)
            outs[0][near_group] = near_ref[pair]
            outs[1][near_group] = near_ref[pair].astype(BF16)


def scores(info, first, lower, upper, maps, half, prior=None, near=None, ids=None):
    rows, depth = lower[0].shape[0], sum(x.shape[1] for x in lower)
    rank = maps.shape[1]
    has_prior, last = prior is not None, ids is not None
    args_rows = [*lower, *upper]
    whole = lambda x: pl.BlockSpec(x.shape, lambda k, s: (0,) * x.ndim)
    args = [*lower, *upper, maps]
    in_specs = [pl.BlockSpec(memory_space=pl.ANY)] * len(args)
    if has_prior:
        in_specs.append(whole(prior))
        args.append(prior)
    if near is not None:
        in_specs.append(whole(near))
        args.append(near)
    if last:
        in_specs.append(
            pl.BlockSpec((2,) + ids.shape[1:], lambda k, s: (first // 2, 0, 0))
        )
        args.append(ids)
    if not last:
        out_shape = [jax.ShapeDtypeStruct((2, CAP * rank, rows), F32)]
    elif first == 0:
        out_shape = [jax.ShapeDtypeStruct((2, rank, rows), F32)]
    else:
        out_shape = [jax.ShapeDtypeStruct((4, rank, rows), kind) for kind in (F32, BF16)]
    return pl.pallas_call(
        lambda *refs: scores_kernel(first, half * depth, len(lower), has_prior, last, *refs),
        grid_spec=pltpu.PrefetchScalarGridSpec(
            num_scalar_prefetch=1,
            grid=(1,),
            in_specs=in_specs,
            out_specs=[whole(x) for x in out_shape],
            scratch_shapes=[
                pltpu.VMEM((2, rows, depth), BF16),
                pltpu.VMEM((2 * CAP, rank, depth), BF16),
                pltpu.SemaphoreType.DMA((len(args_rows),)),
                pltpu.SemaphoreType.DMA((2, CAP, 2)),
            ],
        ),
        out_shape=out_shape,
        compiler_params=params(),
        cost_estimate=cost(4 * rows * depth * CAP * rank, 4 * depth * (CAP * rank + rows)),
        name="scores",
    )(info, *args)


def build_spread(info_ref, lowrank_ref, got_ref, ids_ref, spread):
    rows, lanes = ids_ref.shape[1], ids_ref.shape[2]
    parity, place = info_ref[0], info_ref[1]
    upper = (lax.broadcasted_iota(jnp.int32, (rows, lanes), 1) >= lanes // 2).astype(jnp.int32)
    for slot in range(4):
        local = ((slot // 2) ^ parity) + 2 * (slot % 2)
        group = place ^ local
        values = lowrank_ref[group] + got_ref[group].astype(F32)
        values = jnp.concatenate([values, values], axis=0).T
        wanted = ids_ref[local] - upper
        for piece in range(8):
            spread[slot * rows : (slot + 1) * rows, piece * lanes : (piece + 1) * lanes] = (
                jnp.where(wanted == info_ref[2 + piece], values, 0.0).astype(BF16)
            )


def combine_kernel(build, info_ref, *refs):
    if build:
        lowrank_ref, got_ref, ids_ref, refs = refs[0], refs[1], refs[2], refs[3:]
        near_ref, far_ref, own_ref, core_ref, *blocks, keep_ref, send_ref, spread_ref, maps = refs

        @pl.when(pl.program_id(0) == 0)
        def _():
            build_spread(info_ref, lowrank_ref, got_ref, ids_ref, spread_ref)

    else:
        spread_ref, near_ref, far_ref, own_ref, core_ref, *blocks, keep_ref, send_ref, maps = refs
    parity = info_ref[0]
    rows = near_ref.shape[1]
    held = own_ref.shape[0]
    for index, ref in enumerate((own_ref, core_ref, *blocks)):
        maps[index * held : (index + 1) * held, :] = ref[...]
    delta = jnp.dot(spread_ref[...], maps[...], preferred_element_type=F32)
    for slot in range(4):
        source = near_ref if slot % 2 == 0 else far_ref
        value = source[(slot // 2) ^ parity] + delta[slot * rows : (slot + 1) * rows]
        if slot < 2:
            keep_ref[slot % 2] = value
        else:
            send_ref[slot % 2] = value.astype(BF16)


def combine(info, near, far, own_maps, core_maps, blocks, start, spread=None, build=()):
    rows = near.shape[1]
    width = far.shape[2]
    tile = 512
    first = start // tile
    per_place = core_maps.shape[1] // tile
    held = own_maps.shape[0]
    whole = lambda shape: pl.BlockSpec(shape, lambda n, s: (0,) * len(shape))
    ahead = list(build) if build else [spread]
    spread_shape = (4 * rows, 4 * held)
    in_specs = [whole(x.shape) for x in ahead]
    in_specs += [
        pl.BlockSpec((2, rows, tile), lambda n, s: (0, 0, first + n)),
        pl.BlockSpec((2, rows, tile), lambda n, s: (0, 0, n)),
        pl.BlockSpec((held, tile), lambda n, s: (0, s[1] * per_place + first + n)),
        pl.BlockSpec((held, tile), lambda n, s: (0, first + n)),
    ]
    in_specs += [
        pl.BlockSpec((held, tile), lambda n, s: (0, n)) for _ in blocks
    ]
    out_specs = [pl.BlockSpec((2, rows, tile), lambda n, s: (0, 0, n))] * 2
    out_shape = [jax.ShapeDtypeStruct((2, rows, width), kind) for kind in (F32, BF16)]
    if build:
        out_specs.append(whole(spread_shape))
        out_shape.append(jax.ShapeDtypeStruct(spread_shape, BF16))
    return pl.pallas_call(
        lambda *refs: combine_kernel(bool(build), *refs),
        grid_spec=pltpu.PrefetchScalarGridSpec(
            num_scalar_prefetch=1,
            grid=(width // tile,),
            in_specs=in_specs,
            out_specs=out_specs,
            scratch_shapes=[pltpu.VMEM((4 * held, tile), BF16)],
        ),
        out_shape=out_shape,
        compiler_params=params(),
        cost_estimate=cost(
            32 * rows * held * width, 26 * rows * width + 8 * held * width
        ),
        name="combine",
    )(info, *ahead, near, far, own_maps, core_maps, *blocks)


def per_device_fast(hidden, weight, input_maps, output_maps, slots, lists):
    rows, depth = hidden.shape
    place = lax.axis_index("pool")
    t = lax.axis_index("tensor")
    holding, rank = input_maps.shape[:2]
    held, features = output_maps.shape
    width = features // 4
    starts = [sum(WIDTHS[:i]) for i in range(len(WIDTHS))]
    count = len(WIDTHS)

    part = depth // HALVES
    near_b = swap(hidden, "pool", 1)
    first_a, first_b, second = (
        swap(block, "pool", 2) for block in cut_columns(hidden, (part // 2, part // 2, part))
    )

    core_block = lax.dynamic_slice(output_maps, (0, (place ^ 1) * width), (held, width))
    blocks = [
        lax.dynamic_slice(output_maps, (0, (place ^ other) * width + start), (held, wide))
        for start, wide in zip(starts, WIDTHS)
        for other in (2, 3)
    ]

    order = place ^ jnp.arange(4, dtype=jnp.int32)
    hot = order[:, None] == jnp.arange(4, dtype=jnp.int32)[None, :]
    slots_local = jnp.sum(jnp.where(hot[:, :, None], slots.reshape(1, 4, rows), 0), axis=1)
    lists_local = jnp.sum(jnp.where(hot[:, :, None], lists[None, :, :], 0), axis=1)
    positions = jnp.arange(lists.shape[1], dtype=jnp.int32)
    ids = jnp.sum(
        jnp.where(slots_local[:, :, None] == positions, lists_local[:, None, :], 0), axis=2
    )
    wide_ids = jnp.broadcast_to(ids[:, :, None], (4, rows, 128))
    owned_ids = (ids - place * holding).reshape(4, 1, rows)
    owned = (lists_local >= place * holding) & (lists_local < (place + 1) * holding)
    earlier = positions[None, :] < positions[:, None]
    rank_in_list = jnp.sum(owned[:, None, :] & earlier[None], axis=2)
    caps = jnp.arange(CAP, dtype=jnp.int32)
    chosen = jnp.sum(
        jnp.where(
            owned[:, None, :] & (rank_in_list[:, None, :] == caps[None, :, None]),
            (lists_local - place * holding)[:, None, :],
            0,
        ),
        axis=2,
    ).reshape(4 * CAP)
    picks = jnp.concatenate([place.reshape(1), chosen]).astype(jnp.int32)

    parity = (place ^ t) & 1
    per_owner = held // rank
    half_step = per_owner // 2
    owner_first = [holding * (place ^ j) + per_owner * t for j in range(4)]
    info = jnp.stack(
        [parity, place]
        + [owner_first[j] + half_step * h for j in range(4) for h in range(2)]
    ).astype(jnp.int32)

    ready = lax.optimization_barrier(
        (hidden, near_b, picks, info, wide_ids, owned_ids, core_block, *blocks)
    )
    own_rows, near_b, picks, info, wide_ids, owned_ids, core_block, *blocks = ready
    core_maps = swap(core_block, "pool", 1)

    (near_lowrank,) = scores(picks, 0, [own_rows], [near_b], input_maps, 0, ids=owned_ids)
    near_base = product(
        [tie(own_rows, near_lowrank)], [near_b], weight, 0, None, 0, width, 512
    )

    first_a, first_b = lax.optimization_barrier((first_a, first_b, near_base))[:2]
    a0 = [first_a, first_b]
    b0 = [swap(x, "pool", 1) for x in a0]
    (raw,) = scores(picks, 2, a0, b0, input_maps, 0)
    begun = []
    after = raw
    for index in range(EARLY):
        begun.append(
            product(
                [tie(first_a, after), first_b], b0, weight, 0, None, starts[index], WIDTHS[index], 512
            )
        )
        after = begun[-1]
    a1 = [tie(second, after)]
    b1 = [swap(a1[0], "pool", 1)]
    total, sent = scores(
        picks, 2, a1, b1, input_maps, 1, prior=raw, near=near_lowrank, ids=owned_ids
    )

    def far_piece(index, after, hint=HINT):
        left = [tie(a1[0], after)]
        if index < EARLY:
            piece = product(
                left, b1, weight, 1, begun[index], starts[index], WIDTHS[index], 256, hint
            )
        else:
            piece = product(
                a0 + left, b0 + b1, weight, 0, None, starts[index], WIDTHS[index], 256, hint
            )
        return piece.reshape(2, rows, WIDTHS[index])

    got = [swap(sent, "pool", step) for step in (2, 3, 1)]
    total = total + sum(x.astype(F32) for x in got)

    def start_maps(index, after):
        pair = [tie(x, after) for x in blocks[2 * index : 2 * index + 2]]
        return [swap(x, "pool", 2 + k) for k, x in enumerate(pair)]

    moved = [start_maps(0, sent)]
    sent = total.astype(BF16)
    got = swap(sent, "tensor", 1)
    moved.append(start_maps(1, sent))
    pieces = [far_piece(0, sent, 1)]
    moved[0] = [tie(x, pieces[0]) for x in moved[0]]
    got = lax.optimization_barrier((got, pieces[0]))[0]
    total = total + got.astype(F32)
    sent = total.astype(BF16)
    got = swap(sent, "tensor", 2)
    moved.append(start_maps(2, sent))
    moved[0] = [tie(x, sent) for x in moved[0]]
    got = lax.optimization_barrier((got, *moved[0]))[0]

    near_base = near_base.reshape(2, rows, width)
    side = ((place ^ t) >> 1) & 1
    parts = []
    spread = send = None

    def maps_of(index, after):
        return moved[index] if after is None else [tie(x, after) for x in moved[index]]

    def pace(index):
        return near_base if index < 2 else tie(near_base, started[index - 2])

    started = []

    halves = []

    def finish(index, after):
        keep, got = halves[index]
        got = got if after is None else tie(got, after)
        pair = keep + got.astype(F32)
        sent = jnp.where(side == 0, pair[1], pair[0]).astype(BF16)
        kept = jnp.where(side == 0, pair[0], pair[1])
        started.append(sent)
        return kept + swap(sent, "tensor", 2).astype(F32)

    for chunk in range(count):
        common = (
            info, pace(chunk), pieces[chunk], output_maps, core_maps,
            maps_of(chunk, started[chunk - 2] if chunk > 1 else send), starts[chunk],
        )
        if chunk == 0:
            keep, send, spread = combine(*common, build=(total, got, wide_ids))
            moved.append(start_maps(3, send))
        else:
            keep, send = combine(*common, spread=spread)
        if chunk + 1 < count:
            pieces.append(far_piece(chunk + 1, send))
        halves.append((keep, swap(send, "tensor", 1)))
        if chunk > 0:
            parts.append(finish(chunk - 1, send))
    parts.append(finish(count - 1, started[-1]))
    return jnp.concatenate(parts, axis=1).astype(BF16)


def per_device_general(hidden, weight, input_maps, output_maps, slots, lists):
    rows, depth = hidden.shape
    pool_count = lax.axis_size("pool")
    tensor_count = lax.axis_size("tensor")
    place = lax.axis_index("pool")
    t = lax.axis_index("tensor")
    holding, rank = input_maps.shape[:2]
    held = output_maps.shape[0]
    total_rows = rows * pool_count
    slot_ids = jnp.arange(lists.shape[1], dtype=jnp.int32)
    slot_hot = slots.reshape(pool_count, rows)[:, :, None] == slot_ids
    ids = jnp.sum(jnp.where(slot_hot, lists[:, None, :], 0), axis=2).reshape(total_rows)
    gathered = lax.all_gather(hidden, "pool", axis=0, tiled=True)
    scored = lax.dot_general(
        gathered,
        input_maps.reshape(holding * rank, depth),
        (((1,), (1,)), ((), ())),
        preferred_element_type=F32,
    ).reshape(total_rows, holding, rank)
    owned = place * holding + jnp.arange(holding, dtype=jnp.int32)
    partial = jnp.sum(
        jnp.where((ids[:, None] == owned[None, :])[:, :, None], scored, 0.0), axis=1
    )
    lowrank = lax.psum(partial, ("tensor", "pool")).astype(BF16)
    maps = lax.all_to_all(output_maps, "pool", split_axis=1, concat_axis=0, tiled=True)
    columns = jnp.arange(pool_count * held, dtype=jnp.int32)
    source = (columns // held * tensor_count + t) * held + columns % held
    pick = (source[None, :] % rank == jnp.arange(rank, dtype=jnp.int32)[:, None]).astype(BF16)
    placed = jnp.dot(lowrank, pick, preferred_element_type=F32).astype(BF16)
    spread = jnp.where(ids[:, None] == source[None, :] // rank, placed, jnp.zeros_like(placed))
    value = jnp.dot(gathered, weight, preferred_element_type=F32)
    value = value + jnp.dot(spread, maps, preferred_element_type=F32)
    mixed = lax.psum_scatter(value, "tensor", scatter_dimension=0, tiled=True)
    return mixed.astype(BF16)


def solution(mesh):
    shape = dict(mesh.shape)
    fast = shape["groups"] == 2 and shape["pool"] == 4 and shape["tensor"] == 4
    placed = (
        P(("groups", "pool"), "tensor"),
        P("tensor", "pool"),
        P("pool", None, "tensor"),
        P(("pool", "tensor"), None),
        P("groups"),
        P("groups", None),
    )
    return jax.shard_map(
        per_device_fast if fast else per_device_general,
        mesh=mesh,
        in_specs=placed,
        out_specs=P(("groups", "tensor"), "pool"),
        check_vma=False,
    )
```

```python
import jax
import jax.numpy as jnp
from jax import lax
from jax.experimental import pallas as pl
from jax.experimental.pallas import tpu as pltpu
from jax.sharding import PartitionSpec as P

F32 = jnp.float32
BF16 = jnp.bfloat16
VMEM_LIMIT = 60 * 1024 * 1024
WIDTHS = (512, 512, 512, 512)
CAP = 4
HALVES = 2
HINT = 1000


def partners(count, step):
    return [(i, i ^ step) for i in range(count)]


def swap(values, axis, step):
    return lax.ppermute(values, axis, partners(lax.axis_size(axis), step))


def tie(values, *after):
    return lax.optimization_barrier((values, *after))[0]


def cost(flops, moved, hint=HINT):
    return pl.CostEstimate(flops=flops // hint, bytes_accessed=moved // hint, transcendentals=0)


def params():
    return pltpu.CompilerParams(vmem_limit_bytes=VMEM_LIMIT)


def cut_kernel(ref, *refs):
    outs, sems = refs[:-1], refs[-1]
    copies, start = [], 0
    for index, out in enumerate(outs):
        wide = out.shape[1]
        copies.append(
            pltpu.make_async_copy(ref.at[:, pl.ds(start, wide)], out, sems.at[index])
        )
        start += wide
    for copy in copies:
        copy.start()
    for copy in copies:
        copy.wait()


def cut_columns(array, widths):
    return pl.pallas_call(
        cut_kernel,
        in_specs=[pl.BlockSpec(memory_space=pl.ANY)],
        out_specs=[pl.BlockSpec(memory_space=pl.ANY)] * len(widths),
        out_shape=[jax.ShapeDtypeStruct((array.shape[0], w), array.dtype) for w in widths],
        scratch_shapes=[pltpu.SemaphoreType.DMA((len(widths),))],
        compiler_params=params(),
        cost_estimate=cost(0, 4 * array.size),
        name="cut",
    )(array)


def product_kernel(counts, has_prior, *refs):
    pieces, refs = refs[: sum(counts)], refs[sum(counts) :]
    if has_prior:
        prior_ref, refs = refs[0], refs[1:]
    w_ref, out_ref, rows = refs

    @pl.when(pl.program_id(0) == 0)
    def _():
        height = rows.shape[0] // len(counts)
        spot = 0
        for group, count in enumerate(counts):
            start = 0
            for piece in pieces[spot : spot + count]:
                wide = piece.shape[1]
                rows[group * height : (group + 1) * height, start : start + wide] = piece[...]
                start += wide
            spot += count

    value = jnp.dot(rows[...], w_ref[...], preferred_element_type=F32)
    if has_prior:
        top = prior_ref.shape[0]
        out_ref[:top, :] = value[:top] + prior_ref[...]
        if top < value.shape[0]:
            out_ref[top:, :] = value[top:]
    else:
        out_ref[...] = value


def product(groups, weight, depth_block, first, width, tile, prior=None, prior_block=0, hint=HINT):
    rows = groups[0][0][0].shape[0]
    depth = sum(wide for _, wide, _ in groups[0])
    total = rows * len(groups)
    in_specs, args = [], []
    for group in groups:
        for array, wide, block in group:
            in_specs.append(pl.BlockSpec((rows, wide), lambda n, block=block: (0, block)))
            args.append(array)
    if prior is not None:
        in_specs.append(
            pl.BlockSpec((2 * rows, tile), lambda n: (prior_block, first // tile + n))
        )
        args.append(prior)
    in_specs.append(pl.BlockSpec((depth, tile), lambda n: (depth_block, first // tile + n)))
    args.append(weight)
    counts = [len(group) for group in groups]
    return pl.pallas_call(
        lambda *refs: product_kernel(counts, prior is not None, *refs),
        grid=(width // tile,),
        in_specs=in_specs,
        out_specs=pl.BlockSpec((total, tile), lambda n: (0, n)),
        out_shape=jax.ShapeDtypeStruct((total, width), F32),
        scratch_shapes=[pltpu.VMEM((total, depth), BF16)],
        compiler_params=params(),
        cost_estimate=cost(
            2 * total * depth * width, 2 * depth * (width + total) + 8 * total * width, hint
        ),
        name="base",
    )(*args)


def scores_kernel(first, offset, count, has_prior, last, info_ref, *refs):
    groups, maps_ref, refs = (refs[:count], refs[count : 2 * count]), refs[2 * count], refs[2 * count + 1 :]
    if has_prior:
        prior_ref, refs = refs[0], refs[1:]
    if first == 2 and last:
        near_ref, refs = refs[0], refs[1:]
    if last:
        ids_ref, refs = refs[0], refs[1:]
    outs, (rows, maps, row_sems, map_sems) = refs[:-4], refs[-4:]
    depth = rows.shape[2]
    cut = depth // 2

    def map_copy(pair, k, part):
        chosen = info_ref[1 + (first + pair) * CAP + k]
        return pltpu.make_async_copy(
            maps_ref.at[chosen, :, pl.ds(offset + part * cut, cut)],
            maps.at[pair * CAP + k, :, pl.ds(part * cut, cut)],
            map_sems.at[pair, k, part],
        )

    row_copies = []
    for pair, pieces in enumerate(groups):
        start = 0
        for index, piece in enumerate(pieces):
            row_copies.append(
                pltpu.make_async_copy(
                    piece,
                    rows.at[pair, :, pl.ds(start, piece.shape[1])],
                    row_sems.at[pair * count + index],
                )
            )
            start += piece.shape[1]
    for pair in range(2):
        for copy in row_copies[pair * count : (pair + 1) * count]:
            copy.start()
        for part in range(2):
            for k in range(CAP):
                map_copy(pair, k, part).start()
    for pair in range(2):
        for copy in row_copies[pair * count : (pair + 1) * count]:
            copy.wait()
        total = prior_ref[pair] if has_prior else None
        for part in range(2):
            for k in range(CAP):
                map_copy(pair, k, part).wait()
            columns = slice(part * cut, (part + 1) * cut)
            chosen = maps[pair * CAP : (pair + 1) * CAP, :, columns]
            term = lax.dot_general(
                chosen.reshape(-1, cut),
                rows[pair, :, columns],
                (((1,), (1,)), ((), ())),
                preferred_element_type=F32,
            )
            total = term if total is None else total + term
        if not last:
            outs[0][pair] = total
            continue
        wanted = ids_ref[pair]
        rank = total.shape[0] // CAP
        found = jnp.zeros((rank, total.shape[1]), F32)
        for k in range(CAP):
            mine = info_ref[1 + (first + pair) * CAP + k]
            found += jnp.where(wanted == mine, total[k * rank : (k + 1) * rank], 0.0)
        if first == 0:
            outs[0][pair] = found
        else:
            near_group = info_ref[0] ^ pair
            far_group = near_group ^ 2
            outs[0][far_group] = found
            outs[1][far_group] = found.astype(BF16)
            outs[0][near_group] = near_ref[pair]
            outs[1][near_group] = near_ref[pair].astype(BF16)


def scores(info, first, lower, upper, maps, half, prior=None, near=None, ids=None):
    rows, depth = lower[0].shape[0], sum(x.shape[1] for x in lower)
    rank = maps.shape[1]
    has_prior, last = prior is not None, ids is not None
    args_rows = [*lower, *upper]
    whole = lambda x: pl.BlockSpec(x.shape, lambda k, s: (0,) * x.ndim)
    args = [*lower, *upper, maps]
    in_specs = [pl.BlockSpec(memory_space=pl.ANY)] * len(args)
    if has_prior:
        in_specs.append(whole(prior))
        args.append(prior)
    if near is not None:
        in_specs.append(whole(near))
        args.append(near)
    if last:
        in_specs.append(
            pl.BlockSpec((2,) + ids.shape[1:], lambda k, s: (first // 2, 0, 0))
        )
        args.append(ids)
    if not last:
        out_shape = [jax.ShapeDtypeStruct((2, CAP * rank, rows), F32)]
    elif first == 0:
        out_shape = [jax.ShapeDtypeStruct((2, rank, rows), F32)]
    else:
        out_shape = [jax.ShapeDtypeStruct((4, rank, rows), kind) for kind in (F32, BF16)]
    return pl.pallas_call(
        lambda *refs: scores_kernel(first, half * depth, len(lower), has_prior, last, *refs),
        grid_spec=pltpu.PrefetchScalarGridSpec(
            num_scalar_prefetch=1,
            grid=(1,),
            in_specs=in_specs,
            out_specs=[whole(x) for x in out_shape],
            scratch_shapes=[
                pltpu.VMEM((2, rows, depth), BF16),
                pltpu.VMEM((2 * CAP, rank, depth), BF16),
                pltpu.SemaphoreType.DMA((len(args_rows),)),
                pltpu.SemaphoreType.DMA((2, CAP, 2)),
            ],
        ),
        out_shape=out_shape,
        compiler_params=params(),
        cost_estimate=cost(4 * rows * depth * CAP * rank, 4 * depth * (CAP * rank + rows)),
        name="scores",
    )(info, *args)


def build_spread(info_ref, lowrank_ref, got_ref, ids_ref, spread):
    rows, lanes = ids_ref.shape[1], ids_ref.shape[2]
    parity, place = info_ref[0], info_ref[1]
    upper = (lax.broadcasted_iota(jnp.int32, (rows, lanes), 1) >= lanes // 2).astype(jnp.int32)
    for slot in range(4):
        local = ((slot // 2) ^ parity) + 2 * (slot % 2)
        group = place ^ local
        values = lowrank_ref[group] + got_ref[group].astype(F32)
        values = jnp.concatenate([values, values], axis=0).T
        wanted = ids_ref[local] - upper
        for piece in range(8):
            spread[slot * rows : (slot + 1) * rows, piece * lanes : (piece + 1) * lanes] = (
                jnp.where(wanted == info_ref[2 + piece], values, 0.0).astype(BF16)
            )


def combine_kernel(build, info_ref, *refs):
    if build:
        lowrank_ref, got_ref, ids_ref, refs = refs[0], refs[1], refs[2], refs[3:]
        near_ref, far_ref, own_ref, core_ref, *blocks, keep_ref, send_ref, spread_ref, maps = refs

        @pl.when(pl.program_id(0) == 0)
        def _():
            build_spread(info_ref, lowrank_ref, got_ref, ids_ref, spread_ref)

    else:
        spread_ref, near_ref, far_ref, own_ref, core_ref, *blocks, keep_ref, send_ref, maps = refs
    parity = info_ref[0]
    rows = near_ref.shape[1]
    held = own_ref.shape[0]
    for index, ref in enumerate((own_ref, core_ref, *blocks)):
        maps[index * held : (index + 1) * held, :] = ref[...]
    delta = jnp.dot(spread_ref[...], maps[...], preferred_element_type=F32)
    for slot in range(4):
        source = near_ref if slot % 2 == 0 else far_ref
        value = source[(slot // 2) ^ parity] + delta[slot * rows : (slot + 1) * rows]
        if slot < 2:
            keep_ref[slot % 2] = value
        else:
            send_ref[slot % 2] = value.astype(BF16)


def combine(info, near, far, own_maps, core_maps, blocks, start, spread=None, build=()):
    rows = near.shape[1]
    width = far.shape[2]
    tile = 512
    first = start // tile
    per_place = core_maps.shape[1] // tile
    held = own_maps.shape[0]
    whole = lambda shape: pl.BlockSpec(shape, lambda n, s: (0,) * len(shape))
    ahead = list(build) if build else [spread]
    spread_shape = (4 * rows, 4 * held)
    in_specs = [whole(x.shape) for x in ahead]
    in_specs += [
        pl.BlockSpec((2, rows, tile), lambda n, s: (0, 0, first + n)),
        pl.BlockSpec((2, rows, tile), lambda n, s: (0, 0, n)),
        pl.BlockSpec((held, tile), lambda n, s: (0, s[1] * per_place + first + n)),
        pl.BlockSpec((held, tile), lambda n, s: (0, first + n)),
    ]
    in_specs += [
        pl.BlockSpec((held, tile), lambda n, s: (0, n)) for _ in blocks
    ]
    out_specs = [pl.BlockSpec((2, rows, tile), lambda n, s: (0, 0, n))] * 2
    out_shape = [jax.ShapeDtypeStruct((2, rows, width), kind) for kind in (F32, BF16)]
    if build:
        out_specs.append(whole(spread_shape))
        out_shape.append(jax.ShapeDtypeStruct(spread_shape, BF16))
    return pl.pallas_call(
        lambda *refs: combine_kernel(bool(build), *refs),
        grid_spec=pltpu.PrefetchScalarGridSpec(
            num_scalar_prefetch=1,
            grid=(width // tile,),
            in_specs=in_specs,
            out_specs=out_specs,
            scratch_shapes=[pltpu.VMEM((4 * held, tile), BF16)],
        ),
        out_shape=out_shape,
        compiler_params=params(),
        cost_estimate=cost(
            32 * rows * held * width, 26 * rows * width + 8 * held * width
        ),
        name="combine",
    )(info, *ahead, near, far, own_maps, core_maps, *blocks)


def per_device_fast(hidden, weight, input_maps, output_maps, slots, lists):
    rows, depth = hidden.shape
    place = lax.axis_index("pool")
    t = lax.axis_index("tensor")
    holding, rank = input_maps.shape[:2]
    held, features = output_maps.shape
    width = features // 4
    starts = [sum(WIDTHS[:i]) for i in range(len(WIDTHS))]
    count = len(WIDTHS)

    part = depth // HALVES
    near_b = swap(hidden, "pool", 1)
    first_a, first_b, second = (
        swap(block, "pool", 2) for block in cut_columns(hidden, (part // 2, part // 2, part))
    )

    core_block = lax.dynamic_slice(output_maps, (0, (place ^ 1) * width), (held, width))
    blocks = [
        lax.dynamic_slice(output_maps, (0, (place ^ other) * width + start), (held, wide))
        for start, wide in zip(starts, WIDTHS)
        for other in (2, 3)
    ]

    order = place ^ jnp.arange(4, dtype=jnp.int32)
    hot = order[:, None] == jnp.arange(4, dtype=jnp.int32)[None, :]
    slots_local = jnp.sum(jnp.where(hot[:, :, None], slots.reshape(1, 4, rows), 0), axis=1)
    lists_local = jnp.sum(jnp.where(hot[:, :, None], lists[None, :, :], 0), axis=1)
    positions = jnp.arange(lists.shape[1], dtype=jnp.int32)
    ids = jnp.sum(
        jnp.where(slots_local[:, :, None] == positions, lists_local[:, None, :], 0), axis=2
    )
    wide_ids = jnp.broadcast_to(ids[:, :, None], (4, rows, 128))
    owned_ids = (ids - place * holding).reshape(4, 1, rows)
    owned = (lists_local >= place * holding) & (lists_local < (place + 1) * holding)
    earlier = positions[None, :] < positions[:, None]
    rank_in_list = jnp.sum(owned[:, None, :] & earlier[None], axis=2)
    caps = jnp.arange(CAP, dtype=jnp.int32)
    chosen = jnp.sum(
        jnp.where(
            owned[:, None, :] & (rank_in_list[:, None, :] == caps[None, :, None]),
            (lists_local - place * holding)[:, None, :],
            0,
        ),
        axis=2,
    ).reshape(4 * CAP)
    picks = jnp.concatenate([place.reshape(1), chosen]).astype(jnp.int32)

    parity = (place ^ t) & 1
    per_owner = held // rank
    half_step = per_owner // 2
    owner_first = [holding * (place ^ j) + per_owner * t for j in range(4)]
    info = jnp.stack(
        [parity, place]
        + [owner_first[j] + half_step * h for j in range(4) for h in range(2)]
    ).astype(jnp.int32)

    ready = lax.optimization_barrier(
        (hidden, near_b, picks, info, wide_ids, owned_ids, core_block, *blocks)
    )
    own_rows, near_b, picks, info, wide_ids, owned_ids, core_block, *blocks = ready
    core_maps = swap(core_block, "pool", 1)

    (near_lowrank,) = scores(picks, 0, [own_rows], [near_b], input_maps, 0, ids=owned_ids)
    near_late = product(
        [[(tie(own_rows, near_lowrank), part, 1)], [(near_b, part, 1)]],
        weight, 1, 0, width, 512,
    )

    first_a, first_b = lax.optimization_barrier((first_a, first_b, near_late))[:2]
    a0 = [first_a, first_b]
    b0 = [swap(x, "pool", 1) for x in a0]
    (raw,) = scores(picks, 2, a0, b0, input_maps, 0)
    base = product(
        [
            [(tie(own_rows, raw), part, 0)],
            [(near_b, part, 0)],
            [(x, part // 2, 0) for x in a0],
            [(x, part // 2, 0) for x in b0],
        ],
        weight, 0, 0, width, 512, near_late,
    )
    a1 = tie(second, base)
    b1 = swap(a1, "pool", 1)
    total, sent = scores(
        picks, 2, [a1], [b1], input_maps, 1, prior=raw, near=near_lowrank, ids=owned_ids
    )

    def far_piece(index, after, hint=HINT):
        return product(
            [[(tie(a1, after), part, 0)], [(b1, part, 0)]],
            weight, 1, starts[index], WIDTHS[index], 256, base, 1, hint,
        ).reshape(2, rows, WIDTHS[index])

    got = [swap(sent, "pool", step) for step in (2, 3, 1)]
    pieces = [far_piece(0, sent, 1)]

    def start_maps(index, after):
        pair = blocks[2 * index : 2 * index + 2]
        return [swap(tie(x, after), "pool", 2 + k) for k, x in enumerate(pair)]

    moved = [[swap(blocks[0], "pool", 2), swap(tie(blocks[1], sent), "pool", 3)]]
    moved[0][0] = tie(moved[0][0], sent)
    got = lax.optimization_barrier((*got, moved[0][0], pieces[0]))[:3]
    total = total + sum(x.astype(F32) for x in got)
    sent = total.astype(BF16)
    got = swap(sent, "tensor", 1)
    moved.append(start_maps(1, sent))
    pieces.append(far_piece(1, sent, 1))
    got = tie(got, pieces[1])
    total = total + got.astype(F32)
    sent = total.astype(BF16)
    got = swap(sent, "tensor", 2)
    moved.append(start_maps(2, sent))
    moved[0][1] = tie(moved[0][1], sent)
    got = lax.optimization_barrier((got, *moved[0]))[0]

    near_base = base.reshape(4, rows, width)
    side = ((place ^ t) >> 1) & 1
    parts = []
    spread = send = None

    def maps_of(index, after):
        return moved[index] if after is None else [tie(x, after) for x in moved[index]]

    def pace(index):
        return near_base if index < 2 else tie(near_base, started[index - 2])

    started = []

    halves = []

    def finish(index, after):
        keep, got = halves[index]
        got = got if after is None else tie(got, after)
        pair = keep + got.astype(F32)
        sent = jnp.where(side == 0, pair[1], pair[0]).astype(BF16)
        kept = jnp.where(side == 0, pair[0], pair[1])
        started.append(sent)
        return kept + swap(sent, "tensor", 2).astype(F32)

    for chunk in range(count):
        common = (
            info, pace(chunk), pieces[chunk], output_maps, core_maps,
            maps_of(chunk, started[chunk - 2] if chunk > 1 else send), starts[chunk],
        )
        if chunk == 0:
            keep, send, spread = combine(*common, build=(total, got, wide_ids))
            moved.append(start_maps(3, send))
        else:
            keep, send = combine(*common, spread=spread)
        if chunk == 0:
            pieces.append(far_piece(2, send))
        halves.append((keep, swap(send, "tensor", 1)))
        if chunk > 0:
            parts.append(finish(chunk - 1, send))
        if chunk == 1:
            pieces.append(far_piece(3, started[0]))
    parts.append(finish(count - 1, started[-1]))
    return jnp.concatenate(parts, axis=1).astype(BF16)


def per_device_general(hidden, weight, input_maps, output_maps, slots, lists):
    rows, depth = hidden.shape
    pool_count = lax.axis_size("pool")
    tensor_count = lax.axis_size("tensor")
    place = lax.axis_index("pool")
    t = lax.axis_index("tensor")
    holding, rank = input_maps.shape[:2]
    held = output_maps.shape[0]
    total_rows = rows * pool_count
    slot_ids = jnp.arange(lists.shape[1], dtype=jnp.int32)
    slot_hot = slots.reshape(pool_count, rows)[:, :, None] == slot_ids
    ids = jnp.sum(jnp.where(slot_hot, lists[:, None, :], 0), axis=2).reshape(total_rows)
    gathered = lax.all_gather(hidden, "pool", axis=0, tiled=True)
    scored = lax.dot_general(
        gathered,
        input_maps.reshape(holding * rank, depth),
        (((1,), (1,)), ((), ())),
        preferred_element_type=F32,
    ).reshape(total_rows, holding, rank)
    owned = place * holding + jnp.arange(holding, dtype=jnp.int32)
    partial = jnp.sum(
        jnp.where((ids[:, None] == owned[None, :])[:, :, None], scored, 0.0), axis=1
    )
    lowrank = lax.psum(partial, ("tensor", "pool")).astype(BF16)
    maps = lax.all_to_all(output_maps, "pool", split_axis=1, concat_axis=0, tiled=True)
    columns = jnp.arange(pool_count * held, dtype=jnp.int32)
    source = (columns // held * tensor_count + t) * held + columns % held
    pick = (source[None, :] % rank == jnp.arange(rank, dtype=jnp.int32)[:, None]).astype(BF16)
    placed = jnp.dot(lowrank, pick, preferred_element_type=F32).astype(BF16)
    spread = jnp.where(ids[:, None] == source[None, :] // rank, placed, jnp.zeros_like(placed))
    value = jnp.dot(gathered, weight, preferred_element_type=F32)
    value = value + jnp.dot(spread, maps, preferred_element_type=F32)
    mixed = lax.psum_scatter(value, "tensor", scatter_dimension=0, tiled=True)
    return mixed.astype(BF16)


def solution(mesh):
    shape = dict(mesh.shape)
    fast = shape["groups"] == 2 and shape["pool"] == 4 and shape["tensor"] == 4
    placed = (
        P(("groups", "pool"), "tensor"),
        P("tensor", "pool"),
        P("pool", None, "tensor"),
        P(("pool", "tensor"), None),
        P("groups"),
        P("groups", None),
    )
    return jax.shard_map(
        per_device_fast if fast else per_device_general,
        mesh=mesh,
        in_specs=placed,
        out_specs=P(("groups", "tensor"), "pool"),
        check_vma=False,
    )
```

```python
import jax
import jax.numpy as jnp
from jax import lax
from jax.experimental import pallas as pl
from jax.experimental.pallas import tpu as pltpu
from jax.sharding import PartitionSpec as P

F32 = jnp.float32
BF16 = jnp.bfloat16
WIDTHS = (512, 512, 512, 512)
CAP = 4
HALVES = 2
HINT = 1000


def partners(count, step):
    return [(i, i ^ step) for i in range(count)]


def swap(values, axis, step):
    return lax.ppermute(values, axis, partners(lax.axis_size(axis), step))


def tie(values, *after):
    return lax.optimization_barrier((values, *after))[0]


def cost(flops, moved, hint=HINT):
    return pl.CostEstimate(flops=flops // hint, bytes_accessed=moved // hint, transcendentals=0)


def params(mebibytes):
    return pltpu.CompilerParams(vmem_limit_bytes=mebibytes * 1024 * 1024)


def cut_kernel(ref, *refs):
    outs, (stage, sems) = refs[:-2], refs[-2:]
    inward, outward, start = [], [], 0
    for index, out in enumerate(outs):
        spot = pl.ds(start, out.shape[1])
        inward.append(
            pltpu.make_async_copy(ref.at[:, spot], stage.at[:, spot], sems.at[0, index])
        )
        outward.append(pltpu.make_async_copy(stage.at[:, spot], out, sems.at[1, index]))
        start += out.shape[1]
    for copy in inward:
        copy.start()
    for copy, after in zip(inward, outward):
        copy.wait()
        after.start()
    for copy in outward:
        copy.wait()


def cut_columns(array, widths):
    return pl.pallas_call(
        cut_kernel,
        in_specs=[pl.BlockSpec(memory_space=pl.ANY)],
        out_specs=[pl.BlockSpec(memory_space=pl.ANY)] * len(widths),
        out_shape=[jax.ShapeDtypeStruct((array.shape[0], w), array.dtype) for w in widths],
        scratch_shapes=[
            pltpu.VMEM(array.shape, array.dtype),
            pltpu.SemaphoreType.DMA((2, len(widths))),
        ],
        compiler_params=params(4),
        cost_estimate=cost(0, 4 * array.size),
        name="cut",
    )(array)


def product_kernel(counts, has_prior, *refs):
    pieces, refs = refs[: sum(counts)], refs[sum(counts) :]
    if has_prior:
        prior_ref, refs = refs[0], refs[1:]
    w_ref, out_ref, rows = refs

    @pl.when(pl.program_id(0) == 0)
    def _():
        height = rows.shape[0] // len(counts)
        spot = 0
        for group, count in enumerate(counts):
            start = 0
            for piece in pieces[spot : spot + count]:
                wide = piece.shape[1]
                rows[group * height : (group + 1) * height, start : start + wide] = piece[...]
                start += wide
            spot += count

    value = jnp.dot(rows[...], w_ref[...], preferred_element_type=F32)
    if has_prior:
        top = prior_ref.shape[0]
        out_ref[:top, :] = value[:top] + prior_ref[...]
        if top < value.shape[0]:
            out_ref[top:, :] = value[top:]
    else:
        out_ref[...] = value


def product(groups, weight, depth_block, first, width, tile, prior=None, prior_block=0, hint=HINT):
    rows = groups[0][0][0].shape[0]
    depth = sum(wide for _, wide, _ in groups[0])
    total = rows * len(groups)
    limit = 28 if len(groups) > 2 else 20 if tile > 256 else 14
    in_specs, args = [], []
    for group in groups:
        for array, wide, block in group:
            in_specs.append(pl.BlockSpec((rows, wide), lambda n, block=block: (0, block)))
            args.append(array)
    if prior is not None:
        in_specs.append(
            pl.BlockSpec((2 * rows, tile), lambda n: (prior_block, first // tile + n))
        )
        args.append(prior)
    in_specs.append(pl.BlockSpec((depth, tile), lambda n: (depth_block, first // tile + n)))
    args.append(weight)
    counts = [len(group) for group in groups]
    return pl.pallas_call(
        lambda *refs: product_kernel(counts, prior is not None, *refs),
        grid=(width // tile,),
        in_specs=in_specs,
        out_specs=pl.BlockSpec((total, tile), lambda n: (0, n)),
        out_shape=jax.ShapeDtypeStruct((total, width), F32),
        scratch_shapes=[pltpu.VMEM((total, depth), BF16)],
        compiler_params=params(limit),
        cost_estimate=cost(
            2 * total * depth * width, 2 * depth * (width + total) + 8 * total * width, hint
        ),
        name="base",
    )(*args)


def scores_kernel(first, offset, count, has_prior, last, info_ref, *refs):
    groups, maps_ref, refs = (refs[:count], refs[count : 2 * count]), refs[2 * count], refs[2 * count + 1 :]
    if has_prior:
        prior_ref, refs = refs[0], refs[1:]
    if first == 2 and last:
        near_ref, refs = refs[0], refs[1:]
    if last:
        ids_ref, refs = refs[0], refs[1:]
    outs, (rows, maps, row_sems, map_sems) = refs[:-4], refs[-4:]
    depth = rows.shape[2]
    cut = depth // 2

    def map_copy(pair, k, part):
        chosen = info_ref[1 + (first + pair) * CAP + k]
        return pltpu.make_async_copy(
            maps_ref.at[chosen, :, pl.ds(offset + part * cut, cut)],
            maps.at[pair * CAP + k, :, pl.ds(part * cut, cut)],
            map_sems.at[pair, k, part],
        )

    row_copies = []
    for pair, pieces in enumerate(groups):
        start = 0
        for index, piece in enumerate(pieces):
            row_copies.append(
                pltpu.make_async_copy(
                    piece,
                    rows.at[pair, :, pl.ds(start, piece.shape[1])],
                    row_sems.at[pair * count + index],
                )
            )
            start += piece.shape[1]
    for pair in range(2):
        for copy in row_copies[pair * count : (pair + 1) * count]:
            copy.start()
        for part in range(2):
            for k in range(CAP):
                map_copy(pair, k, part).start()
    for pair in range(2):
        for copy in row_copies[pair * count : (pair + 1) * count]:
            copy.wait()
        total = prior_ref[pair] if has_prior else None
        for part in range(2):
            for k in range(CAP):
                map_copy(pair, k, part).wait()
            columns = slice(part * cut, (part + 1) * cut)
            chosen = maps[pair * CAP : (pair + 1) * CAP, :, columns]
            term = lax.dot_general(
                chosen.reshape(-1, cut),
                rows[pair, :, columns],
                (((1,), (1,)), ((), ())),
                preferred_element_type=F32,
            )
            total = term if total is None else total + term
        if not last:
            outs[0][pair] = total
            continue
        wanted = ids_ref[pair]
        rank = total.shape[0] // CAP
        found = jnp.zeros((rank, total.shape[1]), F32)
        for k in range(CAP):
            mine = info_ref[1 + (first + pair) * CAP + k]
            found += jnp.where(wanted == mine, total[k * rank : (k + 1) * rank], 0.0)
        if first == 0:
            outs[0][pair] = found
        else:
            near_group = info_ref[0] ^ pair
            far_group = near_group ^ 2
            outs[0][far_group] = found
            outs[1][far_group] = found.astype(BF16)
            outs[0][near_group] = near_ref[pair]
            outs[1][near_group] = near_ref[pair].astype(BF16)


def scores(info, first, lower, upper, maps, half, prior=None, near=None, ids=None):
    rows, depth = lower[0].shape[0], sum(x.shape[1] for x in lower)
    rank = maps.shape[1]
    has_prior, last = prior is not None, ids is not None
    args_rows = [*lower, *upper]
    whole = lambda x: pl.BlockSpec(x.shape, lambda k, s: (0,) * x.ndim)
    args = [*lower, *upper, maps]
    in_specs = [pl.BlockSpec(memory_space=pl.ANY)] * len(args)
    if has_prior:
        in_specs.append(whole(prior))
        args.append(prior)
    if near is not None:
        in_specs.append(whole(near))
        args.append(near)
    if last:
        in_specs.append(
            pl.BlockSpec((2,) + ids.shape[1:], lambda k, s: (first // 2, 0, 0))
        )
        args.append(ids)
    if not last:
        out_shape = [jax.ShapeDtypeStruct((2, CAP * rank, rows), F32)]
    elif first == 0:
        out_shape = [jax.ShapeDtypeStruct((2, rank, rows), F32)]
    else:
        out_shape = [jax.ShapeDtypeStruct((4, rank, rows), kind) for kind in (F32, BF16)]
    return pl.pallas_call(
        lambda *refs: scores_kernel(first, half * depth, len(lower), has_prior, last, *refs),
        grid_spec=pltpu.PrefetchScalarGridSpec(
            num_scalar_prefetch=1,
            grid=(1,),
            in_specs=in_specs,
            out_specs=[whole(x) for x in out_shape],
            scratch_shapes=[
                pltpu.VMEM((2, rows, depth), BF16),
                pltpu.VMEM((2 * CAP, rank, depth), BF16),
                pltpu.SemaphoreType.DMA((len(args_rows),)),
                pltpu.SemaphoreType.DMA((2, CAP, 2)),
            ],
        ),
        out_shape=out_shape,
        compiler_params=params(18 if first == 0 else 12),
        cost_estimate=cost(4 * rows * depth * CAP * rank, 4 * depth * (CAP * rank + rows)),
        name="scores",
    )(info, *args)


def build_spread(info_ref, lowrank_ref, got_ref, ids_ref, spread):
    rows, lanes = ids_ref.shape[1], ids_ref.shape[2]
    parity, place = info_ref[0], info_ref[1]
    upper = (lax.broadcasted_iota(jnp.int32, (rows, lanes), 1) >= lanes // 2).astype(jnp.int32)
    for slot in range(4):
        local = ((slot // 2) ^ parity) + 2 * (slot % 2)
        group = place ^ local
        values = lowrank_ref[group] + got_ref[group].astype(F32)
        values = jnp.concatenate([values, values], axis=0).T
        wanted = ids_ref[local] - upper
        for piece in range(8):
            spread[slot * rows : (slot + 1) * rows, piece * lanes : (piece + 1) * lanes] = (
                jnp.where(wanted == info_ref[2 + piece], values, 0.0).astype(BF16)
            )


def combine_kernel(build, info_ref, *refs):
    if build:
        lowrank_ref, got_ref, ids_ref, refs = refs[0], refs[1], refs[2], refs[3:]
        near_ref, far_ref, own_ref, core_ref, *blocks, keep_ref, send_ref, spread_ref, maps = refs

        @pl.when(pl.program_id(0) == 0)
        def _():
            build_spread(info_ref, lowrank_ref, got_ref, ids_ref, spread_ref)

    else:
        spread_ref, near_ref, far_ref, own_ref, core_ref, *blocks, keep_ref, send_ref, maps = refs
    parity = info_ref[0]
    rows = near_ref.shape[1]
    held = own_ref.shape[0]
    for index, ref in enumerate((own_ref, core_ref, *blocks)):
        maps[index * held : (index + 1) * held, :] = ref[...]
    delta = jnp.dot(spread_ref[...], maps[...], preferred_element_type=F32)
    for slot in range(4):
        source = near_ref if slot % 2 == 0 else far_ref
        value = source[(slot // 2) ^ parity] + delta[slot * rows : (slot + 1) * rows]
        if slot < 2:
            keep_ref[slot % 2] = value
        else:
            send_ref[slot % 2] = value.astype(BF16)


def combine(info, near, far, own_maps, core_maps, blocks, start, spread=None, build=()):
    rows = near.shape[1]
    width = far.shape[2]
    tile = 512
    first = start // tile
    per_place = core_maps.shape[1] // tile
    held = own_maps.shape[0]
    whole = lambda shape: pl.BlockSpec(shape, lambda n, s: (0,) * len(shape))
    ahead = list(build) if build else [spread]
    spread_shape = (4 * rows, 4 * held)
    in_specs = [whole(x.shape) for x in ahead]
    in_specs += [
        pl.BlockSpec((2, rows, tile), lambda n, s: (0, 0, first + n)),
        pl.BlockSpec((2, rows, tile), lambda n, s: (0, 0, n)),
        pl.BlockSpec((held, tile), lambda n, s: (0, s[1] * per_place + first + n)),
        pl.BlockSpec((held, tile), lambda n, s: (0, first + n)),
    ]
    in_specs += [
        pl.BlockSpec((held, tile), lambda n, s: (0, n)) for _ in blocks
    ]
    out_specs = [pl.BlockSpec((2, rows, tile), lambda n, s: (0, 0, n))] * 2
    out_shape = [jax.ShapeDtypeStruct((2, rows, width), kind) for kind in (F32, BF16)]
    if build:
        out_specs.append(whole(spread_shape))
        out_shape.append(jax.ShapeDtypeStruct(spread_shape, BF16))
    return pl.pallas_call(
        lambda *refs: combine_kernel(bool(build), *refs),
        grid_spec=pltpu.PrefetchScalarGridSpec(
            num_scalar_prefetch=1,
            grid=(width // tile,),
            in_specs=in_specs,
            out_specs=out_specs,
            scratch_shapes=[pltpu.VMEM((4 * held, tile), BF16)],
        ),
        out_shape=out_shape,
        compiler_params=params(14),
        cost_estimate=cost(
            32 * rows * held * width, 26 * rows * width + 8 * held * width
        ),
        name="combine",
    )(info, *ahead, near, far, own_maps, core_maps, *blocks)


def per_device_fast(hidden, weight, input_maps, output_maps, slots, lists):
    rows, depth = hidden.shape
    place = lax.axis_index("pool")
    t = lax.axis_index("tensor")
    holding, rank = input_maps.shape[:2]
    held, features = output_maps.shape
    width = features // 4
    starts = [sum(WIDTHS[:i]) for i in range(len(WIDTHS))]
    count = len(WIDTHS)

    part = depth // HALVES
    near_b = swap(hidden, "pool", 1)
    first_a, first_b, second = (
        swap(block, "pool", 2) for block in cut_columns(hidden, (part // 2, part // 2, part))
    )

    core_block = lax.dynamic_slice(output_maps, (0, (place ^ 1) * width), (held, width))
    blocks = [
        lax.dynamic_slice(output_maps, (0, (place ^ other) * width + start), (held, wide))
        for start, wide in zip(starts, WIDTHS)
        for other in (2, 3)
    ]

    order = place ^ jnp.arange(4, dtype=jnp.int32)
    hot = order[:, None] == jnp.arange(4, dtype=jnp.int32)[None, :]
    slots_local = jnp.sum(jnp.where(hot[:, :, None], slots.reshape(1, 4, rows), 0), axis=1)
    lists_local = jnp.sum(jnp.where(hot[:, :, None], lists[None, :, :], 0), axis=1)
    positions = jnp.arange(lists.shape[1], dtype=jnp.int32)
    ids = jnp.sum(
        jnp.where(slots_local[:, :, None] == positions, lists_local[:, None, :], 0), axis=2
    )
    wide_ids = jnp.broadcast_to(ids[:, :, None], (4, rows, 128))
    owned_ids = (ids - place * holding).reshape(4, 1, rows)
    owned = (lists_local >= place * holding) & (lists_local < (place + 1) * holding)
    earlier = positions[None, :] < positions[:, None]
    rank_in_list = jnp.sum(owned[:, None, :] & earlier[None], axis=2)
    caps = jnp.arange(CAP, dtype=jnp.int32)
    chosen = jnp.sum(
        jnp.where(
            owned[:, None, :] & (rank_in_list[:, None, :] == caps[None, :, None]),
            (lists_local - place * holding)[:, None, :],
            0,
        ),
        axis=2,
    ).reshape(4 * CAP)
    picks = jnp.concatenate([place.reshape(1), chosen]).astype(jnp.int32)

    parity = (place ^ t) & 1
    per_owner = held // rank
    half_step = per_owner // 2
    owner_first = [holding * (place ^ j) + per_owner * t for j in range(4)]
    info = jnp.stack(
        [parity, place]
        + [owner_first[j] + half_step * h for j in range(4) for h in range(2)]
    ).astype(jnp.int32)

    ready = lax.optimization_barrier(
        (hidden, near_b, picks, info, wide_ids, owned_ids, core_block, *blocks)
    )
    own_rows, near_b, picks, info, wide_ids, owned_ids, core_block, *blocks = ready
    core_maps = swap(core_block, "pool", 1)

    (near_lowrank,) = scores(picks, 0, [own_rows], [near_b], input_maps, 0, ids=owned_ids)
    near_late = product(
        [[(tie(own_rows, near_lowrank), part, 1)], [(near_b, part, 1)]],
        weight, 1, 0, width, 512,
    )

    first_a, first_b = lax.optimization_barrier((first_a, first_b, near_late))[:2]
    a0 = [first_a, first_b]
    b0 = [swap(x, "pool", 1) for x in a0]
    (raw,) = scores(picks, 2, a0, b0, input_maps, 0)
    base = product(
        [
            [(tie(own_rows, raw), part, 0)],
            [(near_b, part, 0)],
            [(x, part // 2, 0) for x in a0],
            [(x, part // 2, 0) for x in b0],
        ],
        weight, 0, 0, width, 512, near_late,
    )
    a1 = tie(second, base)
    b1 = swap(a1, "pool", 1)
    total, sent = scores(
        picks, 2, [a1], [b1], input_maps, 1, prior=raw, near=near_lowrank, ids=owned_ids
    )

    def far_piece(index, after, hint=HINT):
        return product(
            [[(tie(a1, after), part, 0)], [(b1, part, 0)]],
            weight, 1, starts[index], WIDTHS[index], 256, base, 1, hint,
        ).reshape(2, rows, WIDTHS[index])

    got = [swap(sent, "pool", step) for step in (2, 3, 1)]
    pieces = [far_piece(0, sent, 1)]

    def start_maps(index, after):
        pair = blocks[2 * index : 2 * index + 2]
        return [swap(tie(x, after), "pool", 2 + k) for k, x in enumerate(pair)]

    moved = [[swap(blocks[0], "pool", 2), swap(tie(blocks[1], sent), "pool", 3)]]
    moved[0][0] = tie(moved[0][0], sent)
    got = lax.optimization_barrier((*got, moved[0][0], pieces[0]))[:3]
    total = total + sum(x.astype(F32) for x in got)
    sent = total.astype(BF16)
    got = swap(sent, "tensor", 1)
    moved.append(start_maps(1, sent))
    pieces.append(far_piece(1, sent, 1))
    got = tie(got, pieces[1])
    total = total + got.astype(F32)
    sent = total.astype(BF16)
    got = swap(sent, "tensor", 2)
    moved.append(start_maps(2, sent))
    moved[0][1] = tie(moved[0][1], sent)
    got = lax.optimization_barrier((got, *moved[0]))[0]

    near_base = base.reshape(4, rows, width)
    side = ((place ^ t) >> 1) & 1
    parts = []
    spread = send = None

    def maps_of(index, after):
        return moved[index] if after is None else [tie(x, after) for x in moved[index]]

    def pace(index):
        return near_base if index < 2 else tie(near_base, started[index - 2])

    started = []

    halves = []

    def finish(index, after):
        keep, got = halves[index]
        got = got if after is None else tie(got, after)
        pair = keep + got.astype(F32)
        sent = jnp.where(side == 0, pair[1], pair[0]).astype(BF16)
        kept = jnp.where(side == 0, pair[0], pair[1])
        started.append(sent)
        return kept + swap(sent, "tensor", 2).astype(F32)

    for chunk in range(count):
        common = (
            info, pace(chunk), pieces[chunk], output_maps, core_maps,
            maps_of(chunk, started[chunk - 2] if chunk > 1 else send), starts[chunk],
        )
        if chunk == 0:
            keep, send, spread = combine(*common, build=(total, got, wide_ids))
            moved.append(start_maps(3, send))
        else:
            keep, send = combine(*common, spread=spread)
        if chunk == 0:
            pieces.append(far_piece(2, send))
        halves.append((keep, swap(send, "tensor", 1)))
        if chunk > 0:
            parts.append(finish(chunk - 1, send))
        if chunk == 1:
            pieces.append(far_piece(3, started[0]))
    parts.append(finish(count - 1, started[-1]))
    return jnp.concatenate(parts, axis=1).astype(BF16)


def per_device_general(hidden, weight, input_maps, output_maps, slots, lists):
    rows, depth = hidden.shape
    pool_count = lax.axis_size("pool")
    tensor_count = lax.axis_size("tensor")
    place = lax.axis_index("pool")
    t = lax.axis_index("tensor")
    holding, rank = input_maps.shape[:2]
    held = output_maps.shape[0]
    total_rows = rows * pool_count
    slot_ids = jnp.arange(lists.shape[1], dtype=jnp.int32)
    slot_hot = slots.reshape(pool_count, rows)[:, :, None] == slot_ids
    ids = jnp.sum(jnp.where(slot_hot, lists[:, None, :], 0), axis=2).reshape(total_rows)
    gathered = lax.all_gather(hidden, "pool", axis=0, tiled=True)
    scored = lax.dot_general(
        gathered,
        input_maps.reshape(holding * rank, depth),
        (((1,), (1,)), ((), ())),
        preferred_element_type=F32,
    ).reshape(total_rows, holding, rank)
    owned = place * holding + jnp.arange(holding, dtype=jnp.int32)
    partial = jnp.sum(
        jnp.where((ids[:, None] == owned[None, :])[:, :, None], scored, 0.0), axis=1
    )
    lowrank = lax.psum(partial, ("tensor", "pool")).astype(BF16)
    maps = lax.all_to_all(output_maps, "pool", split_axis=1, concat_axis=0, tiled=True)
    columns = jnp.arange(pool_count * held, dtype=jnp.int32)
    source = (columns // held * tensor_count + t) * held + columns % held
    pick = (source[None, :] % rank == jnp.arange(rank, dtype=jnp.int32)[:, None]).astype(BF16)
    placed = jnp.dot(lowrank, pick, preferred_element_type=F32).astype(BF16)
    spread = jnp.where(ids[:, None] == source[None, :] // rank, placed, jnp.zeros_like(placed))
    value = jnp.dot(gathered, weight, preferred_element_type=F32)
    value = value + jnp.dot(spread, maps, preferred_element_type=F32)
    mixed = lax.psum_scatter(value, "tensor", scatter_dimension=0, tiled=True)
    return mixed.astype(BF16)


def solution(mesh):
    shape = dict(mesh.shape)
    fast = shape["groups"] == 2 and shape["pool"] == 4 and shape["tensor"] == 4
    placed = (
        P(("groups", "pool"), "tensor"),
        P("tensor", "pool"),
        P("pool", None, "tensor"),
        P(("pool", "tensor"), None),
        P("groups"),
        P("groups", None),
    )
    return jax.shard_map(
        per_device_fast if fast else per_device_general,
        mesh=mesh,
        in_specs=placed,
        out_specs=P(("groups", "tensor"), "pool"),
        check_vma=False,
    )
```

```python
import jax
import jax.numpy as jnp
from jax import lax
from jax.experimental import pallas as pl
from jax.experimental.pallas import tpu as pltpu
from jax.sharding import PartitionSpec as P

F32 = jnp.float32
BF16 = jnp.bfloat16
VMEM_LIMIT = 48 * 1024 * 1024
WIDTHS = (512, 512, 512, 512)
CAP = 4
HALVES = 2
HINT = 1000


def partners(count, step):
    return [(i, i ^ step) for i in range(count)]


def swap(values, axis, step):
    return lax.ppermute(values, axis, partners(lax.axis_size(axis), step))


def tie(values, *after):
    return lax.optimization_barrier((values, *after))[0]


def cost(flops, moved, hint=HINT):
    return pl.CostEstimate(flops=flops // hint, bytes_accessed=moved // hint, transcendentals=0)


def params():
    return pltpu.CompilerParams(vmem_limit_bytes=VMEM_LIMIT)


def cut_kernel(ref, *refs):
    outs, (stage, sems) = refs[:-2], refs[-2:]
    inward, outward, start = [], [], 0
    for index, out in enumerate(outs):
        spot = pl.ds(start, out.shape[1])
        inward.append(
            pltpu.make_async_copy(ref.at[:, spot], stage.at[:, spot], sems.at[0, index])
        )
        outward.append(pltpu.make_async_copy(stage.at[:, spot], out, sems.at[1, index]))
        start += out.shape[1]
    for copy in inward:
        copy.start()
    for copy, after in zip(inward, outward):
        copy.wait()
        after.start()
    for copy in outward:
        copy.wait()


def cut_columns(array, widths):
    return pl.pallas_call(
        cut_kernel,
        in_specs=[pl.BlockSpec(memory_space=pl.ANY)],
        out_specs=[pl.BlockSpec(memory_space=pl.ANY)] * len(widths),
        out_shape=[jax.ShapeDtypeStruct((array.shape[0], w), array.dtype) for w in widths],
        scratch_shapes=[
            pltpu.VMEM(array.shape, array.dtype),
            pltpu.SemaphoreType.DMA((2, len(widths))),
        ],
        compiler_params=params(),
        cost_estimate=cost(0, 4 * array.size),
        name="cut",
    )(array)


def product_kernel(counts, has_prior, *refs):
    pieces, refs = refs[: sum(counts)], refs[sum(counts) :]
    if has_prior:
        prior_ref, refs = refs[0], refs[1:]
    w_ref, out_ref, rows = refs

    @pl.when(pl.program_id(0) == 0)
    def _():
        height = rows.shape[0] // len(counts)
        spot = 0
        for group, count in enumerate(counts):
            start = 0
            for piece in pieces[spot : spot + count]:
                wide = piece.shape[1]
                rows[group * height : (group + 1) * height, start : start + wide] = piece[...]
                start += wide
            spot += count

    value = jnp.dot(rows[...], w_ref[...], preferred_element_type=F32)
    if has_prior:
        top = prior_ref.shape[0]
        out_ref[:top, :] = value[:top] + prior_ref[...]
        if top < value.shape[0]:
            out_ref[top:, :] = value[top:]
    else:
        out_ref[...] = value


def product(groups, weight, depth_block, first, width, tile, prior=None, prior_block=0, hint=HINT):
    rows = groups[0][0][0].shape[0]
    depth = sum(wide for _, wide, _ in groups[0])
    total = rows * len(groups)
    in_specs, args = [], []
    for group in groups:
        for array, wide, block in group:
            in_specs.append(pl.BlockSpec((rows, wide), lambda n, block=block: (0, block)))
            args.append(array)
    if prior is not None:
        in_specs.append(
            pl.BlockSpec((2 * rows, tile), lambda n: (prior_block, first // tile + n))
        )
        args.append(prior)
    in_specs.append(pl.BlockSpec((depth, tile), lambda n: (depth_block, first // tile + n)))
    args.append(weight)
    counts = [len(group) for group in groups]
    return pl.pallas_call(
        lambda *refs: product_kernel(counts, prior is not None, *refs),
        grid=(width // tile,),
        in_specs=in_specs,
        out_specs=pl.BlockSpec((total, tile), lambda n: (0, n)),
        out_shape=jax.ShapeDtypeStruct((total, width), F32),
        scratch_shapes=[pltpu.VMEM((total, depth), BF16)],
        compiler_params=params(),
        cost_estimate=cost(
            2 * total * depth * width, 2 * depth * (width + total) + 8 * total * width, hint
        ),
        name="base",
    )(*args)


def scores_kernel(first, offset, count, has_prior, last, info_ref, *refs):
    groups, maps_ref, refs = (refs[:count], refs[count : 2 * count]), refs[2 * count], refs[2 * count + 1 :]
    if has_prior:
        prior_ref, refs = refs[0], refs[1:]
    if first == 2 and last:
        near_ref, refs = refs[0], refs[1:]
    if last:
        ids_ref, refs = refs[0], refs[1:]
    outs, (rows, maps, row_sems, map_sems) = refs[:-4], refs[-4:]
    depth = rows.shape[2]
    cut = depth // 2

    def map_copy(pair, k, part):
        chosen = info_ref[1 + (first + pair) * CAP + k]
        return pltpu.make_async_copy(
            maps_ref.at[chosen, :, pl.ds(offset + part * cut, cut)],
            maps.at[pair * CAP + k, :, pl.ds(part * cut, cut)],
            map_sems.at[pair, k, part],
        )

    row_copies = []
    for pair, pieces in enumerate(groups):
        start = 0
        for index, piece in enumerate(pieces):
            row_copies.append(
                pltpu.make_async_copy(
                    piece,
                    rows.at[pair, :, pl.ds(start, piece.shape[1])],
                    row_sems.at[pair * count + index],
                )
            )
            start += piece.shape[1]
    for pair in range(2):
        for copy in row_copies[pair * count : (pair + 1) * count]:
            copy.start()
        for part in range(2):
            for k in range(CAP):
                map_copy(pair, k, part).start()
    for pair in range(2):
        for copy in row_copies[pair * count : (pair + 1) * count]:
            copy.wait()
        total = prior_ref[pair] if has_prior else None
        for part in range(2):
            for k in range(CAP):
                map_copy(pair, k, part).wait()
            columns = slice(part * cut, (part + 1) * cut)
            chosen = maps[pair * CAP : (pair + 1) * CAP, :, columns]
            term = lax.dot_general(
                chosen.reshape(-1, cut),
                rows[pair, :, columns],
                (((1,), (1,)), ((), ())),
                preferred_element_type=F32,
            )
            total = term if total is None else total + term
        if not last:
            outs[0][pair] = total
            continue
        wanted = ids_ref[pair]
        rank = total.shape[0] // CAP
        found = jnp.zeros((rank, total.shape[1]), F32)
        for k in range(CAP):
            mine = info_ref[1 + (first + pair) * CAP + k]
            found += jnp.where(wanted == mine, total[k * rank : (k + 1) * rank], 0.0)
        if first == 0:
            outs[0][pair] = found
        else:
            near_group = info_ref[0] ^ pair
            far_group = near_group ^ 2
            outs[0][far_group] = found
            outs[1][far_group] = found.astype(BF16)
            outs[0][near_group] = near_ref[pair]
            outs[1][near_group] = near_ref[pair].astype(BF16)


def scores(info, first, lower, upper, maps, half, prior=None, near=None, ids=None):
    rows, depth = lower[0].shape[0], sum(x.shape[1] for x in lower)
    rank = maps.shape[1]
    has_prior, last = prior is not None, ids is not None
    args_rows = [*lower, *upper]
    whole = lambda x: pl.BlockSpec(x.shape, lambda k, s: (0,) * x.ndim)
    args = [*lower, *upper, maps]
    in_specs = [pl.BlockSpec(memory_space=pl.ANY)] * len(args)
    if has_prior:
        in_specs.append(whole(prior))
        args.append(prior)
    if near is not None:
        in_specs.append(whole(near))
        args.append(near)
    if last:
        in_specs.append(
            pl.BlockSpec((2,) + ids.shape[1:], lambda k, s: (first // 2, 0, 0))
        )
        args.append(ids)
    if not last:
        out_shape = [jax.ShapeDtypeStruct((2, CAP * rank, rows), F32)]
    elif first == 0:
        out_shape = [jax.ShapeDtypeStruct((2, rank, rows), F32)]
    else:
        out_shape = [jax.ShapeDtypeStruct((4, rank, rows), kind) for kind in (F32, BF16)]
    return pl.pallas_call(
        lambda *refs: scores_kernel(first, half * depth, len(lower), has_prior, last, *refs),
        grid_spec=pltpu.PrefetchScalarGridSpec(
            num_scalar_prefetch=1,
            grid=(1,),
            in_specs=in_specs,
            out_specs=[whole(x) for x in out_shape],
            scratch_shapes=[
                pltpu.VMEM((2, rows, depth), BF16),
                pltpu.VMEM((2 * CAP, rank, depth), BF16),
                pltpu.SemaphoreType.DMA((len(args_rows),)),
                pltpu.SemaphoreType.DMA((2, CAP, 2)),
            ],
        ),
        out_shape=out_shape,
        compiler_params=params(),
        cost_estimate=cost(4 * rows * depth * CAP * rank, 4 * depth * (CAP * rank + rows)),
        name="scores",
    )(info, *args)


def build_spread(info_ref, lowrank_ref, got_ref, ids_ref, spread):
    rows, lanes = ids_ref.shape[1], ids_ref.shape[2]
    parity, place = info_ref[0], info_ref[1]
    upper = (lax.broadcasted_iota(jnp.int32, (rows, lanes), 1) >= lanes // 2).astype(jnp.int32)
    for slot in range(4):
        local = ((slot // 2) ^ parity) + 2 * (slot % 2)
        group = place ^ local
        values = lowrank_ref[group] + got_ref[group].astype(F32)
        values = jnp.concatenate([values, values], axis=0).T
        wanted = ids_ref[local] - upper
        for piece in range(8):
            spread[slot * rows : (slot + 1) * rows, piece * lanes : (piece + 1) * lanes] = (
                jnp.where(wanted == info_ref[2 + piece], values, 0.0).astype(BF16)
            )


def combine_kernel(build, info_ref, *refs):
    if build:
        lowrank_ref, got_ref, ids_ref, refs = refs[0], refs[1], refs[2], refs[3:]
        near_ref, far_ref, own_ref, core_ref, *blocks, keep_ref, send_ref, spread_ref, maps = refs

        @pl.when(pl.program_id(0) == 0)
        def _():
            build_spread(info_ref, lowrank_ref, got_ref, ids_ref, spread_ref)

    else:
        spread_ref, near_ref, far_ref, own_ref, core_ref, *blocks, keep_ref, send_ref, maps = refs
    parity = info_ref[0]
    rows = near_ref.shape[1]
    held = own_ref.shape[0]
    for index, ref in enumerate((own_ref, core_ref, *blocks)):
        maps[index * held : (index + 1) * held, :] = ref[...]
    delta = jnp.dot(spread_ref[...], maps[...], preferred_element_type=F32)
    for slot in range(4):
        source = near_ref if slot % 2 == 0 else far_ref
        value = source[(slot // 2) ^ parity] + delta[slot * rows : (slot + 1) * rows]
        if slot < 2:
            keep_ref[slot % 2] = value
        else:
            send_ref[slot % 2] = value.astype(BF16)


def combine(info, near, far, own_maps, core_maps, blocks, start, spread=None, build=()):
    rows = near.shape[1]
    width = far.shape[2]
    tile = 512
    first = start // tile
    per_place = core_maps.shape[1] // tile
    held = own_maps.shape[0]
    whole = lambda shape: pl.BlockSpec(shape, lambda n, s: (0,) * len(shape))
    ahead = list(build) if build else [spread]
    spread_shape = (4 * rows, 4 * held)
    in_specs = [whole(x.shape) for x in ahead]
    in_specs += [
        pl.BlockSpec((2, rows, tile), lambda n, s: (0, 0, first + n)),
        pl.BlockSpec((2, rows, tile), lambda n, s: (0, 0, n)),
        pl.BlockSpec((held, tile), lambda n, s: (0, s[1] * per_place + first + n)),
        pl.BlockSpec((held, tile), lambda n, s: (0, first + n)),
    ]
    in_specs += [
        pl.BlockSpec((held, tile), lambda n, s: (0, n)) for _ in blocks
    ]
    out_specs = [pl.BlockSpec((2, rows, tile), lambda n, s: (0, 0, n))] * 2
    out_shape = [jax.ShapeDtypeStruct((2, rows, width), kind) for kind in (F32, BF16)]
    if build:
        out_specs.append(whole(spread_shape))
        out_shape.append(jax.ShapeDtypeStruct(spread_shape, BF16))
    return pl.pallas_call(
        lambda *refs: combine_kernel(bool(build), *refs),
        grid_spec=pltpu.PrefetchScalarGridSpec(
            num_scalar_prefetch=1,
            grid=(width // tile,),
            in_specs=in_specs,
            out_specs=out_specs,
            scratch_shapes=[pltpu.VMEM((4 * held, tile), BF16)],
        ),
        out_shape=out_shape,
        compiler_params=params(),
        cost_estimate=cost(
            32 * rows * held * width, 26 * rows * width + 8 * held * width
        ),
        name="combine",
    )(info, *ahead, near, far, own_maps, core_maps, *blocks)


def per_device_fast(hidden, weight, input_maps, output_maps, slots, lists):
    rows, depth = hidden.shape
    place = lax.axis_index("pool")
    t = lax.axis_index("tensor")
    holding, rank = input_maps.shape[:2]
    held, features = output_maps.shape
    width = features // 4
    starts = [sum(WIDTHS[:i]) for i in range(len(WIDTHS))]
    count = len(WIDTHS)

    part = depth // HALVES
    near_b = swap(hidden, "pool", 1)
    first_a, first_b, second = (
        swap(block, "pool", 2) for block in cut_columns(hidden, (part // 2, part // 2, part))
    )

    core_block = lax.dynamic_slice(output_maps, (0, (place ^ 1) * width), (held, width))
    blocks = [
        lax.dynamic_slice(output_maps, (0, (place ^ other) * width + start), (held, wide))
        for start, wide in zip(starts, WIDTHS)
        for other in (2, 3)
    ]

    order = place ^ jnp.arange(4, dtype=jnp.int32)
    hot = order[:, None] == jnp.arange(4, dtype=jnp.int32)[None, :]
    slots_local = jnp.sum(jnp.where(hot[:, :, None], slots.reshape(1, 4, rows), 0), axis=1)
    lists_local = jnp.sum(jnp.where(hot[:, :, None], lists[None, :, :], 0), axis=1)
    positions = jnp.arange(lists.shape[1], dtype=jnp.int32)
    ids = jnp.sum(
        jnp.where(slots_local[:, :, None] == positions, lists_local[:, None, :], 0), axis=2
    )
    wide_ids = jnp.broadcast_to(ids[:, :, None], (4, rows, 128))
    owned_ids = (ids - place * holding).reshape(4, 1, rows)
    owned = (lists_local >= place * holding) & (lists_local < (place + 1) * holding)
    earlier = positions[None, :] < positions[:, None]
    rank_in_list = jnp.sum(owned[:, None, :] & earlier[None], axis=2)
    caps = jnp.arange(CAP, dtype=jnp.int32)
    chosen = jnp.sum(
        jnp.where(
            owned[:, None, :] & (rank_in_list[:, None, :] == caps[None, :, None]),
            (lists_local - place * holding)[:, None, :],
            0,
        ),
        axis=2,
    ).reshape(4 * CAP)
    picks = jnp.concatenate([place.reshape(1), chosen]).astype(jnp.int32)

    parity = (place ^ t) & 1
    per_owner = held // rank
    half_step = per_owner // 2
    owner_first = [holding * (place ^ j) + per_owner * t for j in range(4)]
    info = jnp.stack(
        [parity, place]
        + [owner_first[j] + half_step * h for j in range(4) for h in range(2)]
    ).astype(jnp.int32)

    ready = lax.optimization_barrier(
        (hidden, near_b, picks, info, wide_ids, owned_ids, core_block, *blocks)
    )
    own_rows, near_b, picks, info, wide_ids, owned_ids, core_block, *blocks = ready
    core_maps = swap(core_block, "pool", 1)

    (near_lowrank,) = scores(picks, 0, [own_rows], [near_b], input_maps, 0, ids=owned_ids)
    near_late = product(
        [[(tie(own_rows, near_lowrank), part, 1)], [(near_b, part, 1)]],
        weight, 1, 0, width, 512,
    )

    first_a, first_b = lax.optimization_barrier((first_a, first_b, near_late))[:2]
    a0 = [first_a, first_b]
    b0 = [swap(x, "pool", 1) for x in a0]
    (raw,) = scores(picks, 2, a0, b0, input_maps, 0)
    base = product(
        [
            [(tie(own_rows, raw), part, 0)],
            [(near_b, part, 0)],
            [(x, part // 2, 0) for x in a0],
            [(x, part // 2, 0) for x in b0],
        ],
        weight, 0, 0, width, 512, near_late,
    )
    a1 = tie(second, base)
    b1 = swap(a1, "pool", 1)
    total, sent = scores(
        picks, 2, [a1], [b1], input_maps, 1, prior=raw, near=near_lowrank, ids=owned_ids
    )

    def far_piece(index, after, hint=HINT):
        return product(
            [[(tie(a1, after), part, 0)], [(b1, part, 0)]],
            weight, 1, starts[index], WIDTHS[index], 256, base, 1, hint,
        ).reshape(2, rows, WIDTHS[index])

    got = [swap(sent, "pool", step) for step in (2, 3, 1)]
    pieces = [far_piece(0, sent, 1)]

    def start_maps(index, after):
        pair = blocks[2 * index : 2 * index + 2]
        return [swap(tie(x, after), "pool", 2 + k) for k, x in enumerate(pair)]

    moved = [[swap(blocks[0], "pool", 2), swap(tie(blocks[1], sent), "pool", 3)]]
    moved[0][0] = tie(moved[0][0], sent)
    got = lax.optimization_barrier((*got, moved[0][0], pieces[0]))[:3]
    total = total + sum(x.astype(F32) for x in got)
    sent = total.astype(BF16)
    got = swap(sent, "tensor", 1)
    moved.append(start_maps(1, sent))
    pieces.append(far_piece(1, sent, 1))
    got = tie(got, pieces[1])
    total = total + got.astype(F32)
    sent = total.astype(BF16)
    got = swap(sent, "tensor", 2)
    moved.append(start_maps(2, sent))
    moved[0][1] = tie(moved[0][1], sent)
    got = lax.optimization_barrier((got, *moved[0]))[0]

    near_base = base.reshape(4, rows, width)
    side = ((place ^ t) >> 1) & 1
    parts = []
    spread = send = None

    def maps_of(index, after):
        return moved[index] if after is None else [tie(x, after) for x in moved[index]]

    def pace(index):
        return near_base if index < 2 else tie(near_base, started[index - 2])

    started = []

    halves = []

    def finish(index, after):
        keep, got = halves[index]
        got = got if after is None else tie(got, after)
        pair = keep + got.astype(F32)
        sent = jnp.where(side == 0, pair[1], pair[0]).astype(BF16)
        kept = jnp.where(side == 0, pair[0], pair[1])
        started.append(sent)
        return kept + swap(sent, "tensor", 2).astype(F32)

    for chunk in range(count):
        common = (
            info, pace(chunk), pieces[chunk], output_maps, core_maps,
            maps_of(chunk, started[chunk - 2] if chunk > 1 else send), starts[chunk],
        )
        if chunk == 0:
            keep, send, spread = combine(*common, build=(total, got, wide_ids))
            moved.append(start_maps(3, send))
        else:
            keep, send = combine(*common, spread=spread)
        if chunk == 0:
            pieces.append(far_piece(2, send))
        halves.append((keep, swap(send, "tensor", 1)))
        if chunk > 0:
            parts.append(finish(chunk - 1, send))
        if chunk == 1:
            pieces.append(far_piece(3, started[0]))
    parts.append(finish(count - 1, started[-1]))
    return jnp.concatenate(parts, axis=1).astype(BF16)


def per_device_general(hidden, weight, input_maps, output_maps, slots, lists):
    rows, depth = hidden.shape
    pool_count = lax.axis_size("pool")
    tensor_count = lax.axis_size("tensor")
    place = lax.axis_index("pool")
    t = lax.axis_index("tensor")
    holding, rank = input_maps.shape[:2]
    held = output_maps.shape[0]
    total_rows = rows * pool_count
    slot_ids = jnp.arange(lists.shape[1], dtype=jnp.int32)
    slot_hot = slots.reshape(pool_count, rows)[:, :, None] == slot_ids
    ids = jnp.sum(jnp.where(slot_hot, lists[:, None, :], 0), axis=2).reshape(total_rows)
    gathered = lax.all_gather(hidden, "pool", axis=0, tiled=True)
    scored = lax.dot_general(
        gathered,
        input_maps.reshape(holding * rank, depth),
        (((1,), (1,)), ((), ())),
        preferred_element_type=F32,
    ).reshape(total_rows, holding, rank)
    owned = place * holding + jnp.arange(holding, dtype=jnp.int32)
    partial = jnp.sum(
        jnp.where((ids[:, None] == owned[None, :])[:, :, None], scored, 0.0), axis=1
    )
    lowrank = lax.psum(partial, ("tensor", "pool")).astype(BF16)
    maps = lax.all_to_all(output_maps, "pool", split_axis=1, concat_axis=0, tiled=True)
    columns = jnp.arange(pool_count * held, dtype=jnp.int32)
    source = (columns // held * tensor_count + t) * held + columns % held
    pick = (source[None, :] % rank == jnp.arange(rank, dtype=jnp.int32)[:, None]).astype(BF16)
    placed = jnp.dot(lowrank, pick, preferred_element_type=F32).astype(BF16)
    spread = jnp.where(ids[:, None] == source[None, :] // rank, placed, jnp.zeros_like(placed))
    value = jnp.dot(gathered, weight, preferred_element_type=F32)
    value = value + jnp.dot(spread, maps, preferred_element_type=F32)
    mixed = lax.psum_scatter(value, "tensor", scatter_dimension=0, tiled=True)
    return mixed.astype(BF16)


def solution(mesh):
    shape = dict(mesh.shape)
    fast = shape["groups"] == 2 and shape["pool"] == 4 and shape["tensor"] == 4
    placed = (
        P(("groups", "pool"), "tensor"),
        P("tensor", "pool"),
        P("pool", None, "tensor"),
        P(("pool", "tensor"), None),
        P("groups"),
        P("groups", None),
    )
    return jax.shard_map(
        per_device_fast if fast else per_device_general,
        mesh=mesh,
        in_specs=placed,
        out_specs=P(("groups", "tensor"), "pool"),
        check_vma=False,
    )
```

```python
import jax
import jax.numpy as jnp
from jax import lax
from jax.experimental import pallas as pl
from jax.experimental.pallas import tpu as pltpu
from jax.sharding import PartitionSpec as P

F32 = jnp.float32
BF16 = jnp.bfloat16
VMEM_LIMIT = 48 * 1024 * 1024
WIDTHS = (512, 512, 512, 512)
CAP = 4
HALVES = 2
HINT = 1000


def partners(count, step):
    return [(i, i ^ step) for i in range(count)]


def swap(values, axis, step):
    return lax.ppermute(values, axis, partners(lax.axis_size(axis), step))


def tie(values, *after):
    return lax.optimization_barrier((values, *after))[0]


def cost(flops, moved, hint=HINT):
    return pl.CostEstimate(flops=flops // hint, bytes_accessed=moved // hint, transcendentals=0)


def params():
    return pltpu.CompilerParams(vmem_limit_bytes=VMEM_LIMIT)


def cut_kernel(ref, *refs):
    outs, (stage, sems) = refs[:-2], refs[-2:]
    inward, outward, start = [], [], 0
    for index, out in enumerate(outs):
        spot = pl.ds(start, out.shape[1])
        inward.append(
            pltpu.make_async_copy(ref.at[:, spot], stage.at[:, spot], sems.at[0, index])
        )
        outward.append(pltpu.make_async_copy(stage.at[:, spot], out, sems.at[1, index]))
        start += out.shape[1]
    for copy in inward:
        copy.start()
    for copy, after in zip(inward, outward):
        copy.wait()
        after.start()
    for copy in outward:
        copy.wait()


def cut_columns(array, widths):
    return pl.pallas_call(
        cut_kernel,
        in_specs=[pl.BlockSpec(memory_space=pl.ANY)],
        out_specs=[pl.BlockSpec(memory_space=pl.ANY)] * len(widths),
        out_shape=[jax.ShapeDtypeStruct((array.shape[0], w), array.dtype) for w in widths],
        scratch_shapes=[
            pltpu.VMEM(array.shape, array.dtype),
            pltpu.SemaphoreType.DMA((2, len(widths))),
        ],
        compiler_params=params(),
        cost_estimate=cost(0, 4 * array.size),
        name="cut",
    )(array)


def product_kernel(counts, has_prior, *refs):
    pieces, refs = refs[: sum(counts)], refs[sum(counts) :]
    if has_prior:
        prior_ref, refs = refs[0], refs[1:]
    w_ref, out_ref, rows = refs

    @pl.when(pl.program_id(0) == 0)
    def _():
        height = rows.shape[0] // len(counts)
        spot = 0
        for group, count in enumerate(counts):
            start = 0
            for piece in pieces[spot : spot + count]:
                wide = piece.shape[1]
                rows[group * height : (group + 1) * height, start : start + wide] = piece[...]
                start += wide
            spot += count

    value = jnp.dot(rows[...], w_ref[...], preferred_element_type=F32)
    if has_prior:
        top = prior_ref.shape[0]
        out_ref[:top, :] = value[:top] + prior_ref[...]
        if top < value.shape[0]:
            out_ref[top:, :] = value[top:]
    else:
        out_ref[...] = value


def product(groups, weight, depth_block, first, width, tile, prior=None, prior_block=0, hint=HINT):
    rows = groups[0][0][0].shape[0]
    depth = sum(wide for _, wide, _ in groups[0])
    total = rows * len(groups)
    in_specs, args = [], []
    for group in groups:
        for array, wide, block in group:
            in_specs.append(pl.BlockSpec((rows, wide), lambda n, block=block: (0, block)))
            args.append(array)
    if prior is not None:
        in_specs.append(
            pl.BlockSpec((2 * rows, tile), lambda n: (prior_block, first // tile + n))
        )
        args.append(prior)
    in_specs.append(pl.BlockSpec((depth, tile), lambda n: (depth_block, first // tile + n)))
    args.append(weight)
    counts = [len(group) for group in groups]
    return pl.pallas_call(
        lambda *refs: product_kernel(counts, prior is not None, *refs),
        grid=(width // tile,),
        in_specs=in_specs,
        out_specs=pl.BlockSpec((total, tile), lambda n: (0, n)),
        out_shape=jax.ShapeDtypeStruct((total, width), F32),
        scratch_shapes=[pltpu.VMEM((total, depth), BF16)],
        compiler_params=params(),
        cost_estimate=cost(
            2 * total * depth * width, 2 * depth * (width + total) + 8 * total * width, hint
        ),
        name="base",
    )(*args)


def scores_kernel(first, offset, count, has_prior, last, info_ref, *refs):
    groups, maps_ref, refs = (refs[:count], refs[count : 2 * count]), refs[2 * count], refs[2 * count + 1 :]
    if has_prior:
        prior_ref, refs = refs[0], refs[1:]
    if first == 2 and last:
        near_ref, refs = refs[0], refs[1:]
    if last:
        ids_ref, refs = refs[0], refs[1:]
    outs, (rows, maps, row_sems, map_sems) = refs[:-4], refs[-4:]
    depth = rows.shape[2]
    cut = depth // 2

    def map_copy(pair, k, part):
        chosen = info_ref[1 + (first + pair) * CAP + k]
        return pltpu.make_async_copy(
            maps_ref.at[chosen, :, pl.ds(offset + part * cut, cut)],
            maps.at[pair * CAP + k, :, pl.ds(part * cut, cut)],
            map_sems.at[pair, k, part],
        )

    row_copies = []
    for pair, pieces in enumerate(groups):
        start = 0
        for index, piece in enumerate(pieces):
            row_copies.append(
                pltpu.make_async_copy(
                    piece,
                    rows.at[pair, :, pl.ds(start, piece.shape[1])],
                    row_sems.at[pair * count + index],
                )
            )
            start += piece.shape[1]
    for pair in range(2):
        for copy in row_copies[pair * count : (pair + 1) * count]:
            copy.start()
        for part in range(2):
            for k in range(CAP):
                map_copy(pair, k, part).start()
    for pair in range(2):
        for copy in row_copies[pair * count : (pair + 1) * count]:
            copy.wait()
        total = prior_ref[pair] if has_prior else None
        for part in range(2):
            for k in range(CAP):
                map_copy(pair, k, part).wait()
            columns = slice(part * cut, (part + 1) * cut)
            chosen = maps[pair * CAP : (pair + 1) * CAP, :, columns]
            term = lax.dot_general(
                chosen.reshape(-1, cut),
                rows[pair, :, columns],
                (((1,), (1,)), ((), ())),
                preferred_element_type=F32,
            )
            total = term if total is None else total + term
        if not last:
            outs[0][pair] = total
            continue
        wanted = ids_ref[pair]
        rank = total.shape[0] // CAP
        found = jnp.zeros((rank, total.shape[1]), F32)
        for k in range(CAP):
            mine = info_ref[1 + (first + pair) * CAP + k]
            found += jnp.where(wanted == mine, total[k * rank : (k + 1) * rank], 0.0)
        if first == 0:
            outs[0][pair] = found
        else:
            near_group = info_ref[0] ^ pair
            far_group = near_group ^ 2
            outs[0][far_group] = found
            outs[1][far_group] = found.astype(BF16)
            outs[0][near_group] = near_ref[pair]
            outs[1][near_group] = near_ref[pair].astype(BF16)


def scores(info, first, lower, upper, maps, half, prior=None, near=None, ids=None):
    rows, depth = lower[0].shape[0], sum(x.shape[1] for x in lower)
    rank = maps.shape[1]
    has_prior, last = prior is not None, ids is not None
    args_rows = [*lower, *upper]
    whole = lambda x: pl.BlockSpec(x.shape, lambda k, s: (0,) * x.ndim)
    args = [*lower, *upper, maps]
    in_specs = [pl.BlockSpec(memory_space=pl.ANY)] * len(args)
    if has_prior:
        in_specs.append(whole(prior))
        args.append(prior)
    if near is not None:
        in_specs.append(whole(near))
        args.append(near)
    if last:
        in_specs.append(
            pl.BlockSpec((2,) + ids.shape[1:], lambda k, s: (first // 2, 0, 0))
        )
        args.append(ids)
    if not last:
        out_shape = [jax.ShapeDtypeStruct((2, CAP * rank, rows), F32)]
    elif first == 0:
        out_shape = [jax.ShapeDtypeStruct((2, rank, rows), F32)]
    else:
        out_shape = [jax.ShapeDtypeStruct((4, rank, rows), kind) for kind in (F32, BF16)]
    return pl.pallas_call(
        lambda *refs: scores_kernel(first, half * depth, len(lower), has_prior, last, *refs),
        grid_spec=pltpu.PrefetchScalarGridSpec(
            num_scalar_prefetch=1,
            grid=(1,),
            in_specs=in_specs,
            out_specs=[whole(x) for x in out_shape],
            scratch_shapes=[
                pltpu.VMEM((2, rows, depth), BF16),
                pltpu.VMEM((2 * CAP, rank, depth), BF16),
                pltpu.SemaphoreType.DMA((len(args_rows),)),
                pltpu.SemaphoreType.DMA((2, CAP, 2)),
            ],
        ),
        out_shape=out_shape,
        compiler_params=params(),
        cost_estimate=cost(4 * rows * depth * CAP * rank, 4 * depth * (CAP * rank + rows)),
        name="scores",
    )(info, *args)


def build_spread(info_ref, lowrank_ref, got_ref, ids_ref, spread):
    rows, lanes = ids_ref.shape[1], ids_ref.shape[2]
    parity, place = info_ref[0], info_ref[1]
    upper = (lax.broadcasted_iota(jnp.int32, (rows, lanes), 1) >= lanes // 2).astype(jnp.int32)
    for slot in range(4):
        local = ((slot // 2) ^ parity) + 2 * (slot % 2)
        group = place ^ local
        values = lowrank_ref[group] + got_ref[group].astype(F32)
        values = jnp.concatenate([values, values], axis=0).T
        wanted = ids_ref[local] - upper
        for piece in range(8):
            spread[slot * rows : (slot + 1) * rows, piece * lanes : (piece + 1) * lanes] = (
                jnp.where(wanted == info_ref[2 + piece], values, 0.0).astype(BF16)
            )


def combine_kernel(build, info_ref, *refs):
    if build:
        lowrank_ref, got_ref, ids_ref, refs = refs[0], refs[1], refs[2], refs[3:]
        near_ref, far_ref, own_ref, core_ref, *blocks, keep_ref, send_ref, spread_ref, maps = refs

        @pl.when(pl.program_id(0) == 0)
        def _():
            build_spread(info_ref, lowrank_ref, got_ref, ids_ref, spread_ref)

    else:
        spread_ref, near_ref, far_ref, own_ref, core_ref, *blocks, keep_ref, send_ref, maps = refs
    parity = info_ref[0]
    rows = near_ref.shape[1]
    held = own_ref.shape[0]
    for index, ref in enumerate((own_ref, core_ref, *blocks)):
        maps[index * held : (index + 1) * held, :] = ref[...]
    delta = jnp.dot(spread_ref[...], maps[...], preferred_element_type=F32)
    for slot in range(4):
        source = near_ref if slot % 2 == 0 else far_ref
        value = source[(slot // 2) ^ parity] + delta[slot * rows : (slot + 1) * rows]
        if slot < 2:
            keep_ref[slot % 2] = value
        else:
            send_ref[slot % 2] = value.astype(BF16)


def combine(info, near, far, own_maps, core_maps, blocks, start, spread=None, build=()):
    rows = near.shape[1]
    width = far.shape[2]
    tile = 512
    first = start // tile
    per_place = core_maps.shape[1] // tile
    held = own_maps.shape[0]
    whole = lambda shape: pl.BlockSpec(shape, lambda n, s: (0,) * len(shape))
    ahead = list(build) if build else [spread]
    spread_shape = (4 * rows, 4 * held)
    in_specs = [whole(x.shape) for x in ahead]
    in_specs += [
        pl.BlockSpec((2, rows, tile), lambda n, s: (0, 0, first + n)),
        pl.BlockSpec((2, rows, tile), lambda n, s: (0, 0, n)),
        pl.BlockSpec((held, tile), lambda n, s: (0, s[1] * per_place + first + n)),
        pl.BlockSpec((held, tile), lambda n, s: (0, first + n)),
    ]
    in_specs += [
        pl.BlockSpec((held, tile), lambda n, s: (0, n)) for _ in blocks
    ]
    out_specs = [pl.BlockSpec((2, rows, tile), lambda n, s: (0, 0, n))] * 2
    out_shape = [jax.ShapeDtypeStruct((2, rows, width), kind) for kind in (F32, BF16)]
    if build:
        out_specs.append(whole(spread_shape))
        out_shape.append(jax.ShapeDtypeStruct(spread_shape, BF16))
    return pl.pallas_call(
        lambda *refs: combine_kernel(bool(build), *refs),
        grid_spec=pltpu.PrefetchScalarGridSpec(
            num_scalar_prefetch=1,
            grid=(width // tile,),
            in_specs=in_specs,
            out_specs=out_specs,
            scratch_shapes=[pltpu.VMEM((4 * held, tile), BF16)],
        ),
        out_shape=out_shape,
        compiler_params=params(),
        cost_estimate=cost(
            32 * rows * held * width, 26 * rows * width + 8 * held * width
        ),
        name="combine",
    )(info, *ahead, near, far, own_maps, core_maps, *blocks)


def per_device_fast(hidden, weight, input_maps, output_maps, slots, lists):
    rows, depth = hidden.shape
    place = lax.axis_index("pool")
    t = lax.axis_index("tensor")
    holding, rank = input_maps.shape[:2]
    held, features = output_maps.shape
    width = features // 4
    starts = [sum(WIDTHS[:i]) for i in range(len(WIDTHS))]
    count = len(WIDTHS)

    part = depth // HALVES
    near_b = swap(hidden, "pool", 1)
    *early, late = cut_columns(hidden, (part // 2, part // 2, part))
    first_a, first_b = (swap(block, "pool", 2) for block in early)

    core_block = lax.dynamic_slice(output_maps, (0, (place ^ 1) * width), (held, width))

    def block_for(index, other, source):
        return lax.dynamic_slice(
            source, (0, (place ^ other) * width + starts[index]), (held, WIDTHS[index])
        )

    blocks = [block_for(index, other, output_maps) for index in range(2) for other in (2, 3)]

    order = place ^ jnp.arange(4, dtype=jnp.int32)
    hot = order[:, None] == jnp.arange(4, dtype=jnp.int32)[None, :]
    slots_local = jnp.sum(jnp.where(hot[:, :, None], slots.reshape(1, 4, rows), 0), axis=1)
    lists_local = jnp.sum(jnp.where(hot[:, :, None], lists[None, :, :], 0), axis=1)
    positions = jnp.arange(lists.shape[1], dtype=jnp.int32)
    ids = jnp.sum(
        jnp.where(slots_local[:, :, None] == positions, lists_local[:, None, :], 0), axis=2
    )
    wide_ids = jnp.broadcast_to(ids[:, :, None], (4, rows, 128))
    owned_ids = (ids - place * holding).reshape(4, 1, rows)
    owned = (lists_local >= place * holding) & (lists_local < (place + 1) * holding)
    earlier = positions[None, :] < positions[:, None]
    rank_in_list = jnp.sum(owned[:, None, :] & earlier[None], axis=2)
    caps = jnp.arange(CAP, dtype=jnp.int32)
    chosen = jnp.sum(
        jnp.where(
            owned[:, None, :] & (rank_in_list[:, None, :] == caps[None, :, None]),
            (lists_local - place * holding)[:, None, :],
            0,
        ),
        axis=2,
    ).reshape(4 * CAP)
    picks = jnp.concatenate([place.reshape(1), chosen]).astype(jnp.int32)

    parity = (place ^ t) & 1
    per_owner = held // rank
    half_step = per_owner // 2
    owner_first = [holding * (place ^ j) + per_owner * t for j in range(4)]
    info = jnp.stack(
        [parity, place]
        + [owner_first[j] + half_step * h for j in range(4) for h in range(2)]
    ).astype(jnp.int32)

    ready = lax.optimization_barrier(
        (hidden, near_b, picks, info, wide_ids, owned_ids, core_block, *blocks)
    )
    own_rows, near_b, picks, info, wide_ids, owned_ids, core_block, *blocks = ready
    core_maps = swap(core_block, "pool", 1)

    (near_lowrank,) = scores(picks, 0, [own_rows], [near_b], input_maps, 0, ids=owned_ids)
    second = swap(tie(late, near_lowrank), "pool", 2)
    near_late = product(
        [[(tie(own_rows, near_lowrank), part, 1)], [(near_b, part, 1)]],
        weight, 1, 0, width, 512,
    )

    first_a, first_b = lax.optimization_barrier((first_a, first_b, near_late))[:2]
    a0 = [first_a, first_b]
    b0 = [swap(x, "pool", 1) for x in a0]
    (raw,) = scores(picks, 2, a0, b0, input_maps, 0)
    base = product(
        [
            [(tie(own_rows, raw), part, 0)],
            [(near_b, part, 0)],
            [(x, part // 2, 0) for x in a0],
            [(x, part // 2, 0) for x in b0],
        ],
        weight, 0, 0, width, 512, near_late,
    )
    a1 = tie(second, base)
    b1 = swap(a1, "pool", 1)
    total, sent = scores(
        picks, 2, [a1], [b1], input_maps, 1, prior=raw, near=near_lowrank, ids=owned_ids
    )

    def far_piece(index, after, hint=HINT):
        return product(
            [[(tie(a1, after), part, 0)], [(b1, part, 0)]],
            weight, 1, starts[index], WIDTHS[index], 256, base, 1, hint,
        ).reshape(2, rows, WIDTHS[index])

    got = [swap(sent, "pool", step) for step in (2, 3, 1)]
    pieces = [far_piece(0, sent, 1)]

    def start_maps(index, after):
        pair = later[2 * (index - 2) : 2 * (index - 2) + 2]
        return [swap(tie(x, after), "pool", 2 + k) for k, x in enumerate(pair)]

    moved = [[swap(blocks[0], "pool", 2), swap(tie(blocks[1], sent), "pool", 3)]]
    moved.append([swap(tie(blocks[k], sent), "pool", k) for k in (2, 3)])
    moved[0][0] = tie(moved[0][0], sent)
    got = lax.optimization_barrier((*got, moved[0][0], pieces[0]))[:3]
    total = total + sum(x.astype(F32) for x in got)
    sent = total.astype(BF16)
    got = swap(sent, "tensor", 1)
    pieces.append(far_piece(1, sent, 1))
    moved[0][1] = tie(moved[0][1], sent)
    got = lax.optimization_barrier((got, pieces[1], moved[0][1]))[0]
    total = total + got.astype(F32)
    sent = total.astype(BF16)
    got = swap(sent, "tensor", 2)
    source = tie(output_maps, sent)
    later = [block_for(index, other, source) for index in (2, 3) for other in (2, 3)]
    got, *later = lax.optimization_barrier((got, *later))
    moved.append(start_maps(2, sent))
    moved[1][0] = tie(moved[1][0], sent)
    got = lax.optimization_barrier((got, *moved[0], moved[1][0]))[0]

    near_base = base.reshape(4, rows, width)
    side = ((place ^ t) >> 1) & 1
    parts = []
    spread = send = None

    def maps_of(index, after):
        return moved[index] if after is None else [tie(x, after) for x in moved[index]]

    def pace(index):
        if index == 1:
            moved[2][0] = tie(moved[2][0], send)
            return tie(near_base, moved[2][0])
        return near_base if index < 2 else tie(near_base, started[index - 2])

    started = []

    halves = []

    def finish(index, after):
        keep, got = halves[index]
        got = tie(got, after)
        if index == 2:
            got = tie(got, parts[1])
        pair = keep + got.astype(F32)
        sent = jnp.where(side == 0, pair[1], pair[0]).astype(BF16)
        kept = jnp.where(side == 0, pair[0], pair[1])
        started.append(sent)
        return kept + swap(sent, "tensor", 2).astype(F32)

    for chunk in range(count):
        common = (
            info, pace(chunk), pieces[chunk], output_maps, core_maps,
            maps_of(chunk, started[chunk - 2] if chunk > 1 else send), starts[chunk],
        )
        if chunk == 0:
            keep, send, spread = combine(*common, build=(total, got, wide_ids))
            moved.append(start_maps(3, send))
        else:
            keep, send = combine(*common, spread=spread)
        if chunk == 0:
            pieces.append(far_piece(2, send))
        halves.append((keep, swap(send, "tensor", 1)))
        if chunk > 0:
            parts.append(finish(chunk - 1, send))
        if chunk == 1:
            pieces.append(far_piece(3, started[0]))
    parts.append(finish(count - 1, started[-1]))
    return jnp.concatenate(parts, axis=1).astype(BF16)


def per_device_general(hidden, weight, input_maps, output_maps, slots, lists):
    rows, depth = hidden.shape
    pool_count = lax.axis_size("pool")
    tensor_count = lax.axis_size("tensor")
    place = lax.axis_index("pool")
    t = lax.axis_index("tensor")
    holding, rank = input_maps.shape[:2]
    held = output_maps.shape[0]
    total_rows = rows * pool_count
    slot_ids = jnp.arange(lists.shape[1], dtype=jnp.int32)
    slot_hot = slots.reshape(pool_count, rows)[:, :, None] == slot_ids
    ids = jnp.sum(jnp.where(slot_hot, lists[:, None, :], 0), axis=2).reshape(total_rows)
    gathered = lax.all_gather(hidden, "pool", axis=0, tiled=True)
    scored = lax.dot_general(
        gathered,
        input_maps.reshape(holding * rank, depth),
        (((1,), (1,)), ((), ())),
        preferred_element_type=F32,
    ).reshape(total_rows, holding, rank)
    owned = place * holding + jnp.arange(holding, dtype=jnp.int32)
    partial = jnp.sum(
        jnp.where((ids[:, None] == owned[None, :])[:, :, None], scored, 0.0), axis=1
    )
    lowrank = lax.psum(partial, ("tensor", "pool")).astype(BF16)
    maps = lax.all_to_all(output_maps, "pool", split_axis=1, concat_axis=0, tiled=True)
    columns = jnp.arange(pool_count * held, dtype=jnp.int32)
    source = (columns // held * tensor_count + t) * held + columns % held
    pick = (source[None, :] % rank == jnp.arange(rank, dtype=jnp.int32)[:, None]).astype(BF16)
    placed = jnp.dot(lowrank, pick, preferred_element_type=F32).astype(BF16)
    spread = jnp.where(ids[:, None] == source[None, :] // rank, placed, jnp.zeros_like(placed))
    value = jnp.dot(gathered, weight, preferred_element_type=F32)
    value = value + jnp.dot(spread, maps, preferred_element_type=F32)
    mixed = lax.psum_scatter(value, "tensor", scatter_dimension=0, tiled=True)
    return mixed.astype(BF16)


def solution(mesh):
    shape = dict(mesh.shape)
    fast = shape["groups"] == 2 and shape["pool"] == 4 and shape["tensor"] == 4
    placed = (
        P(("groups", "pool"), "tensor"),
        P("tensor", "pool"),
        P("pool", None, "tensor"),
        P(("pool", "tensor"), None),
        P("groups"),
        P("groups", None),
    )
    return jax.shard_map(
        per_device_fast if fast else per_device_general,
        mesh=mesh,
        in_specs=placed,
        out_specs=P(("groups", "tensor"), "pool"),
        check_vma=False,
    )
```

```python
import jax
import jax.numpy as jnp
from jax import lax
from jax.experimental import pallas as pl
from jax.experimental.pallas import tpu as pltpu
from jax.sharding import PartitionSpec as P

F32 = jnp.float32
BF16 = jnp.bfloat16
VMEM_LIMIT = 48 * 1024 * 1024
WIDTHS = (512, 512, 512, 512)
CAP = 4
HALVES = 2
HINT = 1000


def partners(count, step):
    return [(i, i ^ step) for i in range(count)]


def swap(values, axis, step):
    return lax.ppermute(values, axis, partners(lax.axis_size(axis), step))


def tie(values, *after):
    return lax.optimization_barrier((values, *after))[0]


def cost(flops, moved, hint=HINT):
    return pl.CostEstimate(flops=flops // hint, bytes_accessed=moved // hint, transcendentals=0)


def params():
    return pltpu.CompilerParams(vmem_limit_bytes=VMEM_LIMIT)


def cut_kernel(ref, *refs):
    outs, (stage, sems) = refs[:-2], refs[-2:]
    inward, outward, start = [], [], 0
    for index, out in enumerate(outs):
        spot = pl.ds(start, out.shape[1])
        inward.append(
            pltpu.make_async_copy(ref.at[:, spot], stage.at[:, spot], sems.at[0, index])
        )
        outward.append(pltpu.make_async_copy(stage.at[:, spot], out, sems.at[1, index]))
        start += out.shape[1]
    for copy in inward:
        copy.start()
    for copy, after in zip(inward, outward):
        copy.wait()
        after.start()
    for copy in outward:
        copy.wait()


def cut_columns(array, widths):
    return pl.pallas_call(
        cut_kernel,
        in_specs=[pl.BlockSpec(memory_space=pl.ANY)],
        out_specs=[pl.BlockSpec(memory_space=pl.ANY)] * len(widths),
        out_shape=[jax.ShapeDtypeStruct((array.shape[0], w), array.dtype) for w in widths],
        scratch_shapes=[
            pltpu.VMEM(array.shape, array.dtype),
            pltpu.SemaphoreType.DMA((2, len(widths))),
        ],
        compiler_params=params(),
        cost_estimate=cost(0, 4 * array.size),
        name="cut",
    )(array)


def product_kernel(counts, has_prior, *refs):
    pieces, refs = refs[: sum(counts)], refs[sum(counts) :]
    if has_prior:
        prior_ref, refs = refs[0], refs[1:]
    w_ref, out_ref, rows = refs

    @pl.when(pl.program_id(0) == 0)
    def _():
        height = rows.shape[0] // len(counts)
        spot = 0
        for group, count in enumerate(counts):
            start = 0
            for piece in pieces[spot : spot + count]:
                wide = piece.shape[1]
                rows[group * height : (group + 1) * height, start : start + wide] = piece[...]
                start += wide
            spot += count

    value = jnp.dot(rows[...], w_ref[...], preferred_element_type=F32)
    if has_prior:
        top = prior_ref.shape[0]
        out_ref[:top, :] = value[:top] + prior_ref[...]
        if top < value.shape[0]:
            out_ref[top:, :] = value[top:]
    else:
        out_ref[...] = value


def product(groups, weight, depth_block, first, width, tile, prior=None, prior_block=0, hint=HINT):
    rows = groups[0][0][0].shape[0]
    depth = sum(wide for _, wide, _ in groups[0])
    total = rows * len(groups)
    in_specs, args = [], []
    for group in groups:
        for array, wide, block in group:
            in_specs.append(pl.BlockSpec((rows, wide), lambda n, block=block: (0, block)))
            args.append(array)
    if prior is not None:
        in_specs.append(
            pl.BlockSpec((2 * rows, tile), lambda n: (prior_block, first // tile + n))
        )
        args.append(prior)
    in_specs.append(pl.BlockSpec((depth, tile), lambda n: (depth_block, first // tile + n)))
    args.append(weight)
    counts = [len(group) for group in groups]
    return pl.pallas_call(
        lambda *refs: product_kernel(counts, prior is not None, *refs),
        grid=(width // tile,),
        in_specs=in_specs,
        out_specs=pl.BlockSpec((total, tile), lambda n: (0, n)),
        out_shape=jax.ShapeDtypeStruct((total, width), F32),
        scratch_shapes=[pltpu.VMEM((total, depth), BF16)],
        compiler_params=params(),
        cost_estimate=cost(
            2 * total * depth * width, 2 * depth * (width + total) + 8 * total * width, hint
        ),
        name="base",
    )(*args)


def scores_kernel(first, offset, count, has_prior, last, info_ref, *refs):
    groups, maps_ref, refs = (refs[:count], refs[count : 2 * count]), refs[2 * count], refs[2 * count + 1 :]
    if has_prior:
        prior_ref, refs = refs[0], refs[1:]
    if first == 2 and last:
        near_ref, refs = refs[0], refs[1:]
    if last:
        ids_ref, refs = refs[0], refs[1:]
    outs, (rows, maps, row_sems, map_sems) = refs[:-4], refs[-4:]
    depth = rows.shape[2]
    cut = depth // 2

    def map_copy(pair, k, part):
        chosen = info_ref[1 + (first + pair) * CAP + k]
        return pltpu.make_async_copy(
            maps_ref.at[chosen, :, pl.ds(offset + part * cut, cut)],
            maps.at[pair * CAP + k, :, pl.ds(part * cut, cut)],
            map_sems.at[pair, k, part],
        )

    row_copies = []
    for pair, pieces in enumerate(groups):
        start = 0
        for index, piece in enumerate(pieces):
            row_copies.append(
                pltpu.make_async_copy(
                    piece,
                    rows.at[pair, :, pl.ds(start, piece.shape[1])],
                    row_sems.at[pair * count + index],
                )
            )
            start += piece.shape[1]
    for pair in range(2):
        for copy in row_copies[pair * count : (pair + 1) * count]:
            copy.start()
        for part in range(2):
            for k in range(CAP):
                map_copy(pair, k, part).start()
    for pair in range(2):
        for copy in row_copies[pair * count : (pair + 1) * count]:
            copy.wait()
        total = prior_ref[pair] if has_prior else None
        for part in range(2):
            for k in range(CAP):
                map_copy(pair, k, part).wait()
            columns = slice(part * cut, (part + 1) * cut)
            chosen = maps[pair * CAP : (pair + 1) * CAP, :, columns]
            term = lax.dot_general(
                chosen.reshape(-1, cut),
                rows[pair, :, columns],
                (((1,), (1,)), ((), ())),
                preferred_element_type=F32,
            )
            total = term if total is None else total + term
        if not last:
            outs[0][pair] = total
            continue
        wanted = ids_ref[pair]
        rank = total.shape[0] // CAP
        found = jnp.zeros((rank, total.shape[1]), F32)
        for k in range(CAP):
            mine = info_ref[1 + (first + pair) * CAP + k]
            found += jnp.where(wanted == mine, total[k * rank : (k + 1) * rank], 0.0)
        if first == 0:
            outs[0][pair] = found
        else:
            near_group = info_ref[0] ^ pair
            far_group = near_group ^ 2
            outs[0][far_group] = found
            outs[1][far_group] = found.astype(BF16)
            outs[0][near_group] = near_ref[pair]
            outs[1][near_group] = near_ref[pair].astype(BF16)


def scores(info, first, lower, upper, maps, half, prior=None, near=None, ids=None):
    rows, depth = lower[0].shape[0], sum(x.shape[1] for x in lower)
    rank = maps.shape[1]
    has_prior, last = prior is not None, ids is not None
    args_rows = [*lower, *upper]
    whole = lambda x: pl.BlockSpec(x.shape, lambda k, s: (0,) * x.ndim)
    args = [*lower, *upper, maps]
    in_specs = [pl.BlockSpec(memory_space=pl.ANY)] * len(args)
    if has_prior:
        in_specs.append(whole(prior))
        args.append(prior)
    if near is not None:
        in_specs.append(whole(near))
        args.append(near)
    if last:
        in_specs.append(
            pl.BlockSpec((2,) + ids.shape[1:], lambda k, s: (first // 2, 0, 0))
        )
        args.append(ids)
    if not last:
        out_shape = [jax.ShapeDtypeStruct((2, CAP * rank, rows), F32)]
    elif first == 0:
        out_shape = [jax.ShapeDtypeStruct((2, rank, rows), F32)]
    else:
        out_shape = [jax.ShapeDtypeStruct((4, rank, rows), kind) for kind in (F32, BF16)]
    return pl.pallas_call(
        lambda *refs: scores_kernel(first, half * depth, len(lower), has_prior, last, *refs),
        grid_spec=pltpu.PrefetchScalarGridSpec(
            num_scalar_prefetch=1,
            grid=(1,),
            in_specs=in_specs,
            out_specs=[whole(x) for x in out_shape],
            scratch_shapes=[
                pltpu.VMEM((2, rows, depth), BF16),
                pltpu.VMEM((2 * CAP, rank, depth), BF16),
                pltpu.SemaphoreType.DMA((len(args_rows),)),
                pltpu.SemaphoreType.DMA((2, CAP, 2)),
            ],
        ),
        out_shape=out_shape,
        compiler_params=params(),
        cost_estimate=cost(4 * rows * depth * CAP * rank, 4 * depth * (CAP * rank + rows)),
        name="scores",
    )(info, *args)


def build_spread(info_ref, lowrank_ref, got_ref, ids_ref, spread):
    rows, lanes = ids_ref.shape[1], ids_ref.shape[2]
    parity, place = info_ref[0], info_ref[1]
    upper = (lax.broadcasted_iota(jnp.int32, (rows, lanes), 1) >= lanes // 2).astype(jnp.int32)
    for slot in range(4):
        local = ((slot // 2) ^ parity) + 2 * (slot % 2)
        group = place ^ local
        values = lowrank_ref[group] + got_ref[group].astype(F32)
        values = jnp.concatenate([values, values], axis=0).T
        wanted = ids_ref[local] - upper
        for piece in range(8):
            spread[slot * rows : (slot + 1) * rows, piece * lanes : (piece + 1) * lanes] = (
                jnp.where(wanted == info_ref[2 + piece], values, 0.0).astype(BF16)
            )


def combine_kernel(build, info_ref, *refs):
    if build:
        lowrank_ref, got_ref, ids_ref, refs = refs[0], refs[1], refs[2], refs[3:]
        near_ref, far_ref, own_ref, core_ref, *blocks, keep_ref, send_ref, spread_ref, maps = refs

        @pl.when(pl.program_id(0) == 0)
        def _():
            build_spread(info_ref, lowrank_ref, got_ref, ids_ref, spread_ref)

    else:
        spread_ref, near_ref, far_ref, own_ref, core_ref, *blocks, keep_ref, send_ref, maps = refs
    parity = info_ref[0]
    rows = near_ref.shape[1]
    held = own_ref.shape[0]
    for index, ref in enumerate((own_ref, core_ref, *blocks)):
        maps[index * held : (index + 1) * held, :] = ref[...]
    delta = jnp.dot(spread_ref[...], maps[...], preferred_element_type=F32)
    for slot in range(4):
        source = near_ref if slot % 2 == 0 else far_ref
        value = source[(slot // 2) ^ parity] + delta[slot * rows : (slot + 1) * rows]
        if slot < 2:
            keep_ref[slot % 2] = value
        else:
            send_ref[slot % 2] = value.astype(BF16)


def combine(info, near, far, own_maps, core_maps, blocks, start, spread=None, build=()):
    rows = near.shape[1]
    width = far.shape[2]
    tile = 512
    first = start // tile
    per_place = core_maps.shape[1] // tile
    held = own_maps.shape[0]
    whole = lambda shape: pl.BlockSpec(shape, lambda n, s: (0,) * len(shape))
    ahead = list(build) if build else [spread]
    spread_shape = (4 * rows, 4 * held)
    in_specs = [whole(x.shape) for x in ahead]
    in_specs += [
        pl.BlockSpec((2, rows, tile), lambda n, s: (0, 0, first + n)),
        pl.BlockSpec((2, rows, tile), lambda n, s: (0, 0, n)),
        pl.BlockSpec((held, tile), lambda n, s: (0, s[1] * per_place + first + n)),
        pl.BlockSpec((held, tile), lambda n, s: (0, first + n)),
    ]
    in_specs += [
        pl.BlockSpec((held, tile), lambda n, s: (0, n)) for _ in blocks
    ]
    out_specs = [pl.BlockSpec((2, rows, tile), lambda n, s: (0, 0, n))] * 2
    out_shape = [jax.ShapeDtypeStruct((2, rows, width), kind) for kind in (F32, BF16)]
    if build:
        out_specs.append(whole(spread_shape))
        out_shape.append(jax.ShapeDtypeStruct(spread_shape, BF16))
    return pl.pallas_call(
        lambda *refs: combine_kernel(bool(build), *refs),
        grid_spec=pltpu.PrefetchScalarGridSpec(
            num_scalar_prefetch=1,
            grid=(width // tile,),
            in_specs=in_specs,
            out_specs=out_specs,
            scratch_shapes=[pltpu.VMEM((4 * held, tile), BF16)],
        ),
        out_shape=out_shape,
        compiler_params=params(),
        cost_estimate=cost(
            32 * rows * held * width, 26 * rows * width + 8 * held * width
        ),
        name="combine",
    )(info, *ahead, near, far, own_maps, core_maps, *blocks)


def per_device_fast(hidden, weight, input_maps, output_maps, slots, lists):
    rows, depth = hidden.shape
    place = lax.axis_index("pool")
    t = lax.axis_index("tensor")
    holding, rank = input_maps.shape[:2]
    held, features = output_maps.shape
    width = features // 4
    starts = [sum(WIDTHS[:i]) for i in range(len(WIDTHS))]
    count = len(WIDTHS)

    part = depth // HALVES
    near_b = swap(hidden, "pool", 1)
    *early, late = cut_columns(hidden, (part // 2, part // 2, part))
    first_a, first_b = (swap(block, "pool", 2) for block in early)


    def block_for(index, other, source):
        return lax.dynamic_slice(
            source, (0, (place ^ other) * width + starts[index]), (held, WIDTHS[index])
        )

    order = place ^ jnp.arange(4, dtype=jnp.int32)
    hot = order[:, None] == jnp.arange(4, dtype=jnp.int32)[None, :]
    slots_local = jnp.sum(jnp.where(hot[:, :, None], slots.reshape(1, 4, rows), 0), axis=1)
    lists_local = jnp.sum(jnp.where(hot[:, :, None], lists[None, :, :], 0), axis=1)
    positions = jnp.arange(lists.shape[1], dtype=jnp.int32)
    ids = jnp.sum(
        jnp.where(slots_local[:, :, None] == positions, lists_local[:, None, :], 0), axis=2
    )
    owned_ids = (ids - place * holding).reshape(4, 1, rows)
    owned = (lists_local >= place * holding) & (lists_local < (place + 1) * holding)
    earlier = positions[None, :] < positions[:, None]
    rank_in_list = jnp.sum(owned[:, None, :] & earlier[None], axis=2)
    caps = jnp.arange(CAP, dtype=jnp.int32)
    chosen = jnp.sum(
        jnp.where(
            owned[:, None, :] & (rank_in_list[:, None, :] == caps[None, :, None]),
            (lists_local - place * holding)[:, None, :],
            0,
        ),
        axis=2,
    ).reshape(4 * CAP)
    picks = jnp.concatenate([place.reshape(1), chosen]).astype(jnp.int32)

    parity = (place ^ t) & 1
    per_owner = held // rank
    half_step = per_owner // 2
    owner_first = [holding * (place ^ j) + per_owner * t for j in range(4)]
    info = jnp.stack(
        [parity, place]
        + [owner_first[j] + half_step * h for j in range(4) for h in range(2)]
    ).astype(jnp.int32)

    own_rows, near_b, picks, info, ids, owned_ids = lax.optimization_barrier(
        (hidden, near_b, picks, info, ids, owned_ids)
    )

    (near_lowrank,) = scores(picks, 0, [own_rows], [near_b], input_maps, 0, ids=owned_ids)
    second = swap(tie(late, near_lowrank), "pool", 2)
    near_late = product(
        [[(tie(own_rows, near_lowrank), part, 1)], [(near_b, part, 1)]],
        weight, 1, 0, width, 512,
    )

    first_a, first_b = lax.optimization_barrier((first_a, first_b, near_late))[:2]
    a0 = [first_a, first_b]
    b0 = [swap(x, "pool", 1) for x in a0]
    source, kept_ids, _ = lax.optimization_barrier((output_maps, ids, first_a))
    blocks = [block_for(index, other, source) for index in range(2) for other in (2, 3)]
    wide_ids = jnp.broadcast_to(kept_ids[:, :, None], (4, rows, 128))
    *b0, wide_ids, blocks[0], blocks[1], blocks[2], blocks[3] = lax.optimization_barrier(
        (*b0, wide_ids, *blocks)
    )
    (raw,) = scores(picks, 2, a0, b0, input_maps, 0)
    base = product(
        [
            [(tie(own_rows, raw), part, 0)],
            [(near_b, part, 0)],
            [(x, part // 2, 0) for x in a0],
            [(x, part // 2, 0) for x in b0],
        ],
        weight, 0, 0, width, 512, near_late,
    )
    a1 = tie(second, base)
    b1 = swap(a1, "pool", 1)
    core_block = lax.dynamic_slice(
        tie(output_maps, a1), (0, (place ^ 1) * width), (held, width)
    )
    b1, core_block = lax.optimization_barrier((b1, core_block))
    core_maps = swap(core_block, "pool", 1)
    total, sent = scores(
        picks, 2, [a1], [b1], input_maps, 1, prior=raw, near=near_lowrank, ids=owned_ids
    )

    def far_piece(index, after, hint=HINT):
        return product(
            [[(tie(a1, after), part, 0)], [(b1, part, 0)]],
            weight, 1, starts[index], WIDTHS[index], 256, base, 1, hint,
        ).reshape(2, rows, WIDTHS[index])

    got = [swap(sent, "pool", step) for step in (2, 3, 1)]
    pieces = [far_piece(0, sent, 1)]

    def start_maps(index, after):
        pair = later[2 * (index - 2) : 2 * (index - 2) + 2]
        return [swap(tie(x, after), "pool", 2 + k) for k, x in enumerate(pair)]

    moved = [[swap(blocks[0], "pool", 2), swap(tie(blocks[1], sent), "pool", 3)]]
    moved.append([swap(tie(blocks[k], sent), "pool", k) for k in (2, 3)])
    moved[0][0] = tie(moved[0][0], sent)
    got = lax.optimization_barrier((*got, moved[0][0], pieces[0]))[:3]
    total = total + sum(x.astype(F32) for x in got)
    sent = total.astype(BF16)
    got = swap(sent, "tensor", 1)
    pieces.append(far_piece(1, sent, 1))
    moved[0][1] = tie(moved[0][1], sent)
    got = lax.optimization_barrier((got, pieces[1], moved[0][1]))[0]
    total = total + got.astype(F32)
    sent = total.astype(BF16)
    got = swap(sent, "tensor", 2)
    source = tie(output_maps, sent)
    later = [block_for(index, other, source) for index in (2, 3) for other in (2, 3)]
    got, *later = lax.optimization_barrier((got, *later))
    moved.append(start_maps(2, sent))
    moved[1][0] = tie(moved[1][0], sent)
    got = lax.optimization_barrier((got, *moved[0], moved[1][0]))[0]

    near_base = base.reshape(4, rows, width)
    side = ((place ^ t) >> 1) & 1
    parts = []
    spread = send = None

    def maps_of(index, after):
        return moved[index] if after is None else [tie(x, after) for x in moved[index]]

    def pace(index):
        if index == 1:
            moved[2][0] = tie(moved[2][0], send)
            return tie(near_base, moved[2][0])
        if index == 3:
            return lax.optimization_barrier((near_base, started[1], parts[0]))[0]
        return near_base if index < 2 else tie(near_base, started[index - 2])

    started = []

    halves = []

    def finish(index, after):
        keep, got = halves[index]
        got = tie(got, after)
        if index == 2:
            got = tie(got, parts[1])
        pair = keep + got.astype(F32)
        sent = jnp.where(side == 0, pair[1], pair[0]).astype(BF16)
        kept = jnp.where(side == 0, pair[0], pair[1])
        started.append(sent)
        return kept + swap(sent, "tensor", 2).astype(F32)

    for chunk in range(count):
        common = (
            info, pace(chunk), pieces[chunk], output_maps, core_maps,
            maps_of(chunk, started[chunk - 2] if chunk > 1 else send), starts[chunk],
        )
        if chunk == 0:
            keep, send, spread = combine(*common, build=(total, got, wide_ids))
            moved.append(start_maps(3, send))
        else:
            keep, send = combine(*common, spread=spread)
        if chunk == 0:
            pieces.append(far_piece(2, send))
        halves.append((keep, swap(send, "tensor", 1)))
        if chunk > 0:
            parts.append(finish(chunk - 1, send))
        if chunk == 1:
            pieces.append(far_piece(3, started[0]))
    parts.append(finish(count - 1, started[-1]))
    return jnp.concatenate(parts, axis=1).astype(BF16)


def per_device_general(hidden, weight, input_maps, output_maps, slots, lists):
    rows, depth = hidden.shape
    pool_count = lax.axis_size("pool")
    tensor_count = lax.axis_size("tensor")
    place = lax.axis_index("pool")
    t = lax.axis_index("tensor")
    holding, rank = input_maps.shape[:2]
    held = output_maps.shape[0]
    total_rows = rows * pool_count
    slot_ids = jnp.arange(lists.shape[1], dtype=jnp.int32)
    slot_hot = slots.reshape(pool_count, rows)[:, :, None] == slot_ids
    ids = jnp.sum(jnp.where(slot_hot, lists[:, None, :], 0), axis=2).reshape(total_rows)
    gathered = lax.all_gather(hidden, "pool", axis=0, tiled=True)
    scored = lax.dot_general(
        gathered,
        input_maps.reshape(holding * rank, depth),
        (((1,), (1,)), ((), ())),
        preferred_element_type=F32,
    ).reshape(total_rows, holding, rank)
    owned = place * holding + jnp.arange(holding, dtype=jnp.int32)
    partial = jnp.sum(
        jnp.where((ids[:, None] == owned[None, :])[:, :, None], scored, 0.0), axis=1
    )
    lowrank = lax.psum(partial, ("tensor", "pool")).astype(BF16)
    maps = lax.all_to_all(output_maps, "pool", split_axis=1, concat_axis=0, tiled=True)
    columns = jnp.arange(pool_count * held, dtype=jnp.int32)
    source = (columns // held * tensor_count + t) * held + columns % held
    pick = (source[None, :] % rank == jnp.arange(rank, dtype=jnp.int32)[:, None]).astype(BF16)
    placed = jnp.dot(lowrank, pick, preferred_element_type=F32).astype(BF16)
    spread = jnp.where(ids[:, None] == source[None, :] // rank, placed, jnp.zeros_like(placed))
    value = jnp.dot(gathered, weight, preferred_element_type=F32)
    value = value + jnp.dot(spread, maps, preferred_element_type=F32)
    mixed = lax.psum_scatter(value, "tensor", scatter_dimension=0, tiled=True)
    return mixed.astype(BF16)


def solution(mesh):
    shape = dict(mesh.shape)
    fast = shape["groups"] == 2 and shape["pool"] == 4 and shape["tensor"] == 4
    placed = (
        P(("groups", "pool"), "tensor"),
        P("tensor", "pool"),
        P("pool", None, "tensor"),
        P(("pool", "tensor"), None),
        P("groups"),
        P("groups", None),
    )
    return jax.shard_map(
        per_device_fast if fast else per_device_general,
        mesh=mesh,
        in_specs=placed,
        out_specs=P(("groups", "tensor"), "pool"),
        check_vma=False,
    )
```

```python
import jax
import jax.numpy as jnp
from jax import lax
from jax.experimental import pallas as pl
from jax.experimental.pallas import tpu as pltpu
from jax.sharding import PartitionSpec as P

F32 = jnp.float32
BF16 = jnp.bfloat16
VMEM_LIMIT = 48 * 1024 * 1024
WIDTHS = (512, 512, 512, 512)
CAP = 4
HALVES = 2
HINT = 1000


def partners(count, step):
    return [(i, i ^ step) for i in range(count)]


def swap(values, axis, step):
    return lax.ppermute(values, axis, partners(lax.axis_size(axis), step))


def tie(values, *after):
    return lax.optimization_barrier((values, *after))[0]


def cost(flops, moved, hint=HINT):
    return pl.CostEstimate(flops=flops // hint, bytes_accessed=moved // hint, transcendentals=0)


def params():
    return pltpu.CompilerParams(vmem_limit_bytes=VMEM_LIMIT)


def cut_kernel(ref, *refs):
    outs, (stage, sems) = refs[:-2], refs[-2:]
    inward, outward, start = [], [], 0
    for index, out in enumerate(outs):
        spot = pl.ds(start, out.shape[1])
        inward.append(
            pltpu.make_async_copy(ref.at[:, spot], stage.at[:, spot], sems.at[0, index])
        )
        outward.append(pltpu.make_async_copy(stage.at[:, spot], out, sems.at[1, index]))
        start += out.shape[1]
    for copy in inward:
        copy.start()
    for copy, after in zip(inward, outward):
        copy.wait()
        after.start()
    for copy in outward:
        copy.wait()


def cut_columns(array, widths):
    return pl.pallas_call(
        cut_kernel,
        in_specs=[pl.BlockSpec(memory_space=pl.ANY)],
        out_specs=[pl.BlockSpec(memory_space=pl.ANY)] * len(widths),
        out_shape=[jax.ShapeDtypeStruct((array.shape[0], w), array.dtype) for w in widths],
        scratch_shapes=[
            pltpu.VMEM(array.shape, array.dtype),
            pltpu.SemaphoreType.DMA((2, len(widths))),
        ],
        compiler_params=params(),
        cost_estimate=cost(0, 4 * array.size),
        name="cut",
    )(array)


def product_kernel(counts, has_prior, *refs):
    pieces, refs = refs[: sum(counts)], refs[sum(counts) :]
    if has_prior:
        prior_ref, refs = refs[0], refs[1:]
    w_ref, out_ref, rows = refs

    @pl.when(pl.program_id(0) == 0)
    def _():
        height = rows.shape[0] // len(counts)
        spot = 0
        for group, count in enumerate(counts):
            start = 0
            for piece in pieces[spot : spot + count]:
                wide = piece.shape[1]
                rows[group * height : (group + 1) * height, start : start + wide] = piece[...]
                start += wide
            spot += count

    value = jnp.dot(rows[...], w_ref[...], preferred_element_type=F32)
    if has_prior:
        top = prior_ref.shape[0]
        out_ref[:top, :] = value[:top] + prior_ref[...]
        if top < value.shape[0]:
            out_ref[top:, :] = value[top:]
    else:
        out_ref[...] = value


def product(groups, weight, depth_block, first, width, tile, prior=None, prior_block=0, hint=HINT):
    rows = groups[0][0][0].shape[0]
    depth = sum(wide for _, wide, _ in groups[0])
    total = rows * len(groups)
    in_specs, args = [], []
    for group in groups:
        for array, wide, block in group:
            in_specs.append(pl.BlockSpec((rows, wide), lambda n, block=block: (0, block)))
            args.append(array)
    if prior is not None:
        in_specs.append(
            pl.BlockSpec((2 * rows, tile), lambda n: (prior_block, first // tile + n))
        )
        args.append(prior)
    in_specs.append(pl.BlockSpec((depth, tile), lambda n: (depth_block, first // tile + n)))
    args.append(weight)
    counts = [len(group) for group in groups]
    return pl.pallas_call(
        lambda *refs: product_kernel(counts, prior is not None, *refs),
        grid=(width // tile,),
        in_specs=in_specs,
        out_specs=pl.BlockSpec((total, tile), lambda n: (0, n)),
        out_shape=jax.ShapeDtypeStruct((total, width), F32),
        scratch_shapes=[pltpu.VMEM((total, depth), BF16)],
        compiler_params=params(),
        cost_estimate=cost(
            2 * total * depth * width, 2 * depth * (width + total) + 8 * total * width, hint
        ),
        name="base",
    )(*args)


def scores_kernel(first, offset, count, has_prior, last, info_ref, *refs):
    groups, maps_ref, refs = (refs[:count], refs[count : 2 * count]), refs[2 * count], refs[2 * count + 1 :]
    if has_prior:
        prior_ref, refs = refs[0], refs[1:]
    if first == 2 and last:
        near_ref, refs = refs[0], refs[1:]
    if last:
        ids_ref, refs = refs[0], refs[1:]
    outs, (rows, maps, row_sems, map_sems) = refs[:-4], refs[-4:]
    depth = rows.shape[2]
    cut = depth // 2

    def map_copy(pair, k, part):
        chosen = info_ref[1 + (first + pair) * CAP + k]
        return pltpu.make_async_copy(
            maps_ref.at[chosen, :, pl.ds(offset + part * cut, cut)],
            maps.at[pair * CAP + k, :, pl.ds(part * cut, cut)],
            map_sems.at[pair, k, part],
        )

    row_copies = []
    for pair, pieces in enumerate(groups):
        start = 0
        for index, piece in enumerate(pieces):
            row_copies.append(
                pltpu.make_async_copy(
                    piece,
                    rows.at[pair, :, pl.ds(start, piece.shape[1])],
                    row_sems.at[pair * count + index],
                )
            )
            start += piece.shape[1]
    for pair in range(2):
        for copy in row_copies[pair * count : (pair + 1) * count]:
            copy.start()
        for part in range(2):
            for k in range(CAP):
                map_copy(pair, k, part).start()
    for pair in range(2):
        for copy in row_copies[pair * count : (pair + 1) * count]:
            copy.wait()
        total = prior_ref[pair] if has_prior else None
        for part in range(2):
            for k in range(CAP):
                map_copy(pair, k, part).wait()
            columns = slice(part * cut, (part + 1) * cut)
            chosen = maps[pair * CAP : (pair + 1) * CAP, :, columns]
            term = lax.dot_general(
                chosen.reshape(-1, cut),
                rows[pair, :, columns],
                (((1,), (1,)), ((), ())),
                preferred_element_type=F32,
            )
            total = term if total is None else total + term
        if not last:
            outs[0][pair] = total
            continue
        wanted = ids_ref[pair]
        rank = total.shape[0] // CAP
        found = jnp.zeros((rank, total.shape[1]), F32)
        for k in range(CAP):
            mine = info_ref[1 + (first + pair) * CAP + k]
            found += jnp.where(wanted == mine, total[k * rank : (k + 1) * rank], 0.0)
        if first == 0:
            outs[0][pair] = found
        else:
            near_group = info_ref[0] ^ pair
            far_group = near_group ^ 2
            outs[0][far_group] = found
            outs[1][far_group] = found.astype(BF16)
            outs[0][near_group] = near_ref[pair]
            outs[1][near_group] = near_ref[pair].astype(BF16)


def scores(info, first, lower, upper, maps, half, prior=None, near=None, ids=None):
    rows, depth = lower[0].shape[0], sum(x.shape[1] for x in lower)
    rank = maps.shape[1]
    has_prior, last = prior is not None, ids is not None
    args_rows = [*lower, *upper]
    whole = lambda x: pl.BlockSpec(x.shape, lambda k, s: (0,) * x.ndim)
    args = [*lower, *upper, maps]
    in_specs = [pl.BlockSpec(memory_space=pl.ANY)] * len(args)
    if has_prior:
        in_specs.append(whole(prior))
        args.append(prior)
    if near is not None:
        in_specs.append(whole(near))
        args.append(near)
    if last:
        in_specs.append(
            pl.BlockSpec((2,) + ids.shape[1:], lambda k, s: (first // 2, 0, 0))
        )
        args.append(ids)
    if not last:
        out_shape = [jax.ShapeDtypeStruct((2, CAP * rank, rows), F32)]
    elif first == 0:
        out_shape = [jax.ShapeDtypeStruct((2, rank, rows), F32)]
    else:
        out_shape = [jax.ShapeDtypeStruct((4, rank, rows), kind) for kind in (F32, BF16)]
    return pl.pallas_call(
        lambda *refs: scores_kernel(first, half * depth, len(lower), has_prior, last, *refs),
        grid_spec=pltpu.PrefetchScalarGridSpec(
            num_scalar_prefetch=1,
            grid=(1,),
            in_specs=in_specs,
            out_specs=[whole(x) for x in out_shape],
            scratch_shapes=[
                pltpu.VMEM((2, rows, depth), BF16),
                pltpu.VMEM((2 * CAP, rank, depth), BF16),
                pltpu.SemaphoreType.DMA((len(args_rows),)),
                pltpu.SemaphoreType.DMA((2, CAP, 2)),
            ],
        ),
        out_shape=out_shape,
        compiler_params=params(),
        cost_estimate=cost(4 * rows * depth * CAP * rank, 4 * depth * (CAP * rank + rows)),
        name="scores",
    )(info, *args)


def build_spread(info_ref, lowrank_ref, got_ref, ids_ref, spread):
    rows, lanes = ids_ref.shape[1], ids_ref.shape[2]
    parity, place = info_ref[0], info_ref[1]
    upper = (lax.broadcasted_iota(jnp.int32, (rows, lanes), 1) >= lanes // 2).astype(jnp.int32)
    for slot in range(4):
        local = ((slot // 2) ^ parity) + 2 * (slot % 2)
        group = place ^ local
        values = lowrank_ref[group] + got_ref[group].astype(F32)
        values = jnp.concatenate([values, values], axis=0).T
        wanted = ids_ref[local] - upper
        for piece in range(8):
            spread[slot * rows : (slot + 1) * rows, piece * lanes : (piece + 1) * lanes] = (
                jnp.where(wanted == info_ref[2 + piece], values, 0.0).astype(BF16)
            )


def combine_kernel(build, info_ref, *refs):
    if build:
        lowrank_ref, got_ref, ids_ref, refs = refs[0], refs[1], refs[2], refs[3:]
        near_ref, far_ref, own_ref, core_ref, *blocks, keep_ref, send_ref, spread_ref, maps = refs

        @pl.when(pl.program_id(0) == 0)
        def _():
            build_spread(info_ref, lowrank_ref, got_ref, ids_ref, spread_ref)

    else:
        spread_ref, near_ref, far_ref, own_ref, core_ref, *blocks, keep_ref, send_ref, maps = refs
    parity = info_ref[0]
    rows = near_ref.shape[1]
    held = own_ref.shape[0]
    for index, ref in enumerate((own_ref, core_ref, *blocks)):
        maps[index * held : (index + 1) * held, :] = ref[...]
    delta = jnp.dot(spread_ref[...], maps[...], preferred_element_type=F32)
    for slot in range(4):
        source = near_ref if slot % 2 == 0 else far_ref
        value = source[(slot // 2) ^ parity] + delta[slot * rows : (slot + 1) * rows]
        if slot < 2:
            keep_ref[slot % 2] = value
        else:
            send_ref[slot % 2] = value.astype(BF16)


def combine(info, near, far, own_maps, core_maps, blocks, start, spread=None, build=()):
    rows = near.shape[1]
    width = far.shape[2]
    tile = 512
    first = start // tile
    per_place = core_maps.shape[1] // tile
    held = own_maps.shape[0]
    whole = lambda shape: pl.BlockSpec(shape, lambda n, s: (0,) * len(shape))
    ahead = list(build) if build else [spread]
    spread_shape = (4 * rows, 4 * held)
    in_specs = [whole(x.shape) for x in ahead]
    in_specs += [
        pl.BlockSpec((2, rows, tile), lambda n, s: (0, 0, first + n)),
        pl.BlockSpec((2, rows, tile), lambda n, s: (0, 0, n)),
        pl.BlockSpec((held, tile), lambda n, s: (0, s[1] * per_place + first + n)),
        pl.BlockSpec((held, tile), lambda n, s: (0, first + n)),
    ]
    in_specs += [
        pl.BlockSpec((held, tile), lambda n, s: (0, n)) for _ in blocks
    ]
    out_specs = [pl.BlockSpec((2, rows, tile), lambda n, s: (0, 0, n))] * 2
    out_shape = [jax.ShapeDtypeStruct((2, rows, width), kind) for kind in (F32, BF16)]
    if build:
        out_specs.append(whole(spread_shape))
        out_shape.append(jax.ShapeDtypeStruct(spread_shape, BF16))
    return pl.pallas_call(
        lambda *refs: combine_kernel(bool(build), *refs),
        grid_spec=pltpu.PrefetchScalarGridSpec(
            num_scalar_prefetch=1,
            grid=(width // tile,),
            in_specs=in_specs,
            out_specs=out_specs,
            scratch_shapes=[pltpu.VMEM((4 * held, tile), BF16)],
        ),
        out_shape=out_shape,
        compiler_params=params(),
        cost_estimate=cost(
            32 * rows * held * width, 26 * rows * width + 8 * held * width
        ),
        name="combine",
    )(info, *ahead, near, far, own_maps, core_maps, *blocks)


def per_device_fast(hidden, weight, input_maps, output_maps, slots, lists):
    rows, depth = hidden.shape
    place = lax.axis_index("pool")
    t = lax.axis_index("tensor")
    holding, rank = input_maps.shape[:2]
    held, features = output_maps.shape
    width = features // 4
    starts = [sum(WIDTHS[:i]) for i in range(len(WIDTHS))]
    count = len(WIDTHS)

    part = depth // HALVES
    near_b = swap(hidden, "pool", 1)
    *early, late = cut_columns(hidden, (part // 2, part // 2, part))
    first_a, first_b = (swap(block, "pool", 2) for block in early)


    def block_for(index, other, source):
        return lax.dynamic_slice(
            source, (0, (place ^ other) * width + starts[index]), (held, WIDTHS[index])
        )

    order = place ^ jnp.arange(4, dtype=jnp.int32)
    hot = order[:, None] == jnp.arange(4, dtype=jnp.int32)[None, :]
    slots_local = jnp.sum(jnp.where(hot[:, :, None], slots.reshape(1, 4, rows), 0), axis=1)
    lists_local = jnp.sum(jnp.where(hot[:, :, None], lists[None, :, :], 0), axis=1)
    positions = jnp.arange(lists.shape[1], dtype=jnp.int32)
    ids = jnp.sum(
        jnp.where(slots_local[:, :, None] == positions, lists_local[:, None, :], 0), axis=2
    )
    owned_ids = (ids - place * holding).reshape(4, 1, rows)
    owned = (lists_local >= place * holding) & (lists_local < (place + 1) * holding)
    earlier = positions[None, :] < positions[:, None]
    rank_in_list = jnp.sum(owned[:, None, :] & earlier[None], axis=2)
    caps = jnp.arange(CAP, dtype=jnp.int32)
    chosen = jnp.sum(
        jnp.where(
            owned[:, None, :] & (rank_in_list[:, None, :] == caps[None, :, None]),
            (lists_local - place * holding)[:, None, :],
            0,
        ),
        axis=2,
    ).reshape(4 * CAP)
    picks = jnp.concatenate([place.reshape(1), chosen]).astype(jnp.int32)

    parity = (place ^ t) & 1
    per_owner = held // rank
    half_step = per_owner // 2
    owner_first = [holding * (place ^ j) + per_owner * t for j in range(4)]
    info = jnp.stack(
        [parity, place]
        + [owner_first[j] + half_step * h for j in range(4) for h in range(2)]
    ).astype(jnp.int32)

    own_rows, near_b, picks, info, ids, owned_ids = lax.optimization_barrier(
        (hidden, near_b, picks, info, ids, owned_ids)
    )

    (near_lowrank,) = scores(picks, 0, [own_rows], [near_b], input_maps, 0, ids=owned_ids)
    second = swap(tie(late, near_lowrank), "pool", 2)
    near_late = product(
        [[(tie(own_rows, near_lowrank), part, 1)], [(near_b, part, 1)]],
        weight, 1, 0, width, 512,
    )

    first_a, first_b = lax.optimization_barrier((first_a, first_b, near_late))[:2]
    a0 = [first_a, first_b]
    b0 = [swap(x, "pool", 1) for x in a0]
    source, kept_ids, _ = lax.optimization_barrier((output_maps, ids, first_a))
    blocks = [block_for(index, other, source) for index in range(2) for other in (2, 3)]
    wide_ids = jnp.broadcast_to(kept_ids[:, :, None], (4, rows, 128))
    *b0, wide_ids, blocks[0], blocks[1], blocks[2], blocks[3] = lax.optimization_barrier(
        (*b0, wide_ids, *blocks)
    )
    (raw,) = scores(picks, 2, a0, b0, input_maps, 0)
    base = product(
        [
            [(tie(own_rows, raw), part, 0)],
            [(near_b, part, 0)],
            [(x, part // 2, 0) for x in a0],
            [(x, part // 2, 0) for x in b0],
        ],
        weight, 0, 0, width, 512, near_late,
    )
    a1 = tie(second, base)
    b1 = swap(a1, "pool", 1)
    core_block = lax.dynamic_slice(
        tie(output_maps, a1), (0, (place ^ 1) * width), (held, width)
    )
    b1, core_block = lax.optimization_barrier((b1, core_block))
    core_maps = swap(core_block, "pool", 1)
    total, sent = scores(
        picks, 2, [a1], [b1], input_maps, 1, prior=raw, near=near_lowrank, ids=owned_ids
    )

    def far_piece(index, after, hint=HINT):
        return product(
            [[(tie(a1, after), part, 0)], [(b1, part, 0)]],
            weight, 1, starts[index], WIDTHS[index], 256, base, 1, hint,
        ).reshape(2, rows, WIDTHS[index])

    got = [swap(sent, "pool", step) for step in (2, 3, 1)]
    pieces = [far_piece(0, sent, 1)]

    def start_maps(index, after):
        pair = later[2 * (index - 2) : 2 * (index - 2) + 2]
        return [swap(tie(x, after), "pool", 2 + k) for k, x in enumerate(pair)]

    moved = [[swap(blocks[0], "pool", 2), swap(tie(blocks[1], sent), "pool", 3)]]
    moved.append([swap(tie(blocks[k], sent), "pool", k) for k in (2, 3)])
    moved[0][0] = tie(moved[0][0], sent)
    got = lax.optimization_barrier((*got, moved[0][0], pieces[0]))[:3]
    total = total + sum(x.astype(F32) for x in got)
    sent = total.astype(BF16)
    got = swap(sent, "tensor", 1)
    pieces.append(far_piece(1, sent, 1))
    moved[0][1] = tie(moved[0][1], sent)
    got = lax.optimization_barrier((got, pieces[1], moved[0][1]))[0]
    total = total + got.astype(F32)
    sent = total.astype(BF16)
    got = swap(sent, "tensor", 2)
    source = tie(output_maps, sent)
    later = [block_for(index, other, source) for index in (2, 3) for other in (2, 3)]
    got, *later = lax.optimization_barrier((got, *later))
    moved.append(start_maps(2, sent))
    moved[1][0] = tie(moved[1][0], sent)
    got = lax.optimization_barrier((got, *moved[0], moved[1][0]))[0]

    near_base = base.reshape(4, rows, width)
    side = ((place ^ t) >> 1) & 1
    parts = []
    spread = send = None

    def maps_of(index, after):
        return moved[index] if after is None else [tie(x, after) for x in moved[index]]

    def pace(index):
        if index == 3:
            return lax.optimization_barrier((near_base, started[1], parts[0]))[0]
        return near_base if index < 2 else tie(near_base, started[index - 2])

    started = []

    halves = []

    def finish(index, after):
        keep, got = halves[index]
        got = tie(got, after)
        if index == 2:
            got = tie(got, parts[1])
        pair = keep + got.astype(F32)
        sent = jnp.where(side == 0, pair[1], pair[0]).astype(BF16)
        kept = jnp.where(side == 0, pair[0], pair[1])
        started.append(sent)
        return kept + swap(sent, "tensor", 2).astype(F32)

    for chunk in range(count):
        common = (
            info, pace(chunk), pieces[chunk], output_maps, core_maps,
            maps_of(chunk, started[chunk - 2] if chunk > 1 else send), starts[chunk],
        )
        if chunk == 0:
            keep, send, spread = combine(*common, build=(total, got, wide_ids))
            moved.append(start_maps(3, send))
        else:
            keep, send = combine(*common, spread=spread)
        if chunk == 0:
            pieces.append(far_piece(2, send))
        halves.append((keep, swap(send, "tensor", 1)))
        if chunk > 0:
            parts.append(finish(chunk - 1, send))
        if chunk == 1:
            pieces.append(far_piece(3, started[0]))
    parts.append(finish(count - 1, started[-1]))
    return jnp.concatenate(parts, axis=1).astype(BF16)


def per_device_general(hidden, weight, input_maps, output_maps, slots, lists):
    rows, depth = hidden.shape
    pool_count = lax.axis_size("pool")
    tensor_count = lax.axis_size("tensor")
    place = lax.axis_index("pool")
    t = lax.axis_index("tensor")
    holding, rank = input_maps.shape[:2]
    held = output_maps.shape[0]
    total_rows = rows * pool_count
    slot_ids = jnp.arange(lists.shape[1], dtype=jnp.int32)
    slot_hot = slots.reshape(pool_count, rows)[:, :, None] == slot_ids
    ids = jnp.sum(jnp.where(slot_hot, lists[:, None, :], 0), axis=2).reshape(total_rows)
    gathered = lax.all_gather(hidden, "pool", axis=0, tiled=True)
    scored = lax.dot_general(
        gathered,
        input_maps.reshape(holding * rank, depth),
        (((1,), (1,)), ((), ())),
        preferred_element_type=F32,
    ).reshape(total_rows, holding, rank)
    owned = place * holding + jnp.arange(holding, dtype=jnp.int32)
    partial = jnp.sum(
        jnp.where((ids[:, None] == owned[None, :])[:, :, None], scored, 0.0), axis=1
    )
    lowrank = lax.psum(partial, ("tensor", "pool")).astype(BF16)
    maps = lax.all_to_all(output_maps, "pool", split_axis=1, concat_axis=0, tiled=True)
    columns = jnp.arange(pool_count * held, dtype=jnp.int32)
    source = (columns // held * tensor_count + t) * held + columns % held
    pick = (source[None, :] % rank == jnp.arange(rank, dtype=jnp.int32)[:, None]).astype(BF16)
    placed = jnp.dot(lowrank, pick, preferred_element_type=F32).astype(BF16)
    spread = jnp.where(ids[:, None] == source[None, :] // rank, placed, jnp.zeros_like(placed))
    value = jnp.dot(gathered, weight, preferred_element_type=F32)
    value = value + jnp.dot(spread, maps, preferred_element_type=F32)
    mixed = lax.psum_scatter(value, "tensor", scatter_dimension=0, tiled=True)
    return mixed.astype(BF16)


def solution(mesh):
    shape = dict(mesh.shape)
    fast = shape["groups"] == 2 and shape["pool"] == 4 and shape["tensor"] == 4
    placed = (
        P(("groups", "pool"), "tensor"),
        P("tensor", "pool"),
        P("pool", None, "tensor"),
        P(("pool", "tensor"), None),
        P("groups"),
        P("groups", None),
    )
    return jax.shard_map(
        per_device_fast if fast else per_device_general,
        mesh=mesh,
        in_specs=placed,
        out_specs=P(("groups", "tensor"), "pool"),
        check_vma=False,
    )
```

```python
import jax
import jax.numpy as jnp
from jax import lax
from jax.experimental import pallas as pl
from jax.experimental.pallas import tpu as pltpu
from jax.sharding import PartitionSpec as P

F32 = jnp.float32
BF16 = jnp.bfloat16
VMEM_LIMIT = 52 * 1024 * 1024
WIDTHS = (512, 512, 512, 512)
CAP = 4
HALVES = 2
HINT = 1000


def partners(count, step):
    return [(i, i ^ step) for i in range(count)]


def swap(values, axis, step):
    return lax.ppermute(values, axis, partners(lax.axis_size(axis), step))


def tie(values, *after):
    return lax.optimization_barrier((values, *after))[0]


def cost(flops, moved, hint=HINT):
    return pl.CostEstimate(flops=flops // hint, bytes_accessed=moved // hint, transcendentals=0)


def params():
    return pltpu.CompilerParams(vmem_limit_bytes=VMEM_LIMIT)


def cut_kernel(ref, *refs):
    outs, (stage, sems) = refs[:-2], refs[-2:]
    inward, outward, start = [], [], 0
    for index, out in enumerate(outs):
        spot = pl.ds(start, out.shape[1])
        inward.append(
            pltpu.make_async_copy(ref.at[:, spot], stage.at[:, spot], sems.at[0, index])
        )
        outward.append(pltpu.make_async_copy(stage.at[:, spot], out, sems.at[1, index]))
        start += out.shape[1]
    for copy in inward:
        copy.start()
    for copy, after in zip(inward, outward):
        copy.wait()
        after.start()
    for copy in outward:
        copy.wait()


def cut_columns(array, widths):
    return pl.pallas_call(
        cut_kernel,
        in_specs=[pl.BlockSpec(memory_space=pl.ANY)],
        out_specs=[pl.BlockSpec(memory_space=pl.ANY)] * len(widths),
        out_shape=[jax.ShapeDtypeStruct((array.shape[0], w), array.dtype) for w in widths],
        scratch_shapes=[
            pltpu.VMEM(array.shape, array.dtype),
            pltpu.SemaphoreType.DMA((2, len(widths))),
        ],
        compiler_params=params(),
        cost_estimate=cost(0, 4 * array.size),
        name="cut",
    )(array)


def product_kernel(counts, has_prior, *refs):
    pieces, refs = refs[: sum(counts)], refs[sum(counts) :]
    if has_prior:
        prior_ref, refs = refs[0], refs[1:]
    w_ref, out_ref, rows = refs

    @pl.when(pl.program_id(0) == 0)
    def _():
        height = rows.shape[0] // len(counts)
        spot = 0
        for group, count in enumerate(counts):
            start = 0
            for piece in pieces[spot : spot + count]:
                wide = piece.shape[1]
                rows[group * height : (group + 1) * height, start : start + wide] = piece[...]
                start += wide
            spot += count

    value = jnp.dot(rows[...], w_ref[...], preferred_element_type=F32)
    if has_prior:
        top = prior_ref.shape[0]
        out_ref[:top, :] = value[:top] + prior_ref[...]
        if top < value.shape[0]:
            out_ref[top:, :] = value[top:]
    else:
        out_ref[...] = value


def product(groups, weight, depth_block, first, width, tile, prior=None, prior_block=0, hint=HINT):
    rows = groups[0][0][0].shape[0]
    depth = sum(wide for _, wide, _ in groups[0])
    total = rows * len(groups)
    in_specs, args = [], []
    for group in groups:
        for array, wide, block in group:
            in_specs.append(pl.BlockSpec((rows, wide), lambda n, block=block: (0, block)))
            args.append(array)
    if prior is not None:
        in_specs.append(
            pl.BlockSpec((2 * rows, tile), lambda n: (prior_block, first // tile + n))
        )
        args.append(prior)
    in_specs.append(pl.BlockSpec((depth, tile), lambda n: (depth_block, first // tile + n)))
    args.append(weight)
    counts = [len(group) for group in groups]
    return pl.pallas_call(
        lambda *refs: product_kernel(counts, prior is not None, *refs),
        grid=(width // tile,),
        in_specs=in_specs,
        out_specs=pl.BlockSpec((total, tile), lambda n: (0, n)),
        out_shape=jax.ShapeDtypeStruct((total, width), F32),
        scratch_shapes=[pltpu.VMEM((total, depth), BF16)],
        compiler_params=params(),
        cost_estimate=cost(
            2 * total * depth * width, 2 * depth * (width + total) + 8 * total * width, hint
        ),
        name="base",
    )(*args)


def scores_kernel(first, offset, count, has_prior, last, info_ref, *refs):
    groups, maps_ref, refs = (refs[:count], refs[count : 2 * count]), refs[2 * count], refs[2 * count + 1 :]
    if has_prior:
        prior_ref, refs = refs[0], refs[1:]
    if first == 2 and last:
        near_ref, refs = refs[0], refs[1:]
    if last:
        ids_ref, refs = refs[0], refs[1:]
    outs, (rows, maps, row_sems, map_sems) = refs[:-4], refs[-4:]
    depth = rows.shape[2]
    cut = depth // 2

    def map_copy(pair, k, part):
        chosen = info_ref[1 + (first + pair) * CAP + k]
        return pltpu.make_async_copy(
            maps_ref.at[chosen, :, pl.ds(offset + part * cut, cut)],
            maps.at[pair * CAP + k, :, pl.ds(part * cut, cut)],
            map_sems.at[pair, k, part],
        )

    row_copies = []
    for pair, pieces in enumerate(groups):
        start = 0
        for index, piece in enumerate(pieces):
            row_copies.append(
                pltpu.make_async_copy(
                    piece,
                    rows.at[pair, :, pl.ds(start, piece.shape[1])],
                    row_sems.at[pair * count + index],
                )
            )
            start += piece.shape[1]
    for pair in range(2):
        for copy in row_copies[pair * count : (pair + 1) * count]:
            copy.start()
        for part in range(2):
            for k in range(CAP):
                map_copy(pair, k, part).start()
    for pair in range(2):
        for copy in row_copies[pair * count : (pair + 1) * count]:
            copy.wait()
        total = prior_ref[pair] if has_prior else None
        for part in range(2):
            for k in range(CAP):
                map_copy(pair, k, part).wait()
            columns = slice(part * cut, (part + 1) * cut)
            chosen = maps[pair * CAP : (pair + 1) * CAP, :, columns]
            term = lax.dot_general(
                chosen.reshape(-1, cut),
                rows[pair, :, columns],
                (((1,), (1,)), ((), ())),
                preferred_element_type=F32,
            )
            total = term if total is None else total + term
        if not last:
            outs[0][pair] = total
            continue
        wanted = ids_ref[pair]
        rank = total.shape[0] // CAP
        found = jnp.zeros((rank, total.shape[1]), F32)
        for k in range(CAP):
            mine = info_ref[1 + (first + pair) * CAP + k]
            found += jnp.where(wanted == mine, total[k * rank : (k + 1) * rank], 0.0)
        if first == 0:
            outs[0][pair] = found
        else:
            near_group = info_ref[0] ^ pair
            far_group = near_group ^ 2
            outs[0][far_group] = found
            outs[1][far_group] = found.astype(BF16)
            outs[0][near_group] = near_ref[pair]
            outs[1][near_group] = near_ref[pair].astype(BF16)


def scores(info, first, lower, upper, maps, half, prior=None, near=None, ids=None):
    rows, depth = lower[0].shape[0], sum(x.shape[1] for x in lower)
    rank = maps.shape[1]
    has_prior, last = prior is not None, ids is not None
    args_rows = [*lower, *upper]
    whole = lambda x: pl.BlockSpec(x.shape, lambda k, s: (0,) * x.ndim)
    args = [*lower, *upper, maps]
    in_specs = [pl.BlockSpec(memory_space=pl.ANY)] * len(args)
    if has_prior:
        in_specs.append(whole(prior))
        args.append(prior)
    if near is not None:
        in_specs.append(whole(near))
        args.append(near)
    if last:
        in_specs.append(
            pl.BlockSpec((2,) + ids.shape[1:], lambda k, s: (first // 2, 0, 0))
        )
        args.append(ids)
    if not last:
        out_shape = [jax.ShapeDtypeStruct((2, CAP * rank, rows), F32)]
    elif first == 0:
        out_shape = [jax.ShapeDtypeStruct((2, rank, rows), F32)]
    else:
        out_shape = [jax.ShapeDtypeStruct((4, rank, rows), kind) for kind in (F32, BF16)]
    return pl.pallas_call(
        lambda *refs: scores_kernel(first, half * depth, len(lower), has_prior, last, *refs),
        grid_spec=pltpu.PrefetchScalarGridSpec(
            num_scalar_prefetch=1,
            grid=(1,),
            in_specs=in_specs,
            out_specs=[whole(x) for x in out_shape],
            scratch_shapes=[
                pltpu.VMEM((2, rows, depth), BF16),
                pltpu.VMEM((2 * CAP, rank, depth), BF16),
                pltpu.SemaphoreType.DMA((len(args_rows),)),
                pltpu.SemaphoreType.DMA((2, CAP, 2)),
            ],
        ),
        out_shape=out_shape,
        compiler_params=params(),
        cost_estimate=cost(4 * rows * depth * CAP * rank, 4 * depth * (CAP * rank + rows)),
        name="scores",
    )(info, *args)


def build_spread(info_ref, lowrank_ref, got_ref, ids_ref, spread):
    rows, lanes = ids_ref.shape[1], ids_ref.shape[2]
    parity, place = info_ref[0], info_ref[1]
    upper = (lax.broadcasted_iota(jnp.int32, (rows, lanes), 1) >= lanes // 2).astype(jnp.int32)
    for slot in range(4):
        local = ((slot // 2) ^ parity) + 2 * (slot % 2)
        group = place ^ local
        values = lowrank_ref[group] + got_ref[group].astype(F32)
        values = jnp.concatenate([values, values], axis=0).T
        wanted = ids_ref[local] - upper
        for piece in range(8):
            spread[slot * rows : (slot + 1) * rows, piece * lanes : (piece + 1) * lanes] = (
                jnp.where(wanted == info_ref[2 + piece], values, 0.0).astype(BF16)
            )


def combine_kernel(build, info_ref, *refs):
    if build:
        lowrank_ref, got_ref, ids_ref, refs = refs[0], refs[1], refs[2], refs[3:]
        near_ref, far_ref, own_ref, core_ref, *blocks, keep_ref, send_ref, spread_ref, maps = refs

        @pl.when(pl.program_id(0) == 0)
        def _():
            build_spread(info_ref, lowrank_ref, got_ref, ids_ref, spread_ref)

    else:
        spread_ref, near_ref, far_ref, own_ref, core_ref, *blocks, keep_ref, send_ref, maps = refs
    parity = info_ref[0]
    rows = near_ref.shape[1]
    held = own_ref.shape[0]
    for index, ref in enumerate((own_ref, core_ref, *blocks)):
        maps[index * held : (index + 1) * held, :] = ref[...]
    delta = jnp.dot(spread_ref[...], maps[...], preferred_element_type=F32)
    for slot in range(4):
        source = near_ref if slot % 2 == 0 else far_ref
        value = source[(slot // 2) ^ parity] + delta[slot * rows : (slot + 1) * rows]
        if slot < 2:
            keep_ref[slot % 2] = value
        else:
            send_ref[slot % 2] = value.astype(BF16)


def combine(info, near, far, own_maps, core_maps, blocks, start, spread=None, build=()):
    rows = near.shape[1]
    width = far.shape[2]
    tile = 512
    first = start // tile
    per_place = core_maps.shape[1] // tile
    held = own_maps.shape[0]
    whole = lambda shape: pl.BlockSpec(shape, lambda n, s: (0,) * len(shape))
    ahead = list(build) if build else [spread]
    spread_shape = (4 * rows, 4 * held)
    in_specs = [whole(x.shape) for x in ahead]
    in_specs += [
        pl.BlockSpec((2, rows, tile), lambda n, s: (0, 0, first + n)),
        pl.BlockSpec((2, rows, tile), lambda n, s: (0, 0, n)),
        pl.BlockSpec((held, tile), lambda n, s: (0, s[1] * per_place + first + n)),
        pl.BlockSpec((held, tile), lambda n, s: (0, first + n)),
    ]
    in_specs += [
        pl.BlockSpec((held, tile), lambda n, s: (0, n)) for _ in blocks
    ]
    out_specs = [pl.BlockSpec((2, rows, tile), lambda n, s: (0, 0, n))] * 2
    out_shape = [jax.ShapeDtypeStruct((2, rows, width), kind) for kind in (F32, BF16)]
    if build:
        out_specs.append(whole(spread_shape))
        out_shape.append(jax.ShapeDtypeStruct(spread_shape, BF16))
    return pl.pallas_call(
        lambda *refs: combine_kernel(bool(build), *refs),
        grid_spec=pltpu.PrefetchScalarGridSpec(
            num_scalar_prefetch=1,
            grid=(width // tile,),
            in_specs=in_specs,
            out_specs=out_specs,
            scratch_shapes=[pltpu.VMEM((4 * held, tile), BF16)],
        ),
        out_shape=out_shape,
        compiler_params=params(),
        cost_estimate=cost(
            32 * rows * held * width, 26 * rows * width + 8 * held * width
        ),
        name="combine",
    )(info, *ahead, near, far, own_maps, core_maps, *blocks)


def per_device_fast(hidden, weight, input_maps, output_maps, slots, lists):
    rows, depth = hidden.shape
    place = lax.axis_index("pool")
    t = lax.axis_index("tensor")
    holding, rank = input_maps.shape[:2]
    held, features = output_maps.shape
    width = features // 4
    starts = [sum(WIDTHS[:i]) for i in range(len(WIDTHS))]
    count = len(WIDTHS)

    part = depth // HALVES
    near_b = swap(hidden, "pool", 1)
    *early, late = cut_columns(hidden, (part // 2, part // 2, part))
    first_a, first_b = (swap(block, "pool", 2) for block in early)


    def block_for(index, other, source):
        return lax.dynamic_slice(
            source, (0, (place ^ other) * width + starts[index]), (held, WIDTHS[index])
        )

    order = place ^ jnp.arange(4, dtype=jnp.int32)
    hot = order[:, None] == jnp.arange(4, dtype=jnp.int32)[None, :]
    slots_local = jnp.sum(jnp.where(hot[:, :, None], slots.reshape(1, 4, rows), 0), axis=1)
    lists_local = jnp.sum(jnp.where(hot[:, :, None], lists[None, :, :], 0), axis=1)
    positions = jnp.arange(lists.shape[1], dtype=jnp.int32)
    ids = jnp.sum(
        jnp.where(slots_local[:, :, None] == positions, lists_local[:, None, :], 0), axis=2
    )
    owned_ids = (ids - place * holding).reshape(4, 1, rows)
    owned = (lists_local >= place * holding) & (lists_local < (place + 1) * holding)
    earlier = positions[None, :] < positions[:, None]
    rank_in_list = jnp.sum(owned[:, None, :] & earlier[None], axis=2)
    caps = jnp.arange(CAP, dtype=jnp.int32)
    chosen = jnp.sum(
        jnp.where(
            owned[:, None, :] & (rank_in_list[:, None, :] == caps[None, :, None]),
            (lists_local - place * holding)[:, None, :],
            0,
        ),
        axis=2,
    ).reshape(4 * CAP)
    picks = jnp.concatenate([place.reshape(1), chosen]).astype(jnp.int32)

    parity = (place ^ t) & 1
    per_owner = held // rank
    half_step = per_owner // 2
    owner_first = [holding * (place ^ j) + per_owner * t for j in range(4)]
    info = jnp.stack(
        [parity, place]
        + [owner_first[j] + half_step * h for j in range(4) for h in range(2)]
    ).astype(jnp.int32)

    own_rows, near_b, picks, info, ids, owned_ids = lax.optimization_barrier(
        (hidden, near_b, picks, info, ids, owned_ids)
    )

    (near_lowrank,) = scores(picks, 0, [own_rows], [near_b], input_maps, 0, ids=owned_ids)
    second = swap(tie(late, near_lowrank), "pool", 2)
    near_late = product(
        [[(tie(own_rows, near_lowrank), part, 1)], [(near_b, part, 1)]],
        weight, 1, 0, width, 512,
    )

    first_a, first_b = lax.optimization_barrier((first_a, first_b, near_late))[:2]
    a0 = [first_a, first_b]
    b0 = [swap(x, "pool", 1) for x in a0]
    source, kept_ids, _ = lax.optimization_barrier((output_maps, ids, first_a))
    blocks = [block_for(index, other, source) for index in range(2) for other in (2, 3)]
    wide_ids = jnp.broadcast_to(kept_ids[:, :, None], (4, rows, 128))
    *b0, wide_ids, blocks[0], blocks[1], blocks[2], blocks[3] = lax.optimization_barrier(
        (*b0, wide_ids, *blocks)
    )
    (raw,) = scores(picks, 2, a0, b0, input_maps, 0)
    base = product(
        [
            [(tie(own_rows, raw), part, 0)],
            [(near_b, part, 0)],
            [(x, part // 2, 0) for x in a0],
            [(x, part // 2, 0) for x in b0],
        ],
        weight, 0, 0, width, 512, near_late,
    )
    a1 = tie(second, base)
    b1 = swap(a1, "pool", 1)
    core_block = lax.dynamic_slice(
        tie(output_maps, a1), (0, (place ^ 1) * width), (held, width)
    )
    b1, core_block = lax.optimization_barrier((b1, core_block))
    core_maps = swap(core_block, "pool", 1)
    total, sent = scores(
        picks, 2, [a1], [b1], input_maps, 1, prior=raw, near=near_lowrank, ids=owned_ids
    )

    def far_piece(index, after, hint=HINT):
        return product(
            [[(tie(a1, after), part, 0)], [(b1, part, 0)]],
            weight, 1, starts[index], WIDTHS[index], 256, base, 1, hint,
        ).reshape(2, rows, WIDTHS[index])

    got = [swap(sent, "pool", step) for step in (2, 3, 1)]
    pieces = [far_piece(0, sent, 1)]

    def start_maps(index, after):
        pair = later[2 * (index - 2) : 2 * (index - 2) + 2]
        return [swap(tie(x, after), "pool", 2 + k) for k, x in enumerate(pair)]

    moved = [[swap(blocks[0], "pool", 2), swap(tie(blocks[1], sent), "pool", 3)]]
    moved.append([swap(tie(blocks[k], sent), "pool", k) for k in (2, 3)])
    moved[0][0] = tie(moved[0][0], sent)
    got = lax.optimization_barrier((*got, moved[0][0], pieces[0]))[:3]
    total = total + sum(x.astype(F32) for x in got)
    sent = total.astype(BF16)
    got = swap(sent, "tensor", 1)
    pieces.append(far_piece(1, sent, 1))
    moved[0][1] = tie(moved[0][1], sent)
    got = lax.optimization_barrier((got, pieces[1], moved[0][1]))[0]
    total = total + got.astype(F32)
    sent = total.astype(BF16)
    got = swap(sent, "tensor", 2)
    source = tie(output_maps, sent)
    later = [block_for(index, other, source) for index in (2, 3) for other in (2, 3)]
    got, *later = lax.optimization_barrier((got, *later))
    moved.append(start_maps(2, sent))
    moved[1][0] = tie(moved[1][0], sent)
    got = lax.optimization_barrier((got, *moved[0], moved[1][0]))[0]

    near_base = base.reshape(4, rows, width)
    side = ((place ^ t) >> 1) & 1
    parts = []
    spread = send = None

    def maps_of(index, after):
        return moved[index] if after is None else [tie(x, after) for x in moved[index]]

    def pace(index):
        if index == 3:
            return lax.optimization_barrier((near_base, started[1], parts[0]))[0]
        return near_base if index < 2 else tie(near_base, started[index - 2])

    started = []

    halves = []

    def finish(index, after):
        keep, got = halves[index]
        got = tie(got, after)
        if index == 2:
            got = tie(got, parts[1])
        pair = keep + got.astype(F32)
        sent = jnp.where(side == 0, pair[1], pair[0]).astype(BF16)
        kept = jnp.where(side == 0, pair[0], pair[1])
        started.append(sent)
        return kept + swap(sent, "tensor", 2).astype(F32)

    for chunk in range(count):
        common = (
            info, pace(chunk), pieces[chunk], output_maps, core_maps,
            maps_of(chunk, started[chunk - 2] if chunk > 1 else send), starts[chunk],
        )
        if chunk == 0:
            keep, send, spread = combine(*common, build=(total, got, wide_ids))
            moved.append(start_maps(3, send))
        else:
            keep, send = combine(*common, spread=spread)
        if chunk == 0:
            pieces.append(far_piece(2, send))
        halves.append((keep, swap(send, "tensor", 1)))
        if chunk > 0:
            parts.append(finish(chunk - 1, send))
        if chunk == 1:
            pieces.append(far_piece(3, started[0]))
    parts.append(finish(count - 1, started[-1]))
    return jnp.concatenate(parts, axis=1).astype(BF16)


def per_device_general(hidden, weight, input_maps, output_maps, slots, lists):
    rows, depth = hidden.shape
    pool_count = lax.axis_size("pool")
    tensor_count = lax.axis_size("tensor")
    place = lax.axis_index("pool")
    t = lax.axis_index("tensor")
    holding, rank = input_maps.shape[:2]
    held = output_maps.shape[0]
    total_rows = rows * pool_count
    slot_ids = jnp.arange(lists.shape[1], dtype=jnp.int32)
    slot_hot = slots.reshape(pool_count, rows)[:, :, None] == slot_ids
    ids = jnp.sum(jnp.where(slot_hot, lists[:, None, :], 0), axis=2).reshape(total_rows)
    gathered = lax.all_gather(hidden, "pool", axis=0, tiled=True)
    scored = lax.dot_general(
        gathered,
        input_maps.reshape(holding * rank, depth),
        (((1,), (1,)), ((), ())),
        preferred_element_type=F32,
    ).reshape(total_rows, holding, rank)
    owned = place * holding + jnp.arange(holding, dtype=jnp.int32)
    partial = jnp.sum(
        jnp.where((ids[:, None] == owned[None, :])[:, :, None], scored, 0.0), axis=1
    )
    lowrank = lax.psum(partial, ("tensor", "pool")).astype(BF16)
    maps = lax.all_to_all(output_maps, "pool", split_axis=1, concat_axis=0, tiled=True)
    columns = jnp.arange(pool_count * held, dtype=jnp.int32)
    source = (columns // held * tensor_count + t) * held + columns % held
    pick = (source[None, :] % rank == jnp.arange(rank, dtype=jnp.int32)[:, None]).astype(BF16)
    placed = jnp.dot(lowrank, pick, preferred_element_type=F32).astype(BF16)
    spread = jnp.where(ids[:, None] == source[None, :] // rank, placed, jnp.zeros_like(placed))
    value = jnp.dot(gathered, weight, preferred_element_type=F32)
    value = value + jnp.dot(spread, maps, preferred_element_type=F32)
    mixed = lax.psum_scatter(value, "tensor", scatter_dimension=0, tiled=True)
    return mixed.astype(BF16)


def solution(mesh):
    shape = dict(mesh.shape)
    fast = shape["groups"] == 2 and shape["pool"] == 4 and shape["tensor"] == 4
    placed = (
        P(("groups", "pool"), "tensor"),
        P("tensor", "pool"),
        P("pool", None, "tensor"),
        P(("pool", "tensor"), None),
        P("groups"),
        P("groups", None),
    )
    return jax.shard_map(
        per_device_fast if fast else per_device_general,
        mesh=mesh,
        in_specs=placed,
        out_specs=P(("groups", "tensor"), "pool"),
        check_vma=False,
    )
```

```python
import jax
import jax.numpy as jnp
from jax import lax
from jax.experimental import pallas as pl
from jax.experimental.pallas import tpu as pltpu
from jax.sharding import PartitionSpec as P

F32 = jnp.float32
BF16 = jnp.bfloat16
VMEM_LIMIT = 48 * 1024 * 1024
WIDTHS = (512, 512, 512, 512)
CAP = 4
HALVES = 2
HINT = 1000


def partners(count, step):
    return [(i, i ^ step) for i in range(count)]


def swap(values, axis, step):
    return lax.ppermute(values, axis, partners(lax.axis_size(axis), step))


def tie(values, *after):
    return lax.optimization_barrier((values, *after))[0]


def cost(flops, moved, hint=HINT):
    return pl.CostEstimate(flops=flops // hint, bytes_accessed=moved // hint, transcendentals=0)


def params():
    return pltpu.CompilerParams(vmem_limit_bytes=VMEM_LIMIT)


def cut_kernel(ref, *refs):
    outs, (stage, sems) = refs[:-2], refs[-2:]
    inward, outward, start = [], [], 0
    for index, out in enumerate(outs):
        spot = pl.ds(start, out.shape[1])
        inward.append(
            pltpu.make_async_copy(ref.at[:, spot], stage.at[:, spot], sems.at[0, index])
        )
        outward.append(pltpu.make_async_copy(stage.at[:, spot], out, sems.at[1, index]))
        start += out.shape[1]
    for copy in inward:
        copy.start()
    for copy, after in zip(inward, outward):
        copy.wait()
        after.start()
    for copy in outward:
        copy.wait()


def cut_columns(array, widths):
    return pl.pallas_call(
        cut_kernel,
        in_specs=[pl.BlockSpec(memory_space=pl.ANY)],
        out_specs=[pl.BlockSpec(memory_space=pl.ANY)] * len(widths),
        out_shape=[jax.ShapeDtypeStruct((array.shape[0], w), array.dtype) for w in widths],
        scratch_shapes=[
            pltpu.VMEM(array.shape, array.dtype),
            pltpu.SemaphoreType.DMA((2, len(widths))),
        ],
        compiler_params=params(),
        cost_estimate=cost(0, 4 * array.size),
        name="cut",
    )(array)


def product_kernel(counts, has_prior, *refs):
    pieces, refs = refs[: sum(counts)], refs[sum(counts) :]
    if has_prior:
        prior_ref, refs = refs[0], refs[1:]
    w_ref, out_ref, rows = refs

    @pl.when(pl.program_id(0) == 0)
    def _():
        height = rows.shape[0] // len(counts)
        spot = 0
        for group, count in enumerate(counts):
            start = 0
            for piece in pieces[spot : spot + count]:
                wide = piece.shape[1]
                rows[group * height : (group + 1) * height, start : start + wide] = piece[...]
                start += wide
            spot += count

    value = jnp.dot(rows[...], w_ref[...], preferred_element_type=F32)
    if has_prior:
        top = prior_ref.shape[0]
        out_ref[:top, :] = value[:top] + prior_ref[...]
        if top < value.shape[0]:
            out_ref[top:, :] = value[top:]
    else:
        out_ref[...] = value


def product(groups, weight, depth_block, first, width, tile, prior=None, prior_block=0, hint=HINT):
    rows = groups[0][0][0].shape[0]
    depth = sum(wide for _, wide, _ in groups[0])
    total = rows * len(groups)
    in_specs, args = [], []
    for group in groups:
        for array, wide, block in group:
            in_specs.append(pl.BlockSpec((rows, wide), lambda n, block=block: (0, block)))
            args.append(array)
    if prior is not None:
        in_specs.append(
            pl.BlockSpec((2 * rows, tile), lambda n: (prior_block, first // tile + n))
        )
        args.append(prior)
    in_specs.append(pl.BlockSpec((depth, tile), lambda n: (depth_block, first // tile + n)))
    args.append(weight)
    counts = [len(group) for group in groups]
    return pl.pallas_call(
        lambda *refs: product_kernel(counts, prior is not None, *refs),
        grid=(width // tile,),
        in_specs=in_specs,
        out_specs=pl.BlockSpec((total, tile), lambda n: (0, n)),
        out_shape=jax.ShapeDtypeStruct((total, width), F32),
        scratch_shapes=[pltpu.VMEM((total, depth), BF16)],
        compiler_params=params(),
        cost_estimate=cost(
            2 * total * depth * width, 2 * depth * (width + total) + 8 * total * width, hint
        ),
        name="base",
    )(*args)


def scores_kernel(first, offset, count, has_prior, last, info_ref, *refs):
    groups, maps_ref, refs = (refs[:count], refs[count : 2 * count]), refs[2 * count], refs[2 * count + 1 :]
    if has_prior:
        prior_ref, refs = refs[0], refs[1:]
    if first == 2 and last:
        near_ref, refs = refs[0], refs[1:]
    if last:
        ids_ref, refs = refs[0], refs[1:]
    outs, (rows, maps, row_sems, map_sems) = refs[:-4], refs[-4:]
    depth = rows.shape[2]
    cut = depth // 2

    def map_copy(pair, k, part):
        chosen = info_ref[1 + (first + pair) * CAP + k]
        return pltpu.make_async_copy(
            maps_ref.at[chosen, :, pl.ds(offset + part * cut, cut)],
            maps.at[pair * CAP + k, :, pl.ds(part * cut, cut)],
            map_sems.at[pair, k, part],
        )

    row_copies = []
    for pair, pieces in enumerate(groups):
        start = 0
        for index, piece in enumerate(pieces):
            row_copies.append(
                pltpu.make_async_copy(
                    piece,
                    rows.at[pair, :, pl.ds(start, piece.shape[1])],
                    row_sems.at[pair * count + index],
                )
            )
            start += piece.shape[1]
    for pair in range(2):
        for copy in row_copies[pair * count : (pair + 1) * count]:
            copy.start()
        for part in range(2):
            for k in range(CAP):
                map_copy(pair, k, part).start()
    for pair in range(2):
        for copy in row_copies[pair * count : (pair + 1) * count]:
            copy.wait()
        total = prior_ref[pair] if has_prior else None
        for part in range(2):
            for k in range(CAP):
                map_copy(pair, k, part).wait()
            columns = slice(part * cut, (part + 1) * cut)
            chosen = maps[pair * CAP : (pair + 1) * CAP, :, columns]
            term = lax.dot_general(
                chosen.reshape(-1, cut),
                rows[pair, :, columns],
                (((1,), (1,)), ((), ())),
                preferred_element_type=F32,
            )
            total = term if total is None else total + term
        if not last:
            outs[0][pair] = total
            continue
        wanted = ids_ref[pair]
        rank = total.shape[0] // CAP
        found = jnp.zeros((rank, total.shape[1]), F32)
        for k in range(CAP):
            mine = info_ref[1 + (first + pair) * CAP + k]
            found += jnp.where(wanted == mine, total[k * rank : (k + 1) * rank], 0.0)
        if first == 0:
            outs[0][pair] = found
        else:
            near_group = info_ref[0] ^ pair
            far_group = near_group ^ 2
            outs[0][far_group] = found
            outs[1][far_group] = found.astype(BF16)
            outs[0][near_group] = near_ref[pair]
            outs[1][near_group] = near_ref[pair].astype(BF16)


def scores(info, first, lower, upper, maps, half, prior=None, near=None, ids=None):
    rows, depth = lower[0].shape[0], sum(x.shape[1] for x in lower)
    rank = maps.shape[1]
    has_prior, last = prior is not None, ids is not None
    args_rows = [*lower, *upper]
    whole = lambda x: pl.BlockSpec(x.shape, lambda k, s: (0,) * x.ndim)
    args = [*lower, *upper, maps]
    in_specs = [pl.BlockSpec(memory_space=pl.ANY)] * len(args)
    if has_prior:
        in_specs.append(whole(prior))
        args.append(prior)
    if near is not None:
        in_specs.append(whole(near))
        args.append(near)
    if last:
        in_specs.append(
            pl.BlockSpec((2,) + ids.shape[1:], lambda k, s: (first // 2, 0, 0))
        )
        args.append(ids)
    if not last:
        out_shape = [jax.ShapeDtypeStruct((2, CAP * rank, rows), F32)]
    elif first == 0:
        out_shape = [jax.ShapeDtypeStruct((2, rank, rows), F32)]
    else:
        out_shape = [jax.ShapeDtypeStruct((4, rank, rows), kind) for kind in (F32, BF16)]
    return pl.pallas_call(
        lambda *refs: scores_kernel(first, half * depth, len(lower), has_prior, last, *refs),
        grid_spec=pltpu.PrefetchScalarGridSpec(
            num_scalar_prefetch=1,
            grid=(1,),
            in_specs=in_specs,
            out_specs=[whole(x) for x in out_shape],
            scratch_shapes=[
                pltpu.VMEM((2, rows, depth), BF16),
                pltpu.VMEM((2 * CAP, rank, depth), BF16),
                pltpu.SemaphoreType.DMA((len(args_rows),)),
                pltpu.SemaphoreType.DMA((2, CAP, 2)),
            ],
        ),
        out_shape=out_shape,
        compiler_params=params(),
        cost_estimate=cost(4 * rows * depth * CAP * rank, 4 * depth * (CAP * rank + rows)),
        name="scores",
    )(info, *args)


def build_spread(info_ref, lowrank_ref, got_ref, ids_ref, spread):
    rows, lanes = ids_ref.shape[1], ids_ref.shape[2]
    parity, place = info_ref[0], info_ref[1]
    upper = (lax.broadcasted_iota(jnp.int32, (rows, lanes), 1) >= lanes // 2).astype(jnp.int32)
    for slot in range(4):
        local = ((slot // 2) ^ parity) + 2 * (slot % 2)
        group = place ^ local
        values = lowrank_ref[group] + got_ref[group].astype(F32)
        values = jnp.concatenate([values, values], axis=0).T
        wanted = ids_ref[local] - upper
        for piece in range(8):
            spread[slot * rows : (slot + 1) * rows, piece * lanes : (piece + 1) * lanes] = (
                jnp.where(wanted == info_ref[2 + piece], values, 0.0).astype(BF16)
            )


def combine_kernel(build, info_ref, *refs):
    if build:
        lowrank_ref, got_ref, ids_ref, refs = refs[0], refs[1], refs[2], refs[3:]
        near_ref, far_ref, own_ref, core_ref, *blocks, keep_ref, send_ref, spread_ref, maps = refs

        @pl.when(pl.program_id(0) == 0)
        def _():
            build_spread(info_ref, lowrank_ref, got_ref, ids_ref, spread_ref)

    else:
        spread_ref, near_ref, far_ref, own_ref, core_ref, *blocks, keep_ref, send_ref, maps = refs
    parity = info_ref[0]
    rows = near_ref.shape[1]
    held = own_ref.shape[0]
    for index, ref in enumerate((own_ref, core_ref, *blocks)):
        maps[index * held : (index + 1) * held, :] = ref[...]
    delta = jnp.dot(spread_ref[...], maps[...], preferred_element_type=F32)
    for slot in range(4):
        source = near_ref if slot % 2 == 0 else far_ref
        value = source[(slot // 2) ^ parity] + delta[slot * rows : (slot + 1) * rows]
        if slot < 2:
            keep_ref[slot % 2] = value
        else:
            send_ref[slot % 2] = value.astype(BF16)


def combine(info, near, far, own_maps, core_maps, blocks, start, spread=None, build=()):
    rows = near.shape[1]
    width = far.shape[2]
    tile = 512
    first = start // tile
    per_place = core_maps.shape[1] // tile
    held = own_maps.shape[0]
    whole = lambda shape: pl.BlockSpec(shape, lambda n, s: (0,) * len(shape))
    ahead = list(build) if build else [spread]
    spread_shape = (4 * rows, 4 * held)
    in_specs = [whole(x.shape) for x in ahead]
    in_specs += [
        pl.BlockSpec((2, rows, tile), lambda n, s: (0, 0, first + n)),
        pl.BlockSpec((2, rows, tile), lambda n, s: (0, 0, n)),
        pl.BlockSpec((held, tile), lambda n, s: (0, s[1] * per_place + first + n)),
        pl.BlockSpec((held, tile), lambda n, s: (0, first + n)),
    ]
    in_specs += [
        pl.BlockSpec((held, tile), lambda n, s: (0, n)) for _ in blocks
    ]
    out_specs = [pl.BlockSpec((2, rows, tile), lambda n, s: (0, 0, n))] * 2
    out_shape = [jax.ShapeDtypeStruct((2, rows, width), kind) for kind in (F32, BF16)]
    if build:
        out_specs.append(whole(spread_shape))
        out_shape.append(jax.ShapeDtypeStruct(spread_shape, BF16))
    return pl.pallas_call(
        lambda *refs: combine_kernel(bool(build), *refs),
        grid_spec=pltpu.PrefetchScalarGridSpec(
            num_scalar_prefetch=1,
            grid=(width // tile,),
            in_specs=in_specs,
            out_specs=out_specs,
            scratch_shapes=[pltpu.VMEM((4 * held, tile), BF16)],
        ),
        out_shape=out_shape,
        compiler_params=params(),
        cost_estimate=cost(
            32 * rows * held * width, 26 * rows * width + 8 * held * width
        ),
        name="combine",
    )(info, *ahead, near, far, own_maps, core_maps, *blocks)


def per_device_fast(hidden, weight, input_maps, output_maps, slots, lists):
    rows, depth = hidden.shape
    place = lax.axis_index("pool")
    t = lax.axis_index("tensor")
    holding, rank = input_maps.shape[:2]
    held, features = output_maps.shape
    width = features // 4
    starts = [sum(WIDTHS[:i]) for i in range(len(WIDTHS))]
    count = len(WIDTHS)

    part = depth // HALVES
    near_b = swap(hidden, "pool", 1)
    *early, late = cut_columns(hidden, (part // 2, part // 2, part))
    first_a, first_b = (swap(block, "pool", 2) for block in early)


    def block_for(index, other, source):
        return lax.dynamic_slice(
            source, (0, (place ^ other) * width + starts[index]), (held, WIDTHS[index])
        )

    order = place ^ jnp.arange(4, dtype=jnp.int32)
    hot = order[:, None] == jnp.arange(4, dtype=jnp.int32)[None, :]
    slots_local = jnp.sum(jnp.where(hot[:, :, None], slots.reshape(1, 4, rows), 0), axis=1)
    lists_local = jnp.sum(jnp.where(hot[:, :, None], lists[None, :, :], 0), axis=1)
    positions = jnp.arange(lists.shape[1], dtype=jnp.int32)
    ids = jnp.sum(
        jnp.where(slots_local[:, :, None] == positions, lists_local[:, None, :], 0), axis=2
    )
    owned_ids = (ids - place * holding).reshape(4, 1, rows)
    owned = (lists_local >= place * holding) & (lists_local < (place + 1) * holding)
    earlier = positions[None, :] < positions[:, None]
    rank_in_list = jnp.sum(owned[:, None, :] & earlier[None], axis=2)
    caps = jnp.arange(CAP, dtype=jnp.int32)
    chosen = jnp.sum(
        jnp.where(
            owned[:, None, :] & (rank_in_list[:, None, :] == caps[None, :, None]),
            (lists_local - place * holding)[:, None, :],
            0,
        ),
        axis=2,
    ).reshape(4 * CAP)
    picks = jnp.concatenate([place.reshape(1), chosen]).astype(jnp.int32)

    parity = (place ^ t) & 1
    per_owner = held // rank
    half_step = per_owner // 2
    owner_first = [holding * (place ^ j) + per_owner * t for j in range(4)]
    info = jnp.stack(
        [parity, place]
        + [owner_first[j] + half_step * h for j in range(4) for h in range(2)]
    ).astype(jnp.int32)

    own_rows, near_b, picks, info, ids, owned_ids = lax.optimization_barrier(
        (hidden, near_b, picks, info, ids, owned_ids)
    )

    (near_lowrank,) = scores(picks, 0, [own_rows], [near_b], input_maps, 0, ids=owned_ids)
    second = swap(tie(late, near_lowrank), "pool", 2)
    near_late = product(
        [[(tie(own_rows, near_lowrank), part, 1)], [(near_b, part, 1)]],
        weight, 1, 0, width, 512,
    )

    first_a, first_b = lax.optimization_barrier((first_a, first_b, near_late))[:2]
    a0 = [first_a, first_b]
    b0 = [swap(x, "pool", 1) for x in a0]
    source, kept_ids, _ = lax.optimization_barrier((output_maps, ids, first_a))
    blocks = [block_for(index, other, source) for index in range(2) for other in (2, 3)]
    wide_ids = jnp.broadcast_to(kept_ids[:, :, None], (4, rows, 128))
    *b0, wide_ids, blocks[0], blocks[1], blocks[2], blocks[3] = lax.optimization_barrier(
        (*b0, wide_ids, *blocks)
    )
    (raw,) = scores(picks, 2, a0, b0, input_maps, 0)
    base = product(
        [
            [(tie(own_rows, raw), part, 0)],
            [(near_b, part, 0)],
            [(x, part // 2, 0) for x in a0],
            [(x, part // 2, 0) for x in b0],
        ],
        weight, 0, 0, width, 512, near_late,
    )
    a1 = tie(second, base)
    b1 = swap(a1, "pool", 1)
    core_block = lax.dynamic_slice(
        tie(output_maps, a1), (0, (place ^ 1) * width), (held, width)
    )
    b1, core_block = lax.optimization_barrier((b1, core_block))
    core_maps = swap(core_block, "pool", 1)
    total, sent = scores(
        picks, 2, [a1], [b1], input_maps, 1, prior=raw, near=near_lowrank, ids=owned_ids
    )

    def far_piece(index, after, hint=HINT):
        return product(
            [[(tie(a1, after), part, 0)], [(b1, part, 0)]],
            weight, 1, starts[index], WIDTHS[index], 256, base, 1, hint,
        ).reshape(2, rows, WIDTHS[index])

    got = [swap(sent, "pool", step) for step in (2, 3, 1)]
    pieces = [far_piece(0, sent, 1)]

    def start_maps(index, after):
        pair = later[2 * (index - 2) : 2 * (index - 2) + 2]
        return [swap(tie(x, after), "pool", 2 + k) for k, x in enumerate(pair)]

    moved = [[swap(blocks[0], "pool", 2), swap(tie(blocks[1], sent), "pool", 3)]]
    moved.append([swap(tie(blocks[k], sent), "pool", k) for k in (2, 3)])
    moved[0][0] = tie(moved[0][0], sent)
    got = lax.optimization_barrier((*got, moved[0][0], pieces[0]))[:3]
    total = total + sum(x.astype(F32) for x in got)
    sent = total.astype(BF16)
    got = swap(sent, "tensor", 1)
    pieces.append(far_piece(1, sent, 1))
    moved[0][1] = tie(moved[0][1], sent)
    got = lax.optimization_barrier((got, pieces[1], moved[0][1]))[0]
    total = total + got.astype(F32)
    sent = total.astype(BF16)
    got = swap(sent, "tensor", 2)
    source = tie(output_maps, sent)
    later = [block_for(index, other, source) for index in (2, 3) for other in (2, 3)]
    got, *later = lax.optimization_barrier((got, *later))
    moved.append(start_maps(2, sent))
    moved[1][0] = tie(moved[1][0], sent)
    got = lax.optimization_barrier((got, *moved[0], moved[1][0]))[0]

    near_base = base.reshape(4, rows, width)
    side = ((place ^ t) >> 1) & 1
    parts = []
    spread = send = None

    def maps_of(index, after):
        return moved[index] if after is None else [tie(x, after) for x in moved[index]]

    def pace(index):
        if index == 1:
            moved[2][0] = tie(moved[2][0], pieces[2])
            return lax.optimization_barrier((near_base, moved[2][0], pieces[2]))[0]
        if index == 3:
            return lax.optimization_barrier((near_base, started[1], parts[0]))[0]
        return near_base if index < 2 else tie(near_base, started[index - 2])

    started = []

    halves = []

    def finish(index, after):
        keep, got = halves[index]
        got = tie(got, after)
        if index == 2:
            got = tie(got, parts[1])
        pair = keep + got.astype(F32)
        sent = jnp.where(side == 0, pair[1], pair[0]).astype(BF16)
        kept = jnp.where(side == 0, pair[0], pair[1])
        started.append(sent)
        return kept + swap(sent, "tensor", 2).astype(F32)

    for chunk in range(count):
        common = (
            info, pace(chunk), pieces[chunk], output_maps, core_maps,
            maps_of(chunk, started[chunk - 2] if chunk > 1 else send), starts[chunk],
        )
        if chunk == 0:
            keep, send, spread = combine(*common, build=(total, got, wide_ids))
            moved.append(start_maps(3, send))
        else:
            keep, send = combine(*common, spread=spread)
        if chunk == 0:
            pieces.append(far_piece(2, send))
        halves.append((keep, swap(send, "tensor", 1)))
        if chunk > 0:
            parts.append(finish(chunk - 1, send))
        if chunk == 1:
            pieces.append(far_piece(3, started[0]))
    parts.append(finish(count - 1, started[-1]))
    return jnp.concatenate(parts, axis=1).astype(BF16)


def per_device_general(hidden, weight, input_maps, output_maps, slots, lists):
    rows, depth = hidden.shape
    pool_count = lax.axis_size("pool")
    tensor_count = lax.axis_size("tensor")
    place = lax.axis_index("pool")
    t = lax.axis_index("tensor")
    holding, rank = input_maps.shape[:2]
    held = output_maps.shape[0]
    total_rows = rows * pool_count
    slot_ids = jnp.arange(lists.shape[1], dtype=jnp.int32)
    slot_hot = slots.reshape(pool_count, rows)[:, :, None] == slot_ids
    ids = jnp.sum(jnp.where(slot_hot, lists[:, None, :], 0), axis=2).reshape(total_rows)
    gathered = lax.all_gather(hidden, "pool", axis=0, tiled=True)
    scored = lax.dot_general(
        gathered,
        input_maps.reshape(holding * rank, depth),
        (((1,), (1,)), ((), ())),
        preferred_element_type=F32,
    ).reshape(total_rows, holding, rank)
    owned = place * holding + jnp.arange(holding, dtype=jnp.int32)
    partial = jnp.sum(
        jnp.where((ids[:, None] == owned[None, :])[:, :, None], scored, 0.0), axis=1
    )
    lowrank = lax.psum(partial, ("tensor", "pool")).astype(BF16)
    maps = lax.all_to_all(output_maps, "pool", split_axis=1, concat_axis=0, tiled=True)
    columns = jnp.arange(pool_count * held, dtype=jnp.int32)
    source = (columns // held * tensor_count + t) * held + columns % held
    pick = (source[None, :] % rank == jnp.arange(rank, dtype=jnp.int32)[:, None]).astype(BF16)
    placed = jnp.dot(lowrank, pick, preferred_element_type=F32).astype(BF16)
    spread = jnp.where(ids[:, None] == source[None, :] // rank, placed, jnp.zeros_like(placed))
    value = jnp.dot(gathered, weight, preferred_element_type=F32)
    value = value + jnp.dot(spread, maps, preferred_element_type=F32)
    mixed = lax.psum_scatter(value, "tensor", scatter_dimension=0, tiled=True)
    return mixed.astype(BF16)


def solution(mesh):
    shape = dict(mesh.shape)
    fast = shape["groups"] == 2 and shape["pool"] == 4 and shape["tensor"] == 4
    placed = (
        P(("groups", "pool"), "tensor"),
        P("tensor", "pool"),
        P("pool", None, "tensor"),
        P(("pool", "tensor"), None),
        P("groups"),
        P("groups", None),
    )
    return jax.shard_map(
        per_device_fast if fast else per_device_general,
        mesh=mesh,
        in_specs=placed,
        out_specs=P(("groups", "tensor"), "pool"),
        check_vma=False,
    )
```
